32 devices in a mesh: seq: 16 (over z, x, core), head: 2 (over y).
Axes of the slice: x: 2, y: 2, z: 4, core: 2. Of those that a mesh axis runs over, the one named last changes fastest.
Arguments:
- query_rows: bfloat16 [2048, 3072], P(('seq', 'head')), may hold values from -5 to 5
- key_rows: bfloat16 [2048, 3072], P(('seq', 'head')), may hold values from -5 to 5
- value_rows: bfloat16 [2048, 3072], P(('seq', 'head')), may hold values from -6 to 6
- out_grad: bfloat16 [2048, 3072], P(('seq', 'head')), may hold values from -6 to 6
- block_mask: int32 [2, 4, 4], replicated, may hold values 0 or 1
Outputs:
- attended: bfloat16 [2048, 3072], P(('seq', 'head'))
- grad_query: bfloat16 [2048, 3072], P(('seq', 'head'))
- grad_keys: bfloat16 [2048, 3072], P(('seq', 'head'))
- grad_values: bfloat16 [2048, 3072], P(('seq', 'head'))
The draws below stay inside these ranges and needn't reach their ends.
All inputs are finite; a program needn't handle non-finite values.
Results may differ from the reference program's by a relative error of at most 0.024.
Values may be sent and summed in bfloat16 or wider, within the bound.
No kernel may reach another device: no remote copies, remote signals or barrier semaphores. Data moves between devices by JAX's collectives and lax.ppermute only.
A program may use at most 64 MiB of HBM per device.

```python
import math
import jax
import jax.numpy as jnp
from jax import lax

HD = 128
HEADS = 24
BLOCK = 128
GROUP = 4
F_TOK = 512
NB = 4
LEVELS = 2
TOKENS = 2048


def draw_query_rows(key, part):
    row_count = TOKENS
    col_count = HEADS * HD
    drawn = jnp.clip(jax.random.normal(jax.random.fold_in(key, 1), (row_count, col_count), jnp.float32), -5.0, 5.0)
    return drawn.astype(jnp.bfloat16)


def draw_key_rows(key, part):
    row_count = TOKENS
    col_count = HEADS * HD
    drawn = jnp.clip(jax.random.normal(jax.random.fold_in(key, 2), (row_count, col_count), jnp.float32), -5.0, 5.0)
    return drawn.astype(jnp.bfloat16)


def with_ends(result, rng, low, top_value):
    spot = [jax.random.randint(jax.random.fold_in(rng, axis), (), 0, length) for axis, length in enumerate(result.shape)]
    main_axis = result.shape.index(max(result.shape))
    next_to = spot[:main_axis] + [(spot[main_axis] + 1) % result.shape[main_axis]] + spot[main_axis + 1:]
    return result.at[tuple(spot)].set(low).at[tuple(next_to)].set(top_value)


def levels(stream_key, extent, cuts, least, high):
    loudness = 1.0
    for axis_at, parts in cuts:
        heights = jax.random.uniform(jax.random.fold_in(jax.random.fold_in(stream_key, 6), axis_at), (parts,), jnp.float32, least / len(cuts), high / len(cuts))
        loudness = loudness * jnp.repeat(jnp.exp(heights), extent[axis_at] // parts).reshape((-1,) + (1,) * (len(extent) - 1 - axis_at))
    return loudness


def bell_draw(rng, shape, spread, limit, pieces=(), dtype=jnp.bfloat16):
    gain = levels(rng, shape, pieces, -0.22, 0.18) if pieces else 1.0
    values = jax.random.normal(rng, shape, jnp.float32) * spread * gain
    return jnp.minimum(jnp.maximum(values, -limit), limit).astype(dtype)


def setup_inputs(seed: int = 0) -> dict:
    keys = jax.random.split(jax.random.key(seed), 6)
    query_rows = draw_query_rows(jax.random.fold_in(keys[5], 71), 0)
    key_rows = draw_key_rows(jax.random.fold_in(keys[5], 71), 0)
    value_rows = bell_draw(keys[2], (TOKENS, HEADS * HD), 1.0, 6.0, ((0, 32),))
    out_grad = bell_draw(keys[3], (TOKENS, HEADS * HD), 1.0, 6.0, ((0, 32),))
    block_mask = with_ends((jax.random.randint(keys[4], (LEVELS, NB, NB), 0, 2) < 1).astype(jnp.int32), jax.random.fold_in(keys[4], 1), 0, 1)
    return {"query_rows": query_rows, "key_rows": key_rows, "value_rows": value_rows, "out_grad": out_grad, "block_mask": block_mask}


def widen_mask(bits):
    blocks = bits.shape[0]
    grid = jnp.broadcast_to((bits > 0)[:, None, :, None], (blocks, BLOCK, blocks, BLOCK))
    return grid.reshape(blocks * BLOCK, blocks * BLOCK)

def reference(query_rows, key_rows, value_rows, out_grad, block_mask):
    token_count, width = query_rows.shape
    frame_count = token_count // F_TOK
    head_count = width // HD
    block_rows = F_TOK // GROUP
    score_scale = 1.0 / math.sqrt(HD)

    def framed(rows):
        return rows.reshape(frame_count, F_TOK, head_count, HD)
    query_f, key_f, value_f, grad_f = (framed(query_rows), framed(key_rows), framed(value_rows), framed(out_grad))
    level_masks = [widen_mask(block_mask[level_index]) for level_index in range(LEVELS)]
    offsets = [0]
    for level_index in range(LEVELS):
        for orient in (1, -1):
            offsets.append(-orient * (1 << level_index))

    def one_frame(frame_index, carry):
        out_acc, dq_acc, dk_acc, dv_acc = carry
        allowed_list = [jnp.ones((F_TOK, F_TOK), bool)]
        spot = 1
        for level_index in range(LEVELS):
            for orient in (1, -1):
                partner = frame_index + offsets[spot]
                inside = (partner >= 0) & (partner < frame_count)
                allowed_list.append(level_masks[level_index] & inside)
                spot += 1
        allowed = jnp.concatenate(allowed_list, axis=1)
        places = [jnp.clip(frame_index + shift_by, 0, frame_count - 1).astype(jnp.int32) for shift_by in offsets]
        keys_all = jnp.concatenate([lax.dynamic_index_in_dim(key_f, place, 0, keepdims=False) for place in places], axis=0).astype(jnp.float32)
        values_all = jnp.concatenate([lax.dynamic_index_in_dim(value_f, place, 0, keepdims=False) for place in places], axis=0).astype(jnp.float32)
        query_now = lax.dynamic_index_in_dim(query_f, frame_index, 0, keepdims=False).astype(jnp.float32)
        grad_now = lax.dynamic_index_in_dim(grad_f, frame_index, 0, keepdims=False).astype(jnp.float32)
        scores = jnp.einsum('qhd,khd->hqk', query_now, keys_all) * score_scale
        scores = jnp.where(allowed[None], scores, -jnp.inf)
        peak = lax.optimization_barrier(jnp.max(scores, axis=2, keepdims=True))
        logsum = peak + jnp.log(lax.optimization_barrier(jnp.sum(jnp.exp(scores - peak), axis=2, keepdims=True)))
        probability = jnp.exp(scores - logsum)
        weights = probability.astype(jnp.bfloat16)
        weights32 = weights.astype(jnp.float32)
        attended = jnp.einsum('hqk,khd->qhd', weights32, values_all).astype(jnp.bfloat16)
        grad_weights = jnp.einsum('qhd,khd->hqk', grad_now, values_all)
        delta = jnp.transpose(lax.optimization_barrier(jnp.sum(grad_now * attended.astype(jnp.float32), axis=2)))[:, :, None]
        grad_scores = (probability * (grad_weights - delta) * score_scale).astype(jnp.bfloat16)
        scores32 = grad_scores.astype(jnp.float32)
        grad_q = jnp.einsum('hqk,khd->qhd', scores32, keys_all).astype(jnp.bfloat16)
        key_count = scores32.shape[2]
        key_part = jnp.einsum('hgqk,gqhd->gkhd', scores32.reshape(head_count, GROUP, block_rows, key_count), query_now.reshape(GROUP, block_rows, head_count, HD))
        value_part = jnp.einsum('hgqk,gqhd->gkhd', weights32.reshape(head_count, GROUP, block_rows, key_count), grad_now.reshape(GROUP, block_rows, head_count, HD))
        key_part = lax.optimization_barrier(key_part.astype(jnp.bfloat16)).astype(jnp.float32).sum(axis=0)
        value_part = lax.optimization_barrier(value_part.astype(jnp.bfloat16)).astype(jnp.float32).sum(axis=0)
        key_part = key_part.reshape(len(offsets), F_TOK, head_count, HD)
        value_part = value_part.reshape(len(offsets), F_TOK, head_count, HD)
        for spot_index, place in enumerate(places):
            dk_acc = dk_acc.at[place].add(key_part[spot_index])
            dv_acc = dv_acc.at[place].add(value_part[spot_index])
        out_acc = lax.dynamic_update_index_in_dim(out_acc, attended, frame_index, 0)
        dq_acc = lax.dynamic_update_index_in_dim(dq_acc, grad_q, frame_index, 0)
        return (out_acc, dq_acc, dk_acc, dv_acc)
    shape = (frame_count, F_TOK, head_count, HD)
    start = (jnp.zeros(shape, jnp.bfloat16), jnp.zeros(shape, jnp.bfloat16), jnp.zeros(shape, jnp.float32), jnp.zeros(shape, jnp.float32))
    out_acc, dq_acc, dk_acc, dv_acc = lax.fori_loop(0, frame_count, one_frame, start)
    return (out_acc.reshape(token_count, width), dq_acc.reshape(token_count, width), dk_acc.astype(jnp.bfloat16).reshape(token_count, width), dv_acc.astype(jnp.bfloat16).reshape(token_count, width))
```

```python
import math

import jax
import jax.numpy as jnp
from jax import lax
from jax.experimental import pallas as pl
from jax.experimental.pallas import tpu as pltpu
from jax.sharding import Mesh
from jax.sharding import PartitionSpec as P

HD = 128
BLOCK = 128
GROUP = 4
SCALE = 1.0 / math.sqrt(HD)
SCALE_LOG2 = SCALE * math.log2(math.e)
MASKED = -1e30
VMEM_BYTES = 40 * 1024 * 1024


def partner_2(shard, axis, distance):
    return lax.ppermute(shard, axis, [(i, i ^ 1 << distance) for i in range(lax.axis_size(axis))])


def passed_along(shard, axis, by):
    peers = lax.axis_size(axis)
    pairs = [(i, i + by) for i in range(peers) if 0 <= i + by < peers]
    return lax.ppermute(shard, axis, pairs)


def widen_mask(bits):
    blocks = bits.shape[0]
    grid = jnp.broadcast_to((bits > 0)[:, None, :, None], (blocks, BLOCK, blocks, BLOCK))
    return grid.reshape(blocks * BLOCK, blocks * BLOCK)


def place_pair(mine, other, is_low, dim):
    return lax.cond(
        is_low,
        lambda pair: jnp.concatenate([pair[0], pair[1]], dim),
        lambda pair: jnp.concatenate([pair[1], pair[0]], dim),
        (mine, other),
    )


def per_device_general(query_rows, key_rows, value_rows, out_grad, block_mask):
    queries, keys_local, values_local, grads_output = (
        lax.all_to_all(query_rows, "head", split_axis=1, concat_axis=0, tiled=True),
        lax.all_to_all(key_rows, "head", split_axis=1, concat_axis=0, tiled=True),
        lax.all_to_all(value_rows, "head", split_axis=1, concat_axis=0, tiled=True),
        lax.all_to_all(out_grad, "head", split_axis=1, concat_axis=0, tiled=True),
    )
    seq_index = lax.axis_index("seq")
    group_bits = GROUP.bit_length() - 1
    rank = seq_index % GROUP
    frame_index = seq_index // GROUP
    frame_count = lax.axis_size("seq") // GROUP
    level_count = block_mask.shape[0]
    block_rows = queries.shape[0]
    frame_tokens = block_rows * GROUP
    head_count = queries.shape[1] // HD
    score_scale = 1.0 / math.sqrt(HD)
    own_pair = jnp.stack([keys_local, values_local])

    def low_bit(bit):
        return seq_index >> bit & 1 == 0

    whole_pair = own_pair
    for bit in range(group_bits):
        other = partner_2(whole_pair, "seq", bit)
        whole_pair = place_pair(whole_pair, other, low_bit(bit), 1)
    partner_list = []
    for level_index in range(level_count):
        for orient in (1, -1):
            partner_list.append(
                passed_along(whole_pair, "seq", orient * GROUP * (1 << level_index))
            )
    every_pair = jnp.concatenate([whole_pair] + partner_list, axis=1)
    keys_all, values_all = (every_pair[0], every_pair[1])
    allowed_list = [jnp.ones((block_rows, frame_tokens), bool)]
    for level_index in range(level_count):
        for orient in (1, -1):
            partner = frame_index - orient * (1 << level_index)
            inside = (partner >= 0) & (partner < frame_count)
            allowed_list.append(
                lax.dynamic_slice_in_dim(
                    widen_mask(block_mask[level_index]), rank * block_rows, block_rows, 0
                )
                & inside
            )
    allowed = jnp.concatenate(allowed_list, axis=1)

    def head_scores(query_head, keys_head):
        scores = (
            jnp.einsum("qd,kd->qk", query_head, keys_head, preferred_element_type=jnp.float32)
            * score_scale
        )
        return jnp.where(allowed, scores, -jnp.inf)

    outputs = []
    logsums = []
    for head_index in range(head_count):
        columns = slice(head_index * HD, (head_index + 1) * HD)
        scores = head_scores(queries[:, columns], keys_all[:, columns])
        peak = jnp.max(scores, axis=1, keepdims=True)
        logsum = peak + jnp.log(jnp.sum(jnp.exp(scores - peak), axis=1, keepdims=True))
        weights = jnp.exp(scores - logsum).astype(jnp.bfloat16)
        outputs.append(
            jnp.dot(weights, values_all[:, columns], preferred_element_type=jnp.float32).astype(
                jnp.bfloat16
            )
        )
        logsums.append(logsum)
    attended = jnp.concatenate(outputs, axis=1)
    query_grads = []
    key_grads = []
    value_grads = []
    for head_index in range(head_count):
        columns = slice(head_index * HD, (head_index + 1) * HD)
        query_head = queries[:, columns]
        grad_head = grads_output[:, columns]
        scores = head_scores(query_head, keys_all[:, columns])
        probability = jnp.exp(scores - logsums[head_index])
        weights = probability.astype(jnp.bfloat16)
        grad_weights = jnp.einsum(
            "qd,kd->qk", grad_head, values_all[:, columns], preferred_element_type=jnp.float32
        )
        delta_row = jnp.sum(
            grad_head.astype(jnp.float32) * attended[:, columns].astype(jnp.float32),
            axis=1,
            keepdims=True,
        )
        grad_scores = (probability * (grad_weights - delta_row) * score_scale).astype(jnp.bfloat16)
        query_grads.append(
            jnp.dot(grad_scores, keys_all[:, columns], preferred_element_type=jnp.float32).astype(
                jnp.bfloat16
            )
        )
        key_grads.append(
            jnp.einsum(
                "qk,qd->kd", grad_scores, query_head, preferred_element_type=jnp.float32
            ).astype(jnp.bfloat16)
        )
        value_grads.append(
            jnp.einsum("qk,qd->kd", weights, grad_head, preferred_element_type=jnp.float32).astype(
                jnp.bfloat16
            )
        )
    grad_query = jnp.concatenate(query_grads, axis=1)
    grad_pair = jnp.stack(
        [jnp.concatenate(key_grads, axis=1), jnp.concatenate(value_grads, axis=1)]
    )
    total = grad_pair[:, :frame_tokens].astype(jnp.float32)
    piece_index = 1
    for level_index in range(level_count):
        for orient in (1, -1):
            piece = grad_pair[:, piece_index * frame_tokens : (piece_index + 1) * frame_tokens]
            returned = passed_along(piece, "seq", -orient * GROUP * (1 << level_index))
            total = total + returned.astype(jnp.float32)
            piece_index += 1
    for bit in reversed(range(group_bits)):
        half = total.shape[1] // 2
        first_half = total[:, :half]
        second_half = total[:, half:]
        is_low = low_bit(bit)
        outgoing = jnp.where(is_low, second_half, first_half)
        staying = jnp.where(is_low, first_half, second_half)
        total = staying + partner_2(outgoing, "seq", bit)
    grad_keys = total[0].astype(jnp.bfloat16)
    grad_values = total[1].astype(jnp.bfloat16)
    return (
        lax.all_to_all(attended, "head", split_axis=0, concat_axis=1, tiled=True),
        lax.all_to_all(grad_query, "head", split_axis=0, concat_axis=1, tiled=True),
        lax.all_to_all(grad_keys, "head", split_axis=0, concat_axis=1, tiled=True),
        lax.all_to_all(grad_values, "head", split_axis=0, concat_axis=1, tiled=True),
    )


NT = (((1,), (1,)), ((), ()))
F32 = jnp.float32
BF16 = jnp.bfloat16


def dot(a, b):
    return jnp.dot(a, b, preferred_element_type=F32)


def dot_nt(a, b):
    return lax.dot_general(a, b, NT, preferred_element_type=F32)


def rows_of(ref, which):
    part = ref[:, which]
    return part.reshape(part.shape[0] * part.shape[1], part.shape[2])


def put_rows(ref, which, rows):
    ref[:, which] = rows.reshape(ref.shape[0], ref.shape[2], ref.shape[3])


def bias_rows(mask_ref, level, valid, blocks):
    lane_block = lax.broadcasted_iota(jnp.int32, (1, blocks * BLOCK), 1) // BLOCK
    rows = []
    for key_block in range(blocks):
        row = jnp.zeros((1, blocks * BLOCK), F32)
        for query_block in range(blocks):
            open_ = (mask_ref[level, query_block, key_block] > 0) & valid
            value = jnp.where(open_, 0.0, MASKED).astype(F32)
            row = jnp.where(lane_block == query_block, value, row)
        rows.append(row)
    return rows


def masked_scores(keys, queries, bias):
    scores = dot_nt(keys, queries) * SCALE_LOG2
    if bias is None:
        return scores
    blocks = len(bias)
    return jnp.concatenate(
        [scores[j * BLOCK : (j + 1) * BLOCK] + bias[j] for j in range(blocks)], axis=0
    )


def near_forward_kernel(frame_ref, mask_ref, qg_ref, kv0_ref, kv1_ref, kv3_ref, e_ref, acc_ref, ml_ref):
    tokens = e_ref.shape[2]
    blocks = tokens // BLOCK
    frame = frame_ref[0]
    inner = (frame == 1) | (frame == 2)
    queries = rows_of(qg_ref, 0)
    slots = (
        (kv0_ref, None),
        (kv1_ref, bias_rows(mask_ref, 0, frame >= 0, blocks)),
        (kv3_ref, bias_rows(mask_ref, 0, inner, blocks)),
    )
    scores = [masked_scores(rows_of(ref, 0), queries, bias) for ref, bias in slots]
    peak = scores[0].max(axis=0, keepdims=True)
    for score in scores[1:]:
        peak = jnp.maximum(peak, score.max(axis=0, keepdims=True))
    total = jnp.zeros((1, tokens), F32)
    acc = jnp.zeros((HD, tokens), F32)
    for index, (ref, _) in enumerate(slots):
        e = jnp.exp2(scores[index] - peak)
        total = total + e.sum(axis=0, keepdims=True)
        e = e.astype(BF16)
        e_ref[0, index * tokens : (index + 1) * tokens] = e
        acc = acc + dot(rows_of(ref, 1).T, e)
    acc_ref[0] = acc
    ml_ref[0, 0:1] = peak
    ml_ref[0, 1:2] = total


def far_kernel(
    frame_ref, mask_ref, qg_ref, kva_ref, kvb_ref, acc_ref, ml_ref,
    dkv_ref, att_ref, wd_ref, dq_ref,
):
    tokens = acc_ref.shape[2]
    blocks = tokens // BLOCK
    frame = frame_ref[0]
    inner = (frame == 1) | (frame == 2)
    queries = rows_of(qg_ref, 0)
    keys = jnp.where(inner, rows_of(kvb_ref, 0), rows_of(kva_ref, 0))
    values = jnp.where(inner, rows_of(kvb_ref, 1), rows_of(kva_ref, 1))
    scores = masked_scores(keys, queries, bias_rows(mask_ref, 1, frame >= 0, blocks))
    peak2 = scores.max(axis=0, keepdims=True)
    e = jnp.exp2(scores - peak2)
    total2 = e.sum(axis=0, keepdims=True)
    e = e.astype(BF16)
    acc2 = dot(values.T, e)
    peak1 = ml_ref[0, 0:1]
    peak = jnp.maximum(peak1, peak2)
    near = jnp.exp2(peak1 - peak)
    far = jnp.exp2(peak2 - peak)
    inv = 1.0 / (near * ml_ref[0, 1:2] + far * total2)
    near = near * inv
    far = far * inv
    out = (acc_ref[0] * near + acc2 * far).astype(BF16)
    att = out.T
    att_ref[...] = att.reshape(att_ref.shape)
    grads = rows_of(qg_ref, 1).T.astype(F32)
    delta = (grads * out.astype(F32)).sum(axis=0, keepdims=True)
    wd_ref[0, 0:1] = near
    wd_ref[0, 1:2] = near * delta
    scaled = (grads * far).astype(BF16)
    ds = (e.astype(F32) * (dot(values, scaled) - far * delta)).astype(BF16)
    put_rows(dkv_ref, 0, (dot(ds, queries) * SCALE).astype(BF16))
    put_rows(dkv_ref, 1, dot_nt(e, scaled).astype(BF16))
    dq_ref[0] = dot(keys.T, ds)


def near_backward_kernel(
    qg_ref, kv0_ref, kv1_ref, kv3_ref, e_ref, wd_ref, dq2_ref, att_ref,
    dkv0_ref, dkv1_ref, dkv3_ref, out_ref,
):
    tokens = e_ref.shape[2]
    queries = rows_of(qg_ref, 0)
    grads = rows_of(qg_ref, 1).T.astype(F32)
    near = wd_ref[0, 0:1]
    delta = wd_ref[0, 1:2]
    scaled = (grads * near).astype(BF16)
    dq = dq2_ref[0]
    for index, (kv_ref, dkv_ref) in enumerate(
        ((kv0_ref, dkv0_ref), (kv1_ref, dkv1_ref), (kv3_ref, dkv3_ref))
    ):
        e = e_ref[0, index * tokens : (index + 1) * tokens]
        keys = rows_of(kv_ref, 0)
        ds = (e.astype(F32) * (dot(rows_of(kv_ref, 1), scaled) - delta)).astype(BF16)
        put_rows(dkv_ref, 0, (dot(ds, queries) * SCALE).astype(BF16))
        put_rows(dkv_ref, 1, dot_nt(e, scaled).astype(BF16))
        dq = dq + dot(keys.T, ds)
    put_rows(out_ref, 1, (dq * SCALE).astype(BF16).T)
    out_ref[:, 0] = att_ref[...]


def pack_kernel(a_ref, b_ref, out_ref):
    width = out_ref.shape[3]
    for peer in range(out_ref.shape[0]):
        out_ref[peer, 0] = a_ref[:, peer * width : (peer + 1) * width]
        out_ref[peer, 1] = b_ref[:, peer * width : (peer + 1) * width]


def unpack_kernel(in_ref, a_ref, b_ref):
    width = in_ref.shape[3]
    for peer in range(in_ref.shape[0]):
        a_ref[:, peer * width : (peer + 1) * width] = in_ref[peer, 0]
        b_ref[:, peer * width : (peer + 1) * width] = in_ref[peer, 1]


def params():
    return pltpu.CompilerParams(vmem_limit_bytes=VMEM_BYTES)


def cost(flops, data):
    return pl.CostEstimate(flops=flops, bytes_accessed=data, transcendentals=0)


def per_device_line(query_rows, key_rows, value_rows, out_grad, block_mask):
    plane = ("rank", "head")
    peers = lax.axis_size("rank") * lax.axis_size("head")
    rows, columns = query_rows.shape
    width = columns // peers
    heads = width // HD
    tokens = peers * rows
    pair_shape = (peers, 2, rows, width)
    pair_type = jax.ShapeDtypeStruct(pair_shape, BF16)
    frame = lax.axis_index("frame").astype(jnp.int32).reshape(1)

    def pack(a, b):
        return pl.pallas_call(pack_kernel, out_shape=pair_type)(a, b)

    def unpack(pair):
        row_type = jax.ShapeDtypeStruct((rows, columns), BF16)
        return pl.pallas_call(unpack_kernel, out_shape=(row_type, row_type))(pair)

    def swap(pair):
        return lax.all_to_all(pair, plane, 0, 0, tiled=True)

    smem = pl.BlockSpec(memory_space=pltpu.SMEM)
    pair_spec = pl.BlockSpec((peers, 2, rows, HD), lambda h: (0, 0, 0, h))
    one_spec = pl.BlockSpec((peers, rows, HD), lambda h: (0, 0, h))

    def head_spec(*shape):
        return pl.BlockSpec((1,) + shape, lambda h: (h, 0, 0))

    pair_flops = heads * 2 * tokens * tokens * HD

    kv0 = swap(pack(key_rows, value_rows))
    edge = [(0, 1), (1, 0), (2, 3), (3, 2)]
    middle = [(1, 2), (2, 1)]
    kv3 = lax.ppermute(kv0, "frame", middle)
    kv1 = lax.ppermute(kv0, "frame", edge)
    qg = swap(pack(query_rows, out_grad))
    kv2b = lax.ppermute(kv1, "frame", middle)
    kv2a = lax.ppermute(kv3, "frame", [(1, 0), (2, 3)])

    e, acc, ml = pl.pallas_call(
        near_forward_kernel,
        grid=(heads,),
        in_specs=[smem, smem, pair_spec, pair_spec, pair_spec, pair_spec],
        out_specs=[head_spec(3 * tokens, tokens), head_spec(HD, tokens), head_spec(8, tokens)],
        out_shape=[
            jax.ShapeDtypeStruct((heads, 3 * tokens, tokens), BF16),
            jax.ShapeDtypeStruct((heads, HD, tokens), F32),
            jax.ShapeDtypeStruct((heads, 8, tokens), F32),
        ],
        compiler_params=params(),
        cost_estimate=cost(20 * pair_flops, 8 << 20),
    )(frame, block_mask, qg, kv0, kv1, kv3)

    dkv2, att, wd, dq2 = pl.pallas_call(
        far_kernel,
        grid=(heads,),
        in_specs=[
            smem, smem, pair_spec, pair_spec, pair_spec,
            head_spec(HD, tokens), head_spec(8, tokens),
        ],
        out_specs=[pair_spec, one_spec, head_spec(8, tokens), head_spec(HD, tokens)],
        out_shape=[
            pair_type,
            jax.ShapeDtypeStruct((peers, rows, width), BF16),
            jax.ShapeDtypeStruct((heads, 8, tokens), F32),
            jax.ShapeDtypeStruct((heads, HD, tokens), F32),
        ],
        compiler_params=params(),
        cost_estimate=cost(20 * pair_flops, 8 << 20),
    )(frame, block_mask, qg, kv2a, kv2b, acc, ml)

    back_edge = lax.ppermute(dkv2, "frame", [(0, 1), (3, 2)])
    back_middle = lax.ppermute(dkv2, "frame", middle)

    dkv0, dkv1, dkv3, att_dq = pl.pallas_call(
        near_backward_kernel,
        grid=(heads,),
        in_specs=[
            pair_spec, pair_spec, pair_spec, pair_spec,
            head_spec(3 * tokens, tokens), head_spec(8, tokens), head_spec(HD, tokens), one_spec,
        ],
        out_specs=[pair_spec] * 4,
        out_shape=[pair_type] * 4,
        compiler_params=params(),
        cost_estimate=cost(20 * pair_flops, 8 << 20),
    )(qg, kv0, kv1, kv3, e, wd, dq2, att)

    def added(*pairs):
        total = pairs[0].astype(F32)
        for pair in pairs[1:]:
            total = total + pair.astype(F32)
        return total.astype(BF16)

    last_middle = lax.ppermute(added(dkv3, back_edge), "frame", middle)
    last_edge = lax.ppermute(added(dkv1, back_middle), "frame", edge)
    attended, grad_query = unpack(swap(att_dq))
    grad_keys, grad_values = unpack(swap(added(dkv0, last_edge, last_middle)))
    return attended, grad_query, grad_keys, grad_values


def solution(mesh):
    seq, head = mesh.shape["seq"], mesh.shape["head"]
    frames = seq // GROUP
    line = Mesh(mesh.devices.reshape(frames, GROUP, head), ("frame", "rank", "head"))

    def run(query_rows, key_rows, value_rows, out_grad, block_mask):
        heads = query_rows.shape[1] // HD
        tokens = query_rows.shape[0] // frames
        fits = (
            frames == 4
            and block_mask.shape[0] == 2
            and heads % (GROUP * head) == 0
            and tokens == block_mask.shape[1] * BLOCK
            and tokens // (GROUP * head) % 16 == 0
        )
        if fits:
            body, where, axes = per_device_line, line, ("frame", "rank", "head")
        else:
            body, where, axes = per_device_general, mesh, ("seq", "head")
        row_spec = P(axes, None)
        return jax.shard_map(
            body,
            mesh=where,
            in_specs=(row_spec,) * 4 + (P(),),
            out_specs=(row_spec,) * 4,
            check_vma=False,
        )(query_rows, key_rows, value_rows, out_grad, block_mask)

    return run
```

```python
import math

import jax
import jax.numpy as jnp
from jax import lax
from jax.experimental import pallas as pl
from jax.experimental.pallas import tpu as pltpu
from jax.sharding import Mesh
from jax.sharding import PartitionSpec as P

HD = 128
BLOCK = 128
GROUP = 4
SCALE = 1.0 / math.sqrt(HD)
SCALE_LOG2 = SCALE * math.log2(math.e)
MASKED = -1e30
VMEM_BYTES = 40 * 1024 * 1024


def partner_2(shard, axis, distance):
    return lax.ppermute(shard, axis, [(i, i ^ 1 << distance) for i in range(lax.axis_size(axis))])


def passed_along(shard, axis, by):
    peers = lax.axis_size(axis)
    pairs = [(i, i + by) for i in range(peers) if 0 <= i + by < peers]
    return lax.ppermute(shard, axis, pairs)


def widen_mask(bits):
    blocks = bits.shape[0]
    grid = jnp.broadcast_to((bits > 0)[:, None, :, None], (blocks, BLOCK, blocks, BLOCK))
    return grid.reshape(blocks * BLOCK, blocks * BLOCK)


def place_pair(mine, other, is_low, dim):
    return lax.cond(
        is_low,
        lambda pair: jnp.concatenate([pair[0], pair[1]], dim),
        lambda pair: jnp.concatenate([pair[1], pair[0]], dim),
        (mine, other),
    )


def per_device_general(query_rows, key_rows, value_rows, out_grad, block_mask):
    queries, keys_local, values_local, grads_output = (
        lax.all_to_all(query_rows, "head", split_axis=1, concat_axis=0, tiled=True),
        lax.all_to_all(key_rows, "head", split_axis=1, concat_axis=0, tiled=True),
        lax.all_to_all(value_rows, "head", split_axis=1, concat_axis=0, tiled=True),
        lax.all_to_all(out_grad, "head", split_axis=1, concat_axis=0, tiled=True),
    )
    seq_index = lax.axis_index("seq")
    group_bits = GROUP.bit_length() - 1
    rank = seq_index % GROUP
    frame_index = seq_index // GROUP
    frame_count = lax.axis_size("seq") // GROUP
    level_count = block_mask.shape[0]
    block_rows = queries.shape[0]
    frame_tokens = block_rows * GROUP
    head_count = queries.shape[1] // HD
    score_scale = 1.0 / math.sqrt(HD)
    own_pair = jnp.stack([keys_local, values_local])

    def low_bit(bit):
        return seq_index >> bit & 1 == 0

    whole_pair = own_pair
    for bit in range(group_bits):
        other = partner_2(whole_pair, "seq", bit)
        whole_pair = place_pair(whole_pair, other, low_bit(bit), 1)
    partner_list = []
    for level_index in range(level_count):
        for orient in (1, -1):
            partner_list.append(
                passed_along(whole_pair, "seq", orient * GROUP * (1 << level_index))
            )
    every_pair = jnp.concatenate([whole_pair] + partner_list, axis=1)
    keys_all, values_all = (every_pair[0], every_pair[1])
    allowed_list = [jnp.ones((block_rows, frame_tokens), bool)]
    for level_index in range(level_count):
        for orient in (1, -1):
            partner = frame_index - orient * (1 << level_index)
            inside = (partner >= 0) & (partner < frame_count)
            allowed_list.append(
                lax.dynamic_slice_in_dim(
                    widen_mask(block_mask[level_index]), rank * block_rows, block_rows, 0
                )
                & inside
            )
    allowed = jnp.concatenate(allowed_list, axis=1)

    def head_scores(query_head, keys_head):
        scores = (
            jnp.einsum("qd,kd->qk", query_head, keys_head, preferred_element_type=jnp.float32)
            * score_scale
        )
        return jnp.where(allowed, scores, -jnp.inf)

    outputs = []
    logsums = []
    for head_index in range(head_count):
        columns = slice(head_index * HD, (head_index + 1) * HD)
        scores = head_scores(queries[:, columns], keys_all[:, columns])
        peak = jnp.max(scores, axis=1, keepdims=True)
        logsum = peak + jnp.log(jnp.sum(jnp.exp(scores - peak), axis=1, keepdims=True))
        weights = jnp.exp(scores - logsum).astype(jnp.bfloat16)
        outputs.append(
            jnp.dot(weights, values_all[:, columns], preferred_element_type=jnp.float32).astype(
                jnp.bfloat16
            )
        )
        logsums.append(logsum)
    attended = jnp.concatenate(outputs, axis=1)
    query_grads = []
    key_grads = []
    value_grads = []
    for head_index in range(head_count):
        columns = slice(head_index * HD, (head_index + 1) * HD)
        query_head = queries[:, columns]
        grad_head = grads_output[:, columns]
        scores = head_scores(query_head, keys_all[:, columns])
        probability = jnp.exp(scores - logsums[head_index])
        weights = probability.astype(jnp.bfloat16)
        grad_weights = jnp.einsum(
            "qd,kd->qk", grad_head, values_all[:, columns], preferred_element_type=jnp.float32
        )
        delta_row = jnp.sum(
            grad_head.astype(jnp.float32) * attended[:, columns].astype(jnp.float32),
            axis=1,
            keepdims=True,
        )
        grad_scores = (probability * (grad_weights - delta_row) * score_scale).astype(jnp.bfloat16)
        query_grads.append(
            jnp.dot(grad_scores, keys_all[:, columns], preferred_element_type=jnp.float32).astype(
                jnp.bfloat16
            )
        )
        key_grads.append(
            jnp.einsum(
                "qk,qd->kd", grad_scores, query_head, preferred_element_type=jnp.float32
            ).astype(jnp.bfloat16)
        )
        value_grads.append(
            jnp.einsum("qk,qd->kd", weights, grad_head, preferred_element_type=jnp.float32).astype(
                jnp.bfloat16
            )
        )
    grad_query = jnp.concatenate(query_grads, axis=1)
    grad_pair = jnp.stack(
        [jnp.concatenate(key_grads, axis=1), jnp.concatenate(value_grads, axis=1)]
    )
    total = grad_pair[:, :frame_tokens].astype(jnp.float32)
    piece_index = 1
    for level_index in range(level_count):
        for orient in (1, -1):
            piece = grad_pair[:, piece_index * frame_tokens : (piece_index + 1) * frame_tokens]
            returned = passed_along(piece, "seq", -orient * GROUP * (1 << level_index))
            total = total + returned.astype(jnp.float32)
            piece_index += 1
    for bit in reversed(range(group_bits)):
        half = total.shape[1] // 2
        first_half = total[:, :half]
        second_half = total[:, half:]
        is_low = low_bit(bit)
        outgoing = jnp.where(is_low, second_half, first_half)
        staying = jnp.where(is_low, first_half, second_half)
        total = staying + partner_2(outgoing, "seq", bit)
    grad_keys = total[0].astype(jnp.bfloat16)
    grad_values = total[1].astype(jnp.bfloat16)
    return (
        lax.all_to_all(attended, "head", split_axis=0, concat_axis=1, tiled=True),
        lax.all_to_all(grad_query, "head", split_axis=0, concat_axis=1, tiled=True),
        lax.all_to_all(grad_keys, "head", split_axis=0, concat_axis=1, tiled=True),
        lax.all_to_all(grad_values, "head", split_axis=0, concat_axis=1, tiled=True),
    )


NT = (((1,), (1,)), ((), ()))
F32 = jnp.float32
BF16 = jnp.bfloat16


def dot(a, b):
    return jnp.dot(a, b, preferred_element_type=F32)


def dot_nt(a, b):
    return lax.dot_general(a, b, NT, preferred_element_type=F32)


def rows_of(ref, which):
    part = ref[:, which]
    return part.reshape(part.shape[0] * part.shape[1], part.shape[2])


def flat(ref):
    return ref[...].reshape(ref.shape[0] * ref.shape[1], ref.shape[2])


def put(ref, rows):
    ref[...] = rows.reshape(ref.shape)


def put_rows(ref, which, rows):
    ref[:, which] = rows.reshape(ref.shape[0], ref.shape[2], ref.shape[3])


def bias_rows(mask_ref, level, valid, blocks):
    lane_block = lax.broadcasted_iota(jnp.int32, (1, blocks * BLOCK), 1) // BLOCK
    rows = []
    for key_block in range(blocks):
        row = jnp.zeros((1, blocks * BLOCK), F32)
        for query_block in range(blocks):
            open_ = (mask_ref[level, query_block, key_block] > 0) & valid
            value = jnp.where(open_, 0.0, MASKED).astype(F32)
            row = jnp.where(lane_block == query_block, value, row)
        rows.append(row)
    return rows


def masked_scores(keys, queries, bias):
    scores = dot_nt(keys, queries) * SCALE_LOG2
    if bias is None:
        return scores
    blocks = len(bias)
    return jnp.concatenate(
        [scores[j * BLOCK : (j + 1) * BLOCK] + bias[j] for j in range(blocks)], axis=0
    )


def near_scores_kernel(frame_ref, mask_ref, qg_ref, k0_ref, k1_ref, k3_ref, e_ref, ml_ref):
    tokens = e_ref.shape[2]
    blocks = tokens // BLOCK
    frame = frame_ref[0]
    inner = (frame == 1) | (frame == 2)
    queries = rows_of(qg_ref, 0)
    slots = (
        (k0_ref, None),
        (k1_ref, bias_rows(mask_ref, 0, frame >= 0, blocks)),
        (k3_ref, bias_rows(mask_ref, 0, inner, blocks)),
    )
    scores = [masked_scores(flat(ref), queries, bias) for ref, bias in slots]
    peak = scores[0].max(axis=0, keepdims=True)
    for score in scores[1:]:
        peak = jnp.maximum(peak, score.max(axis=0, keepdims=True))
    total = jnp.zeros((1, tokens), F32)
    for index, score in enumerate(scores):
        e = jnp.exp2(score - peak)
        total = total + e.sum(axis=0, keepdims=True)
        e_ref[0, index * tokens : (index + 1) * tokens] = e.astype(BF16)
    ml_ref[0, 0:1] = peak
    ml_ref[0, 1:2] = total


def far_scores_kernel(frame_ref, mask_ref, qg_ref, ka_ref, kb_ref, ml_ref, e_ref, w_ref, dv_ref):
    tokens = e_ref.shape[2]
    blocks = tokens // BLOCK
    frame = frame_ref[0]
    inner = (frame == 1) | (frame == 2)
    keys = jnp.where(inner, flat(kb_ref), flat(ka_ref))
    bias = bias_rows(mask_ref, 1, frame >= 0, blocks)
    scores = masked_scores(keys, rows_of(qg_ref, 0), bias)
    peak2 = scores.max(axis=0, keepdims=True)
    e = jnp.exp2(scores - peak2)
    total2 = e.sum(axis=0, keepdims=True)
    e = e.astype(BF16)
    peak1 = ml_ref[0, 0:1]
    peak = jnp.maximum(peak1, peak2)
    near = jnp.exp2(peak1 - peak)
    far = jnp.exp2(peak2 - peak)
    inv = 1.0 / (near * ml_ref[0, 1:2] + far * total2)
    far = far * inv
    scaled = (rows_of(qg_ref, 1).T.astype(F32) * far).astype(BF16)
    put(dv_ref, dot_nt(e, scaled).astype(BF16))
    e_ref[0] = e
    w_ref[0, 0:1] = near * inv
    w_ref[0, 1:2] = far


def near_values_kernel(qg_ref, e_ref, w_ref, v0_ref, v1_ref, v3_ref, dv0_ref, dv1_ref, dv3_ref, acc_ref):
    tokens = e_ref.shape[2]
    scaled = (rows_of(qg_ref, 1).T.astype(F32) * w_ref[0, 0:1]).astype(BF16)
    acc = jnp.zeros(acc_ref.shape[1:], F32)
    for index, (v_ref, dv_ref) in enumerate(
        ((v0_ref, dv0_ref), (v1_ref, dv1_ref), (v3_ref, dv3_ref))
    ):
        e = e_ref[0, index * tokens : (index + 1) * tokens]
        put(dv_ref, dot_nt(e, scaled).astype(BF16))
        acc = acc + dot(flat(v_ref).T, e)
    acc_ref[0] = acc


def far_values_kernel(
    frame_ref, qg_ref, ka_ref, kb_ref, va_ref, vb_ref, e_ref, w_ref, acc_ref,
    dk_ref, att_ref, delta_ref, dq_ref,
):
    frame = frame_ref[0]
    inner = (frame == 1) | (frame == 2)
    keys = jnp.where(inner, flat(kb_ref), flat(ka_ref))
    values = jnp.where(inner, flat(vb_ref), flat(va_ref))
    e = e_ref[0]
    near = w_ref[0, 0:1]
    far = w_ref[0, 1:2]
    out = (acc_ref[0] * near + dot(values.T, e) * far).astype(BF16)
    put(att_ref, out.T)
    grads = rows_of(qg_ref, 1).T.astype(F32)
    delta = (grads * out.astype(F32)).sum(axis=0, keepdims=True)
    delta_ref[0, 0:1] = near
    delta_ref[0, 1:2] = near * delta
    scaled = (grads * far).astype(BF16)
    ds = (e.astype(F32) * (dot(values, scaled) - far * delta)).astype(BF16)
    put(dk_ref, (dot(ds, rows_of(qg_ref, 0)) * SCALE).astype(BF16))
    dq_ref[0] = dot(keys.T, ds)


def near_keys_kernel(
    qg_ref, k0_ref, k1_ref, k3_ref, v0_ref, v1_ref, v3_ref, e_ref, delta_ref, dq2_ref, att_ref,
    dk0_ref, dk1_ref, dk3_ref, out_ref,
):
    tokens = e_ref.shape[2]
    queries = rows_of(qg_ref, 0)
    near = delta_ref[0, 0:1]
    delta = delta_ref[0, 1:2]
    scaled = (rows_of(qg_ref, 1).T.astype(F32) * near).astype(BF16)
    dq = dq2_ref[0]
    for index, (k_ref, v_ref, dk_ref) in enumerate(
        ((k0_ref, v0_ref, dk0_ref), (k1_ref, v1_ref, dk1_ref), (k3_ref, v3_ref, dk3_ref))
    ):
        e = e_ref[0, index * tokens : (index + 1) * tokens]
        ds = (e.astype(F32) * (dot(flat(v_ref), scaled) - delta)).astype(BF16)
        put(dk_ref, (dot(ds, queries) * SCALE).astype(BF16))
        dq = dq + dot(flat(k_ref).T, ds)
    put_rows(out_ref, 1, (dq * SCALE).astype(BF16).T)
    out_ref[:, 0] = att_ref[...]


def pack_kernel(in_ref, out_ref, sems):
    peers, _, width = out_ref.shape
    copies = [
        pltpu.make_async_copy(
            in_ref.at[:, peer * width : (peer + 1) * width], out_ref.at[peer], sems.at[peer]
        )
        for peer in range(peers)
    ]
    for copy in copies:
        copy.start()
    for copy in copies:
        copy.wait()


def pack_pair_kernel(a_ref, b_ref, out_ref, sems):
    peers, _, _, width = out_ref.shape
    copies = [
        pltpu.make_async_copy(
            ref.at[:, peer * width : (peer + 1) * width], out_ref.at[peer, which], sems.at[peer, which]
        )
        for peer in range(peers)
        for which, ref in enumerate((a_ref, b_ref))
    ]
    for copy in copies:
        copy.start()
    for copy in copies:
        copy.wait()


def unpack_kernel(in_ref, out_ref, sems):
    peers, _, width = in_ref.shape
    copies = [
        pltpu.make_async_copy(
            in_ref.at[peer], out_ref.at[:, peer * width : (peer + 1) * width], sems.at[peer]
        )
        for peer in range(peers)
    ]
    for copy in copies:
        copy.start()
    for copy in copies:
        copy.wait()


def unpack_pair_kernel(in_ref, a_ref, b_ref, sems):
    peers, _, _, width = in_ref.shape
    copies = [
        pltpu.make_async_copy(
            in_ref.at[peer, which], ref.at[:, peer * width : (peer + 1) * width], sems.at[peer, which]
        )
        for peer in range(peers)
        for which, ref in enumerate((a_ref, b_ref))
    ]
    for copy in copies:
        copy.start()
    for copy in copies:
        copy.wait()


def params():
    return pltpu.CompilerParams(vmem_limit_bytes=VMEM_BYTES)


def cost(flops, data):
    return pl.CostEstimate(flops=flops, bytes_accessed=data, transcendentals=0)


def per_device_line(query_rows, key_rows, value_rows, out_grad, block_mask):
    plane = ("rank", "head")
    peers = lax.axis_size("rank") * lax.axis_size("head")
    rows, columns = query_rows.shape
    width = columns // peers
    heads = width // HD
    tokens = peers * rows
    pair_type = jax.ShapeDtypeStruct((peers, 2, rows, width), BF16)
    one_type = jax.ShapeDtypeStruct((peers, rows, width), BF16)
    row_type = jax.ShapeDtypeStruct((rows, columns), BF16)
    frame = lax.axis_index("frame").astype(jnp.int32).reshape(1)
    anywhere = pl.BlockSpec(memory_space=pl.ANY)

    def moved(kernel, out_shape, sems, *operands):
        several = isinstance(out_shape, tuple)
        return pl.pallas_call(
            kernel,
            in_specs=[anywhere] * len(operands),
            out_specs=(anywhere,) * len(out_shape) if several else anywhere,
            out_shape=out_shape,
            scratch_shapes=[pltpu.SemaphoreType.DMA(sems)],
        )(*operands)

    def pack(rows_):
        return moved(pack_kernel, one_type, (peers,), rows_)

    def pack_pair(a, b):
        return moved(pack_pair_kernel, pair_type, (peers, 2), a, b)

    def unpack(one):
        return moved(unpack_kernel, row_type, (peers,), one)

    def unpack_pair(pair):
        return moved(unpack_pair_kernel, (row_type, row_type), (peers, 2), pair)

    def swap(pair):
        return lax.all_to_all(pair, plane, 0, 0, tiled=True)

    smem = pl.BlockSpec(memory_space=pltpu.SMEM)
    pair_spec = pl.BlockSpec((peers, 2, rows, HD), lambda h: (0, 0, 0, h))
    one_spec = pl.BlockSpec((peers, rows, HD), lambda h: (0, 0, h))

    def head_spec(*shape):
        return pl.BlockSpec((1,) + shape, lambda h: (h, 0, 0))

    def head_type(dtype, *shape):
        return jax.ShapeDtypeStruct((heads,) + shape, dtype)

    near_spec, near_type = head_spec(3 * tokens, tokens), head_type(BF16, 3 * tokens, tokens)
    far_spec, far_type = head_spec(tokens, tokens), head_type(BF16, tokens, tokens)
    stat_spec, stat_type = head_spec(8, tokens), head_type(F32, 8, tokens)
    acc_spec, acc_type = head_spec(HD, tokens), head_type(F32, HD, tokens)
    pair_flops = heads * 2 * tokens * tokens * HD

    def by_head(kernel, in_specs, outs, work):
        return pl.pallas_call(
            kernel,
            grid=(heads,),
            in_specs=in_specs,
            out_specs=[spec for spec, _ in outs],
            out_shape=[kind for _, kind in outs],
            compiler_params=params(),
            cost_estimate=cost(work * pair_flops, 4 << 20),
        )

    edge = [(0, 1), (1, 0), (2, 3), (3, 2)]
    inward = [(0, 1), (3, 2)]
    outward = [(1, 0), (2, 3)]
    middle = [(1, 2), (2, 1)]

    def send(array, pairs):
        return lax.ppermute(array, "frame", pairs)

    k0 = swap(pack(key_rows))
    k1, k3 = send(k0, edge), send(k0, middle)
    qg = swap(pack_pair(query_rows, out_grad))
    v0 = swap(pack(value_rows))
    v1, v3 = send(v0, edge), send(v0, middle)
    k2a, k2b = send(k3, outward), send(k1, middle)

    e_near, ml = by_head(
        near_scores_kernel,
        [smem, smem, pair_spec, one_spec, one_spec, one_spec],
        [(near_spec, near_type), (stat_spec, stat_type)],
        6,
    )(frame, block_mask, qg, k0, k1, k3)
    v2a, v2b = send(v3, outward), send(v1, middle)
    e_far, w, dv2 = by_head(
        far_scores_kernel,
        [smem, smem, pair_spec, one_spec, one_spec, stat_spec],
        [(far_spec, far_type), (stat_spec, stat_type), (one_spec, one_type)],
        6,
    )(frame, block_mask, qg, k2a, k2b, ml)
    dv_edge, dv_middle = send(dv2, inward), send(dv2, middle)
    dv0, dv1, dv3, acc = by_head(
        near_values_kernel,
        [pair_spec, near_spec, stat_spec, one_spec, one_spec, one_spec],
        [(one_spec, one_type)] * 3 + [(acc_spec, acc_type)],
        6,
    )(qg, e_near, w, v0, v1, v3)
    dk2, att, delta, dq2 = by_head(
        far_values_kernel,
        [smem, pair_spec] + [one_spec] * 4 + [far_spec, stat_spec, acc_spec],
        [(one_spec, one_type), (one_spec, one_type), (stat_spec, stat_type), (acc_spec, acc_type)],
        6,
    )(frame, qg, k2a, k2b, v2a, v2b, e_far, w, acc)
    dk_edge, dk_middle = send(dk2, inward), send(dk2, middle)
    dk0, dk1, dk3, att_dq = by_head(
        near_keys_kernel,
        [pair_spec] + [one_spec] * 6 + [near_spec, stat_spec, acc_spec, one_spec],
        [(one_spec, one_type)] * 3 + [(pair_spec, pair_type)],
        9,
    )(qg, k0, k1, k3, v0, v1, v3, e_near, delta, dq2, att)

    def added(*parts):
        total = parts[0].astype(F32)
        for part in parts[1:]:
            total = total + part.astype(F32)
        return total.astype(BF16)

    def last_round(own, first, third, from_edge, from_middle):
        over_middle = send(added(third, from_edge), middle)
        over_edge = send(added(first, from_middle), edge)
        return unpack(swap(added(own, over_edge, over_middle)))

    grad_values = last_round(dv0, dv1, dv3, dv_edge, dv_middle)
    attended, grad_query = unpack_pair(swap(att_dq))
    grad_keys = last_round(dk0, dk1, dk3, dk_edge, dk_middle)
    return attended, grad_query, grad_keys, grad_values


def solution(mesh):
    seq, head = mesh.shape["seq"], mesh.shape["head"]
    frames = seq // GROUP
    line = Mesh(mesh.devices.reshape(frames, GROUP, head), ("frame", "rank", "head"))

    def run(query_rows, key_rows, value_rows, out_grad, block_mask):
        heads = query_rows.shape[1] // HD
        tokens = query_rows.shape[0] // frames
        fits = (
            frames == 4
            and block_mask.shape[0] == 2
            and heads % (GROUP * head) == 0
            and tokens == block_mask.shape[1] * BLOCK
            and tokens // (GROUP * head) % 16 == 0
        )
        if fits:
            body, where, axes = per_device_line, line, ("frame", "rank", "head")
        else:
            body, where, axes = per_device_general, mesh, ("seq", "head")
        row_spec = P(axes, None)
        return jax.shard_map(
            body,
            mesh=where,
            in_specs=(row_spec,) * 4 + (P(),),
            out_specs=(row_spec,) * 4,
            check_vma=False,
        )(query_rows, key_rows, value_rows, out_grad, block_mask)

    return run
```

```python
import math

import jax
import jax.numpy as jnp
from jax import lax
from jax.experimental import pallas as pl
from jax.experimental.pallas import tpu as pltpu
from jax.sharding import Mesh
from jax.sharding import PartitionSpec as P

HD = 128
BLOCK = 128
GROUP = 4
SCALE = 1.0 / math.sqrt(HD)
SCALE_LOG2 = SCALE * math.log2(math.e)
MASKED = -1e30
VMEM_BYTES = 24 * 1024 * 1024


def partner_2(shard, axis, distance):
    return lax.ppermute(shard, axis, [(i, i ^ 1 << distance) for i in range(lax.axis_size(axis))])


def passed_along(shard, axis, by):
    peers = lax.axis_size(axis)
    pairs = [(i, i + by) for i in range(peers) if 0 <= i + by < peers]
    return lax.ppermute(shard, axis, pairs)


def widen_mask(bits):
    blocks = bits.shape[0]
    grid = jnp.broadcast_to((bits > 0)[:, None, :, None], (blocks, BLOCK, blocks, BLOCK))
    return grid.reshape(blocks * BLOCK, blocks * BLOCK)


def place_pair(mine, other, is_low, dim):
    return lax.cond(
        is_low,
        lambda pair: jnp.concatenate([pair[0], pair[1]], dim),
        lambda pair: jnp.concatenate([pair[1], pair[0]], dim),
        (mine, other),
    )


def per_device_general(query_rows, key_rows, value_rows, out_grad, block_mask):
    queries, keys_local, values_local, grads_output = (
        lax.all_to_all(query_rows, "head", split_axis=1, concat_axis=0, tiled=True),
        lax.all_to_all(key_rows, "head", split_axis=1, concat_axis=0, tiled=True),
        lax.all_to_all(value_rows, "head", split_axis=1, concat_axis=0, tiled=True),
        lax.all_to_all(out_grad, "head", split_axis=1, concat_axis=0, tiled=True),
    )
    seq_index = lax.axis_index("seq")
    group_bits = GROUP.bit_length() - 1
    rank = seq_index % GROUP
    frame_index = seq_index // GROUP
    frame_count = lax.axis_size("seq") // GROUP
    level_count = block_mask.shape[0]
    block_rows = queries.shape[0]
    frame_tokens = block_rows * GROUP
    head_count = queries.shape[1] // HD
    score_scale = 1.0 / math.sqrt(HD)
    own_pair = jnp.stack([keys_local, values_local])

    def low_bit(bit):
        return seq_index >> bit & 1 == 0

    whole_pair = own_pair
    for bit in range(group_bits):
        other = partner_2(whole_pair, "seq", bit)
        whole_pair = place_pair(whole_pair, other, low_bit(bit), 1)
    partner_list = []
    for level_index in range(level_count):
        for orient in (1, -1):
            partner_list.append(
                passed_along(whole_pair, "seq", orient * GROUP * (1 << level_index))
            )
    every_pair = jnp.concatenate([whole_pair] + partner_list, axis=1)
    keys_all, values_all = (every_pair[0], every_pair[1])
    allowed_list = [jnp.ones((block_rows, frame_tokens), bool)]
    for level_index in range(level_count):
        for orient in (1, -1):
            partner = frame_index - orient * (1 << level_index)
            inside = (partner >= 0) & (partner < frame_count)
            allowed_list.append(
                lax.dynamic_slice_in_dim(
                    widen_mask(block_mask[level_index]), rank * block_rows, block_rows, 0
                )
                & inside
            )
    allowed = jnp.concatenate(allowed_list, axis=1)

    def head_scores(query_head, keys_head):
        scores = (
            jnp.einsum("qd,kd->qk", query_head, keys_head, preferred_element_type=jnp.float32)
            * score_scale
        )
        return jnp.where(allowed, scores, -jnp.inf)

    outputs = []
    logsums = []
    for head_index in range(head_count):
        columns = slice(head_index * HD, (head_index + 1) * HD)
        scores = head_scores(queries[:, columns], keys_all[:, columns])
        peak = jnp.max(scores, axis=1, keepdims=True)
        logsum = peak + jnp.log(jnp.sum(jnp.exp(scores - peak), axis=1, keepdims=True))
        weights = jnp.exp(scores - logsum).astype(jnp.bfloat16)
        outputs.append(
            jnp.dot(weights, values_all[:, columns], preferred_element_type=jnp.float32).astype(
                jnp.bfloat16
            )
        )
        logsums.append(logsum)
    attended = jnp.concatenate(outputs, axis=1)
    query_grads = []
    key_grads = []
    value_grads = []
    for head_index in range(head_count):
        columns = slice(head_index * HD, (head_index + 1) * HD)
        query_head = queries[:, columns]
        grad_head = grads_output[:, columns]
        scores = head_scores(query_head, keys_all[:, columns])
        probability = jnp.exp(scores - logsums[head_index])
        weights = probability.astype(jnp.bfloat16)
        grad_weights = jnp.einsum(
            "qd,kd->qk", grad_head, values_all[:, columns], preferred_element_type=jnp.float32
        )
        delta_row = jnp.sum(
            grad_head.astype(jnp.float32) * attended[:, columns].astype(jnp.float32),
            axis=1,
            keepdims=True,
        )
        grad_scores = (probability * (grad_weights - delta_row) * score_scale).astype(jnp.bfloat16)
        query_grads.append(
            jnp.dot(grad_scores, keys_all[:, columns], preferred_element_type=jnp.float32).astype(
                jnp.bfloat16
            )
        )
        key_grads.append(
            jnp.einsum(
                "qk,qd->kd", grad_scores, query_head, preferred_element_type=jnp.float32
            ).astype(jnp.bfloat16)
        )
        value_grads.append(
            jnp.einsum("qk,qd->kd", weights, grad_head, preferred_element_type=jnp.float32).astype(
                jnp.bfloat16
            )
        )
    grad_query = jnp.concatenate(query_grads, axis=1)
    grad_pair = jnp.stack(
        [jnp.concatenate(key_grads, axis=1), jnp.concatenate(value_grads, axis=1)]
    )
    total = grad_pair[:, :frame_tokens].astype(jnp.float32)
    piece_index = 1
    for level_index in range(level_count):
        for orient in (1, -1):
            piece = grad_pair[:, piece_index * frame_tokens : (piece_index + 1) * frame_tokens]
            returned = passed_along(piece, "seq", -orient * GROUP * (1 << level_index))
            total = total + returned.astype(jnp.float32)
            piece_index += 1
    for bit in reversed(range(group_bits)):
        half = total.shape[1] // 2
        first_half = total[:, :half]
        second_half = total[:, half:]
        is_low = low_bit(bit)
        outgoing = jnp.where(is_low, second_half, first_half)
        staying = jnp.where(is_low, first_half, second_half)
        total = staying + partner_2(outgoing, "seq", bit)
    grad_keys = total[0].astype(jnp.bfloat16)
    grad_values = total[1].astype(jnp.bfloat16)
    return (
        lax.all_to_all(attended, "head", split_axis=0, concat_axis=1, tiled=True),
        lax.all_to_all(grad_query, "head", split_axis=0, concat_axis=1, tiled=True),
        lax.all_to_all(grad_keys, "head", split_axis=0, concat_axis=1, tiled=True),
        lax.all_to_all(grad_values, "head", split_axis=0, concat_axis=1, tiled=True),
    )


NT = (((1,), (1,)), ((), ()))
F32 = jnp.float32
BF16 = jnp.bfloat16


def dot(a, b):
    return jnp.dot(a, b, preferred_element_type=F32)


def dot_nt(a, b):
    return lax.dot_general(a, b, NT, preferred_element_type=F32)


def head_columns(head):
    return slice(head * HD, (head + 1) * HD)


def flat(ref, head):
    part = ref[:, :, head_columns(head)]
    return part.reshape(part.shape[0] * part.shape[1], HD)


def put(ref, head, rows):
    ref[:, :, head_columns(head)] = rows.reshape(ref.shape[0], ref.shape[1], HD)


def bias_rows(mask_ref, level, valid, blocks):
    lane_block = lax.broadcasted_iota(jnp.int32, (1, blocks * BLOCK), 1) // BLOCK
    rows = []
    for key_block in range(blocks):
        row = jnp.zeros((1, blocks * BLOCK), F32)
        for query_block in range(blocks):
            open_ = (mask_ref[level, query_block, key_block] > 0) & valid
            value = jnp.where(open_, 0.0, MASKED).astype(F32)
            row = jnp.where(lane_block == query_block, value, row)
        rows.append(row)
    return rows


def masked_scores(keys, queries, bias):
    scores = dot_nt(keys, queries) * SCALE_LOG2
    if bias is None:
        return scores
    blocks = len(bias)
    return jnp.concatenate(
        [scores[j * BLOCK : (j + 1) * BLOCK] + bias[j] for j in range(blocks)], axis=0
    )


def near_scores_kernel(frame_ref, mask_ref, q_ref, k0_ref, k1_ref, k3_ref, e_ref, ml_ref):
    heads, _, tokens = e_ref.shape
    blocks = tokens // BLOCK
    frame = frame_ref[0]
    inner = (frame == 1) | (frame == 2)
    bias1 = bias_rows(mask_ref, 0, frame >= 0, blocks)
    bias3 = bias_rows(mask_ref, 0, inner, blocks)
    for head in range(heads):
        queries = flat(q_ref, head)
        slots = ((k0_ref, None), (k1_ref, bias1), (k3_ref, bias3))
        scores = [masked_scores(flat(ref, head), queries, bias) for ref, bias in slots]
        peak = scores[0].max(axis=0, keepdims=True)
        for score in scores[1:]:
            peak = jnp.maximum(peak, score.max(axis=0, keepdims=True))
        total = jnp.zeros((1, tokens), F32)
        for index, score in enumerate(scores):
            e = jnp.exp2(score - peak)
            total = total + e.sum(axis=0, keepdims=True)
            e_ref[head, index * tokens : (index + 1) * tokens] = e.astype(BF16)
        ml_ref[head, 0:1] = peak
        ml_ref[head, 1:2] = total


def far_scores_kernel(frame_ref, mask_ref, q_ref, g_ref, ka_ref, kb_ref, ml_ref, e_ref, w_ref, dv_ref):
    heads, _, tokens = e_ref.shape
    blocks = tokens // BLOCK
    frame = frame_ref[0]
    inner = (frame == 1) | (frame == 2)
    bias = bias_rows(mask_ref, 1, frame >= 0, blocks)
    for head in range(heads):
        keys = jnp.where(inner, flat(kb_ref, head), flat(ka_ref, head))
        scores = masked_scores(keys, flat(q_ref, head), bias)
        peak2 = scores.max(axis=0, keepdims=True)
        e = jnp.exp2(scores - peak2)
        total2 = e.sum(axis=0, keepdims=True)
        e = e.astype(BF16)
        peak1 = ml_ref[head, 0:1]
        peak = jnp.maximum(peak1, peak2)
        near = jnp.exp2(peak1 - peak)
        far = jnp.exp2(peak2 - peak)
        inv = 1.0 / (near * ml_ref[head, 1:2] + far * total2)
        far = far * inv
        scaled = (flat(g_ref, head).T.astype(F32) * far).astype(BF16)
        put(dv_ref, head, dot_nt(e, scaled).astype(BF16))
        e_ref[head] = e
        w_ref[head, 0:1] = near * inv
        w_ref[head, 1:2] = far


def near_values_kernel(g_ref, e_ref, w_ref, v0_ref, v1_ref, v3_ref, dv0_ref, dv1_ref, dv3_ref, acc_ref):
    heads, _, tokens = e_ref.shape
    for head in range(heads):
        scaled = (flat(g_ref, head).T.astype(F32) * w_ref[head, 0:1]).astype(BF16)
        acc = jnp.zeros((HD, tokens), F32)
        for index, (v_ref, dv_ref) in enumerate(
            ((v0_ref, dv0_ref), (v1_ref, dv1_ref), (v3_ref, dv3_ref))
        ):
            e = e_ref[head, index * tokens : (index + 1) * tokens]
            put(dv_ref, head, dot_nt(e, scaled).astype(BF16))
            acc = acc + dot(flat(v_ref, head).T, e)
        acc_ref[head] = acc


def far_values_kernel(
    frame_ref, q_ref, g_ref, ka_ref, kb_ref, va_ref, vb_ref, e_ref, w_ref, acc_ref,
    dk_ref, att_ref, delta_ref, dq_ref,
):
    heads = e_ref.shape[0]
    frame = frame_ref[0]
    inner = (frame == 1) | (frame == 2)
    for head in range(heads):
        keys = jnp.where(inner, flat(kb_ref, head), flat(ka_ref, head))
        values = jnp.where(inner, flat(vb_ref, head), flat(va_ref, head))
        e = e_ref[head]
        near = w_ref[head, 0:1]
        far = w_ref[head, 1:2]
        out = (acc_ref[head] * near + dot(values.T, e) * far).astype(BF16)
        put(att_ref, head, out.T)
        grads = flat(g_ref, head).T.astype(F32)
        delta = (grads * out.astype(F32)).sum(axis=0, keepdims=True)
        delta_ref[head, 0:1] = near
        delta_ref[head, 1:2] = near * delta
        scaled = (grads * far).astype(BF16)
        ds = (e.astype(F32) * (dot(values, scaled) - far * delta)).astype(BF16)
        put(dk_ref, head, (dot(ds, flat(q_ref, head)) * SCALE).astype(BF16))
        dq_ref[head] = dot(keys.T, ds)


def near_keys_kernel(
    q_ref, g_ref, k0_ref, k1_ref, k3_ref, v0_ref, v1_ref, v3_ref, e_ref, delta_ref, dq2_ref,
    dk0_ref, dk1_ref, dk3_ref, dq_ref,
):
    heads, _, tokens = e_ref.shape
    for head in range(heads):
        queries = flat(q_ref, head)
        near = delta_ref[head, 0:1]
        delta = delta_ref[head, 1:2]
        scaled = (flat(g_ref, head).T.astype(F32) * near).astype(BF16)
        dq = dq2_ref[head]
        for index, (k_ref, v_ref, dk_ref) in enumerate(
            ((k0_ref, v0_ref, dk0_ref), (k1_ref, v1_ref, dk1_ref), (k3_ref, v3_ref, dk3_ref))
        ):
            e = e_ref[head, index * tokens : (index + 1) * tokens]
            ds = (e.astype(F32) * (dot(flat(v_ref, head), scaled) - delta)).astype(BF16)
            put(dk_ref, head, (dot(ds, queries) * SCALE).astype(BF16))
            dq = dq + dot(flat(k_ref, head).T, ds)
        put(dq_ref, head, (dq * SCALE).astype(BF16).T)


def add_kernel(frame_ref, own_ref, other_ref, out_ref):
    out_ref[...] = (own_ref[...].astype(F32) + other_ref[...].astype(F32)).astype(BF16)


def add_inner_kernel(frame_ref, own_ref, other_ref, out_ref):
    inner = (frame_ref[0] == 1) | (frame_ref[0] == 2)

    @pl.when(inner)
    def _():
        out_ref[...] = (own_ref[...].astype(F32) + other_ref[...].astype(F32)).astype(BF16)

    @pl.when(jnp.logical_not(inner))
    def _():
        out_ref[...] = own_ref[...]


def last_sum(frame_ref, own_ref, edge_ref, middle_ref):
    inner = (frame_ref[0] == 1) | (frame_ref[0] == 2)
    total = own_ref[...].astype(F32) + edge_ref[...].astype(F32)
    return (total + jnp.where(inner, middle_ref[...].astype(F32), 0.0)).astype(BF16)


def last_add_kernel(frame_ref, own_ref, edge_ref, middle_ref, out_ref):
    out_ref[...] = last_sum(frame_ref, own_ref, edge_ref, middle_ref)


def collect_kernel(frame_ref, own_ref, edge_ref, middle_ref, att_ref, dq_ref, out_ref):
    out_ref[:, 0] = att_ref[...]
    out_ref[:, 1] = dq_ref[...]
    out_ref[:, 2] = last_sum(frame_ref, own_ref, edge_ref, middle_ref)


def pack_kernel(in_ref, out_ref):
    peers, _, width = out_ref.shape
    for peer in range(peers):
        out_ref[peer] = in_ref[:, peer * width : (peer + 1) * width]


def unpack_kernel(in_ref, out_ref):
    peers, _, width = in_ref.shape
    for peer in range(peers):
        out_ref[:, peer * width : (peer + 1) * width] = in_ref[peer]


def unpack_three_kernel(in_ref, a_ref, b_ref, c_ref):
    peers, _, _, width = in_ref.shape
    for peer in range(peers):
        for which, ref in enumerate((a_ref, b_ref, c_ref)):
            ref[:, peer * width : (peer + 1) * width] = in_ref[peer, which]


def params():
    return pltpu.CompilerParams(vmem_limit_bytes=VMEM_BYTES)


def cost(flops, data):
    return pl.CostEstimate(flops=flops, bytes_accessed=data, transcendentals=0)


def per_device_line(query_rows, key_rows, value_rows, out_grad, block_mask):
    plane = ("rank", "head")
    peers = lax.axis_size("rank") * lax.axis_size("head")
    rows, columns = query_rows.shape
    width = columns // peers
    heads = width // HD
    tokens = peers * rows
    one = jax.ShapeDtypeStruct((peers, rows, width), BF16)
    row_type = jax.ShapeDtypeStruct((rows, columns), BF16)
    near_e = jax.ShapeDtypeStruct((heads, 3 * tokens, tokens), BF16)
    far_e = jax.ShapeDtypeStruct((heads, tokens, tokens), BF16)
    stat = jax.ShapeDtypeStruct((heads, 8, tokens), F32)
    sums = jax.ShapeDtypeStruct((heads, HD, tokens), F32)
    frame = lax.axis_index("frame").astype(jnp.int32).reshape(1)
    smem = pl.BlockSpec(memory_space=pltpu.SMEM)
    vmem = pl.BlockSpec(memory_space=pltpu.VMEM)
    pair_flops = heads * 2 * tokens * tokens * HD

    def call(kernel, outs, work, *operands):
        several = isinstance(outs, tuple)
        return pl.pallas_call(
            kernel,
            in_specs=[smem if x.dtype == jnp.int32 else vmem for x in operands],
            out_specs=(vmem,) * len(outs) if several else vmem,
            out_shape=outs,
            compiler_params=params(),
            cost_estimate=cost(work * pair_flops, 4 << 20),
        )(*operands)

    def swap(array):
        return lax.all_to_all(array, plane, 0, 0, tiled=True)

    def enter(rows_):
        return swap(call(pack_kernel, one, 0, rows_))

    def leave(array):
        return call(unpack_kernel, row_type, 0, swap(array))

    devices = ("frame", "rank", "head")
    heads_axis = lax.axis_size("head")

    def pairs_of(partner):
        pairs = []
        for frame_ in range(4):
            for rank in range(GROUP):
                for part in range(heads_axis):
                    there = partner.get(frame_)
                    place = (frame_, rank ^ 1) if there is None else (there, rank)
                    pairs.append(
                        (
                            (frame_ * GROUP + rank) * heads_axis + part,
                            (place[0] * GROUP + place[1]) * heads_axis + part,
                        )
                    )
        return pairs

    edge = pairs_of({0: 1, 1: 0, 2: 3, 3: 2})
    middle = pairs_of({1: 2, 2: 1})

    def send(array, pairs):
        return lax.ppermute(array, devices, pairs)

    k0 = enter(key_rows)
    k1, k3 = send(k0, edge), send(k0, middle)
    q = enter(query_rows)
    v0 = enter(value_rows)
    g = enter(out_grad)
    k2a, k2b = send(k3, edge), send(k1, middle)
    v1, v3 = send(v0, edge), send(v0, middle)
    v2a, v2b = send(v3, edge), send(v1, middle)

    e_near, ml = call(
        near_scores_kernel, (near_e, stat), 6, frame, block_mask, q, k0, k1, k3
    )
    e_far, w, dv2 = call(
        far_scores_kernel, (far_e, stat, one), 4, frame, block_mask, q, g, k2a, k2b, ml
    )
    dv_edge, dv_middle = send(dv2, edge), send(dv2, middle)
    dv0, dv1, dv3, acc = call(
        near_values_kernel, (one, one, one, sums), 6, g, e_near, w, v0, v1, v3
    )
    dk2, att, delta, dq2 = call(
        far_values_kernel, (one, one, stat, sums), 4, frame, q, g, k2a, k2b, v2a, v2b, e_far, w, acc
    )
    dk_edge, dk_middle = send(dk2, edge), send(dk2, middle)
    dk0, dk1, dk3, dq = call(
        near_keys_kernel, (one, one, one, one), 9, q, g, k0, k1, k3, v0, v1, v3, e_near, delta, dq2
    )

    def last_round(first, third, from_edge, from_middle):
        over_middle = send(call(add_kernel, one, 0, frame, third, from_edge), middle)
        over_edge = send(call(add_inner_kernel, one, 0, frame, first, from_middle), edge)
        return over_edge, over_middle

    over = last_round(dv1, dv3, dv_edge, dv_middle)
    three = jax.ShapeDtypeStruct((peers, 3, rows, width), BF16)
    collected = swap(call(collect_kernel, three, 0, frame, dv0, *over, att, dq))
    over = last_round(dk1, dk3, dk_edge, dk_middle)
    attended, grad_query, grad_values = call(
        unpack_three_kernel, (row_type, row_type, row_type), 0, collected
    )
    grad_keys = leave(call(last_add_kernel, one, 0, frame, dk0, *over))
    return attended, grad_query, grad_keys, grad_values


def solution(mesh):
    seq, head = mesh.shape["seq"], mesh.shape["head"]
    frames = seq // GROUP
    line = Mesh(mesh.devices.reshape(frames, GROUP, head), ("frame", "rank", "head"))

    def run(query_rows, key_rows, value_rows, out_grad, block_mask):
        heads = query_rows.shape[1] // HD
        tokens = query_rows.shape[0] // frames
        fits = (
            frames == 4
            and block_mask.shape[0] == 2
            and heads % (GROUP * head) == 0
            and tokens == block_mask.shape[1] * BLOCK
            and tokens // (GROUP * head) % 16 == 0
        )
        if fits:
            body, where, axes = per_device_line, line, ("frame", "rank", "head")
        else:
            body, where, axes = per_device_general, mesh, ("seq", "head")
        row_spec = P(axes, None)
        return jax.shard_map(
            body,
            mesh=where,
            in_specs=(row_spec,) * 4 + (P(),),
            out_specs=(row_spec,) * 4,
            check_vma=False,
        )(query_rows, key_rows, value_rows, out_grad, block_mask)

    return run
```

```python
import math

import jax
import jax.numpy as jnp
from jax import lax
from jax.experimental import pallas as pl
from jax.experimental.pallas import tpu as pltpu
from jax.sharding import Mesh
from jax.sharding import PartitionSpec as P

HD = 128
BLOCK = 128
GROUP = 4
SCALE = 1.0 / math.sqrt(HD)
SCALE_LOG2 = SCALE * math.log2(math.e)
MASKED = -1e30
VMEM_BYTES = 12 * 1024 * 1024


def partner_2(shard, axis, distance):
    return lax.ppermute(shard, axis, [(i, i ^ 1 << distance) for i in range(lax.axis_size(axis))])


def passed_along(shard, axis, by):
    peers = lax.axis_size(axis)
    pairs = [(i, i + by) for i in range(peers) if 0 <= i + by < peers]
    return lax.ppermute(shard, axis, pairs)


def widen_mask(bits):
    blocks = bits.shape[0]
    grid = jnp.broadcast_to((bits > 0)[:, None, :, None], (blocks, BLOCK, blocks, BLOCK))
    return grid.reshape(blocks * BLOCK, blocks * BLOCK)


def place_pair(mine, other, is_low, dim):
    return lax.cond(
        is_low,
        lambda pair: jnp.concatenate([pair[0], pair[1]], dim),
        lambda pair: jnp.concatenate([pair[1], pair[0]], dim),
        (mine, other),
    )


def per_device_general(query_rows, key_rows, value_rows, out_grad, block_mask):
    queries, keys_local, values_local, grads_output = (
        lax.all_to_all(query_rows, "head", split_axis=1, concat_axis=0, tiled=True),
        lax.all_to_all(key_rows, "head", split_axis=1, concat_axis=0, tiled=True),
        lax.all_to_all(value_rows, "head", split_axis=1, concat_axis=0, tiled=True),
        lax.all_to_all(out_grad, "head", split_axis=1, concat_axis=0, tiled=True),
    )
    seq_index = lax.axis_index("seq")
    group_bits = GROUP.bit_length() - 1
    rank = seq_index % GROUP
    frame_index = seq_index // GROUP
    frame_count = lax.axis_size("seq") // GROUP
    level_count = block_mask.shape[0]
    block_rows = queries.shape[0]
    frame_tokens = block_rows * GROUP
    head_count = queries.shape[1] // HD
    score_scale = 1.0 / math.sqrt(HD)
    own_pair = jnp.stack([keys_local, values_local])

    def low_bit(bit):
        return seq_index >> bit & 1 == 0

    whole_pair = own_pair
    for bit in range(group_bits):
        other = partner_2(whole_pair, "seq", bit)
        whole_pair = place_pair(whole_pair, other, low_bit(bit), 1)
    partner_list = []
    for level_index in range(level_count):
        for orient in (1, -1):
            partner_list.append(
                passed_along(whole_pair, "seq", orient * GROUP * (1 << level_index))
            )
    every_pair = jnp.concatenate([whole_pair] + partner_list, axis=1)
    keys_all, values_all = (every_pair[0], every_pair[1])
    allowed_list = [jnp.ones((block_rows, frame_tokens), bool)]
    for level_index in range(level_count):
        for orient in (1, -1):
            partner = frame_index - orient * (1 << level_index)
            inside = (partner >= 0) & (partner < frame_count)
            allowed_list.append(
                lax.dynamic_slice_in_dim(
                    widen_mask(block_mask[level_index]), rank * block_rows, block_rows, 0
                )
                & inside
            )
    allowed = jnp.concatenate(allowed_list, axis=1)

    def head_scores(query_head, keys_head):
        scores = (
            jnp.einsum("qd,kd->qk", query_head, keys_head, preferred_element_type=jnp.float32)
            * score_scale
        )
        return jnp.where(allowed, scores, -jnp.inf)

    outputs = []
    logsums = []
    for head_index in range(head_count):
        columns = slice(head_index * HD, (head_index + 1) * HD)
        scores = head_scores(queries[:, columns], keys_all[:, columns])
        peak = jnp.max(scores, axis=1, keepdims=True)
        logsum = peak + jnp.log(jnp.sum(jnp.exp(scores - peak), axis=1, keepdims=True))
        weights = jnp.exp(scores - logsum).astype(jnp.bfloat16)
        outputs.append(
            jnp.dot(weights, values_all[:, columns], preferred_element_type=jnp.float32).astype(
                jnp.bfloat16
            )
        )
        logsums.append(logsum)
    attended = jnp.concatenate(outputs, axis=1)
    query_grads = []
    key_grads = []
    value_grads = []
    for head_index in range(head_count):
        columns = slice(head_index * HD, (head_index + 1) * HD)
        query_head = queries[:, columns]
        grad_head = grads_output[:, columns]
        scores = head_scores(query_head, keys_all[:, columns])
        probability = jnp.exp(scores - logsums[head_index])
        weights = probability.astype(jnp.bfloat16)
        grad_weights = jnp.einsum(
            "qd,kd->qk", grad_head, values_all[:, columns], preferred_element_type=jnp.float32
        )
        delta_row = jnp.sum(
            grad_head.astype(jnp.float32) * attended[:, columns].astype(jnp.float32),
            axis=1,
            keepdims=True,
        )
        grad_scores = (probability * (grad_weights - delta_row) * score_scale).astype(jnp.bfloat16)
        query_grads.append(
            jnp.dot(grad_scores, keys_all[:, columns], preferred_element_type=jnp.float32).astype(
                jnp.bfloat16
            )
        )
        key_grads.append(
            jnp.einsum(
                "qk,qd->kd", grad_scores, query_head, preferred_element_type=jnp.float32
            ).astype(jnp.bfloat16)
        )
        value_grads.append(
            jnp.einsum("qk,qd->kd", weights, grad_head, preferred_element_type=jnp.float32).astype(
                jnp.bfloat16
            )
        )
    grad_query = jnp.concatenate(query_grads, axis=1)
    grad_pair = jnp.stack(
        [jnp.concatenate(key_grads, axis=1), jnp.concatenate(value_grads, axis=1)]
    )
    total = grad_pair[:, :frame_tokens].astype(jnp.float32)
    piece_index = 1
    for level_index in range(level_count):
        for orient in (1, -1):
            piece = grad_pair[:, piece_index * frame_tokens : (piece_index + 1) * frame_tokens]
            returned = passed_along(piece, "seq", -orient * GROUP * (1 << level_index))
            total = total + returned.astype(jnp.float32)
            piece_index += 1
    for bit in reversed(range(group_bits)):
        half = total.shape[1] // 2
        first_half = total[:, :half]
        second_half = total[:, half:]
        is_low = low_bit(bit)
        outgoing = jnp.where(is_low, second_half, first_half)
        staying = jnp.where(is_low, first_half, second_half)
        total = staying + partner_2(outgoing, "seq", bit)
    grad_keys = total[0].astype(jnp.bfloat16)
    grad_values = total[1].astype(jnp.bfloat16)
    return (
        lax.all_to_all(attended, "head", split_axis=0, concat_axis=1, tiled=True),
        lax.all_to_all(grad_query, "head", split_axis=0, concat_axis=1, tiled=True),
        lax.all_to_all(grad_keys, "head", split_axis=0, concat_axis=1, tiled=True),
        lax.all_to_all(grad_values, "head", split_axis=0, concat_axis=1, tiled=True),
    )


NT = (((1,), (1,)), ((), ()))
F32 = jnp.float32
BF16 = jnp.bfloat16


def dot(a, b):
    return jnp.dot(a, b, preferred_element_type=F32)


def dot_nt(a, b):
    return lax.dot_general(a, b, NT, preferred_element_type=F32)


def head_columns(head):
    return slice(head * HD, (head + 1) * HD)


def flat(ref, head, which=None):
    columns = head_columns(head)
    part = ref[:, :, columns] if which is None else ref[:, which, :, columns]
    return part.reshape(part.shape[0] * part.shape[1], HD)


def put(ref, head, rows, which=None):
    if which is None:
        ref[:, :, head_columns(head)] = rows.reshape(ref.shape[0], ref.shape[1], HD)
    else:
        ref[:, which, :, head_columns(head)] = rows.reshape(ref.shape[0], ref.shape[2], HD)


def bias_rows(mask_ref, level, valid, blocks):
    lane_block = lax.broadcasted_iota(jnp.int32, (1, blocks * BLOCK), 1) // BLOCK
    rows = []
    for key_block in range(blocks):
        row = jnp.zeros((1, blocks * BLOCK), F32)
        for query_block in range(blocks):
            open_ = (mask_ref[level, query_block, key_block] > 0) & valid
            value = jnp.where(open_, 0.0, MASKED).astype(F32)
            row = jnp.where(lane_block == query_block, value, row)
        rows.append(row)
    return rows


def masked_scores(keys, queries, bias):
    scores = dot_nt(keys, queries) * SCALE_LOG2
    if bias is None:
        return scores
    blocks = len(bias)
    return jnp.concatenate(
        [scores[j * BLOCK : (j + 1) * BLOCK] + bias[j] for j in range(blocks)], axis=0
    )


def near_scores_kernel(frame_ref, mask_ref, vqg_ref, k0_ref, k1_ref, k3_ref, e_ref, ml_ref):
    heads, _, tokens = e_ref.shape
    blocks = tokens // BLOCK
    frame = frame_ref[0]
    inner = (frame == 1) | (frame == 2)
    bias1 = bias_rows(mask_ref, 0, frame >= 0, blocks)
    bias3 = bias_rows(mask_ref, 0, inner, blocks)
    for head in range(heads):
        queries = flat(vqg_ref, head, 1)
        slots = ((k0_ref, None), (k1_ref, bias1), (k3_ref, bias3))
        scores = [masked_scores(flat(ref, head), queries, bias) for ref, bias in slots]
        peak = scores[0].max(axis=0, keepdims=True)
        for score in scores[1:]:
            peak = jnp.maximum(peak, score.max(axis=0, keepdims=True))
        total = jnp.zeros((1, tokens), F32)
        for index, score in enumerate(scores):
            e = jnp.exp2(score - peak)
            total = total + e.sum(axis=0, keepdims=True)
            e_ref[head, index * tokens : (index + 1) * tokens] = e.astype(BF16)
        ml_ref[head, 0:1] = peak
        ml_ref[head, 1:2] = total


def far_scores_kernel(frame_ref, mask_ref, vqg_ref, ka_ref, kb_ref, ml_ref, e_ref, w_ref, dv_ref):
    heads, _, tokens = e_ref.shape
    blocks = tokens // BLOCK
    frame = frame_ref[0]
    inner = (frame == 1) | (frame == 2)
    bias = bias_rows(mask_ref, 1, frame >= 0, blocks)
    for head in range(heads):
        keys = jnp.where(inner, flat(kb_ref, head), flat(ka_ref, head))
        scores = masked_scores(keys, flat(vqg_ref, head, 1), bias)
        peak2 = scores.max(axis=0, keepdims=True)
        e = jnp.exp2(scores - peak2)
        total2 = e.sum(axis=0, keepdims=True)
        e = e.astype(BF16)
        peak1 = ml_ref[head, 0:1]
        peak = jnp.maximum(peak1, peak2)
        near = jnp.exp2(peak1 - peak)
        far = jnp.exp2(peak2 - peak)
        inv = 1.0 / (near * ml_ref[head, 1:2] + far * total2)
        far = far * inv
        scaled = (flat(vqg_ref, head, 2).T.astype(F32) * far).astype(BF16)
        put(dv_ref, head, dot_nt(e, scaled).astype(BF16))
        e_ref[head] = e
        w_ref[head, 0:1] = near * inv
        w_ref[head, 1:2] = far


def near_values_kernel(vqg_ref, e_ref, w_ref, v0_ref, v1_ref, v3_ref, dv0_ref, dv1_ref, dv3_ref, acc_ref):
    heads, _, tokens = e_ref.shape
    for head in range(heads):
        scaled = (flat(vqg_ref, head, 2).T.astype(F32) * w_ref[head, 0:1]).astype(BF16)
        acc = jnp.zeros((HD, tokens), F32)
        for index, (v_ref, dv_ref) in enumerate(
            ((v0_ref, dv0_ref), (v1_ref, dv1_ref), (v3_ref, dv3_ref))
        ):
            e = e_ref[head, index * tokens : (index + 1) * tokens]
            put(dv_ref, head, dot_nt(e, scaled).astype(BF16))
            acc = acc + dot(flat(v_ref, head).T, e)
        acc_ref[head] = acc


def far_values_kernel(
    frame_ref, vqg_ref, ka_ref, kb_ref, va_ref, vb_ref, e_ref, w_ref, acc_ref,
    dk_ref, att_ref, delta_ref, dq_ref,
):
    heads = e_ref.shape[0]
    frame = frame_ref[0]
    inner = (frame == 1) | (frame == 2)
    for head in range(heads):
        keys = jnp.where(inner, flat(kb_ref, head), flat(ka_ref, head))
        values = jnp.where(inner, flat(vb_ref, head), flat(va_ref, head))
        e = e_ref[head]
        near = w_ref[head, 0:1]
        far = w_ref[head, 1:2]
        out = (acc_ref[head] * near + dot(values.T, e) * far).astype(BF16)
        put(att_ref, head, out.T)
        grads = flat(vqg_ref, head, 2).T.astype(F32)
        delta = (grads * out.astype(F32)).sum(axis=0, keepdims=True)
        delta_ref[head, 0:1] = near
        delta_ref[head, 1:2] = near * delta
        scaled = (grads * far).astype(BF16)
        ds = (e.astype(F32) * (dot(values, scaled) - far * delta)).astype(BF16)
        put(dk_ref, head, (dot(ds, flat(vqg_ref, head, 1)) * SCALE).astype(BF16))
        dq_ref[head] = dot(keys.T, ds)


def near_keys_kernel(
    vqg_ref, k0_ref, k1_ref, k3_ref, v0_ref, v1_ref, v3_ref, e_ref, delta_ref, dq2_ref, att_ref,
    dk0_ref, dk1_ref, dk3_ref, out_ref,
):
    heads, _, tokens = e_ref.shape
    for head in range(heads):
        queries = flat(vqg_ref, head, 1)
        near = delta_ref[head, 0:1]
        delta = delta_ref[head, 1:2]
        scaled = (flat(vqg_ref, head, 2).T.astype(F32) * near).astype(BF16)
        dq = dq2_ref[head]
        for index, (k_ref, v_ref, dk_ref) in enumerate(
            ((k0_ref, v0_ref, dk0_ref), (k1_ref, v1_ref, dk1_ref), (k3_ref, v3_ref, dk3_ref))
        ):
            e = e_ref[head, index * tokens : (index + 1) * tokens]
            ds = (e.astype(F32) * (dot(flat(v_ref, head), scaled) - delta)).astype(BF16)
            put(dk_ref, head, (dot(ds, queries) * SCALE).astype(BF16))
            dq = dq + dot(flat(k_ref, head).T, ds)
        put(out_ref, head, (dq * SCALE).astype(BF16).T, 1)
    out_ref[:, 0] = att_ref[...]


def add_kernel(frame_ref, own_ref, other_ref, out_ref):
    out_ref[...] = (own_ref[...].astype(F32) + other_ref[...].astype(F32)).astype(BF16)


def add_inner_kernel(frame_ref, own_ref, other_ref, out_ref):
    inner = (frame_ref[0] == 1) | (frame_ref[0] == 2)

    @pl.when(inner)
    def _():
        out_ref[...] = (own_ref[...].astype(F32) + other_ref[...].astype(F32)).astype(BF16)

    @pl.when(jnp.logical_not(inner))
    def _():
        out_ref[...] = own_ref[...]


def last_sum(frame_ref, own_ref, edge_ref, middle_ref):
    inner = (frame_ref[0] == 1) | (frame_ref[0] == 2)
    total = own_ref[...].astype(F32) + edge_ref[...].astype(F32)
    return (total + jnp.where(inner, middle_ref[...].astype(F32), 0.0)).astype(BF16)


def collect_kernel(frame_ref, *refs):
    out_ref = refs[-1]
    for which in range(out_ref.shape[1]):
        out_ref[:, which] = last_sum(frame_ref, *refs[3 * which : 3 * which + 3])


def pack_kernel(*refs):
    out_ref = refs[-1]
    width = out_ref.shape[3]
    for peer in range(out_ref.shape[0]):
        for which, ref in enumerate(refs[:-1]):
            out_ref[peer, which] = ref[:, peer * width : (peer + 1) * width]


def first_kernel(in_ref, out_ref):
    out_ref[...] = in_ref[:, 0]


def unpack_kernel(in_ref, *out_refs):
    peers, _, _, width = in_ref.shape
    for peer in range(peers):
        for which, ref in enumerate(out_refs):
            ref[:, peer * width : (peer + 1) * width] = in_ref[peer, which]


def params():
    return pltpu.CompilerParams(vmem_limit_bytes=VMEM_BYTES)


def cost(flops, data):
    return pl.CostEstimate(flops=flops, bytes_accessed=data, transcendentals=0)


def per_device_line(query_rows, key_rows, value_rows, out_grad, block_mask):
    plane = ("rank", "head")
    peers = lax.axis_size("rank") * lax.axis_size("head")
    rows, columns = query_rows.shape
    width = columns // peers
    heads = width // HD
    tokens = peers * rows
    one = jax.ShapeDtypeStruct((peers, rows, width), BF16)
    row_type = jax.ShapeDtypeStruct((rows, columns), BF16)
    near_e = jax.ShapeDtypeStruct((heads, 3 * tokens, tokens), BF16)
    far_e = jax.ShapeDtypeStruct((heads, tokens, tokens), BF16)
    stat = jax.ShapeDtypeStruct((heads, 8, tokens), F32)
    accum = jax.ShapeDtypeStruct((heads, HD, tokens), F32)
    frame = lax.axis_index("frame").astype(jnp.int32).reshape(1)
    smem = pl.BlockSpec(memory_space=pltpu.SMEM)
    vmem = pl.BlockSpec(memory_space=pltpu.VMEM)
    pair_flops = heads * 2 * tokens * tokens * HD

    def call(kernel, outs, work, *operands):
        several = isinstance(outs, tuple)
        return pl.pallas_call(
            kernel,
            in_specs=[smem if x.dtype == jnp.int32 else vmem for x in operands],
            out_specs=(vmem,) * len(outs) if several else vmem,
            out_shape=outs,
            compiler_params=params(),
            cost_estimate=cost(work * pair_flops, 4 << 20),
        )(*operands)

    def swap(array):
        return lax.all_to_all(array, plane, 0, 0, tiled=True)

    def packed(count):
        return jax.ShapeDtypeStruct((peers, count, rows, width), BF16)

    def leave(packed):
        return call(unpack_kernel, (row_type,) * packed.shape[1], 0, swap(packed))

    pair = packed(2)
    devices = ("frame", "rank", "head")
    heads_axis = lax.axis_size("head")

    def pairs_of(partner):
        pairs = []
        for frame_ in range(4):
            for rank in range(GROUP):
                for part in range(heads_axis):
                    there = partner.get(frame_)
                    place = (frame_, rank ^ 1) if there is None else (there, rank)
                    pairs.append(
                        (
                            (frame_ * GROUP + rank) * heads_axis + part,
                            (place[0] * GROUP + place[1]) * heads_axis + part,
                        )
                    )
        return pairs

    edge = pairs_of({0: 1, 1: 0, 2: 3, 3: 2})
    middle = pairs_of({1: 2, 2: 1})

    def send(array, pairs):
        return lax.ppermute(array, devices, pairs)

    k0 = swap(call(pack_kernel, packed(1), 0, key_rows)).reshape(one.shape)
    k1, k3 = send(k0, edge), send(k0, middle)
    vqg = swap(call(pack_kernel, packed(3), 0, value_rows, query_rows, out_grad))
    v0 = call(first_kernel, one, 0, vqg)
    ka, kb = send(k3, edge), send(k1, middle)
    v1, v3 = send(v0, edge), send(v0, middle)
    va, vb = send(v3, edge), send(v1, middle)

    def sums(first, third, from_edge, from_middle):
        return (
            call(add_kernel, one, 0, frame, third, from_edge),
            call(add_inner_kernel, one, 0, frame, first, from_middle),
        )

    e_near, ml = call(
        near_scores_kernel, (near_e, stat), 6, frame, block_mask, vqg, k0, k1, k3
    )
    e_far, w, dv2 = call(
        far_scores_kernel, (far_e, stat, one), 4, frame, block_mask, vqg, ka, kb, ml
    )
    dv_edge, dv_middle = send(dv2, edge), send(dv2, middle)
    dv0, dv1, dv3, acc = call(
        near_values_kernel, (one, one, one, accum), 6, vqg, e_near, w, v0, v1, v3
    )
    dv_third, dv_first = sums(dv1, dv3, dv_edge, dv_middle)
    dv_over = send(dv_first, edge), send(dv_third, middle)
    acc, dv_first, dv_third = lax.optimization_barrier((acc, dv_first, dv_third))
    dk2, att, delta, dq2 = call(
        far_values_kernel, (one, one, stat, accum), 4, frame, vqg, ka, kb, va, vb, e_far, w, acc
    )
    dk_edge, dk_middle = send(dk2, edge), send(dk2, middle)
    delta, dv_over = lax.optimization_barrier((delta, dv_over))
    dk0, dk1, dk3, att_dq = call(
        near_keys_kernel, (one, one, one, pair), 9,
        vqg, k0, k1, k3, v0, v1, v3, e_near, delta, dq2, att,
    )
    attended, grad_query = leave(att_dq)
    dk_third, dk_first = sums(dk1, dk3, dk_edge, dk_middle)
    dk_over = send(dk_first, edge), send(dk_third, middle)
    grad_keys, grad_values = leave(
        call(collect_kernel, pair, 0, frame, dk0, *dk_over, dv0, *dv_over)
    )
    return attended, grad_query, grad_keys, grad_values


def solution(mesh):
    seq, head = mesh.shape["seq"], mesh.shape["head"]
    frames = seq // GROUP
    line = Mesh(mesh.devices.reshape(frames, GROUP, head), ("frame", "rank", "head"))

    def run(query_rows, key_rows, value_rows, out_grad, block_mask):
        heads = query_rows.shape[1] // HD
        tokens = query_rows.shape[0] // frames
        fits = (
            frames == 4
            and block_mask.shape[0] == 2
            and heads % (GROUP * head) == 0
            and tokens == block_mask.shape[1] * BLOCK
            and tokens // (GROUP * head) % 16 == 0
        )
        if fits:
            body, where, axes = per_device_line, line, ("frame", "rank", "head")
        else:
            body, where, axes = per_device_general, mesh, ("seq", "head")
        row_spec = P(axes, None)
        return jax.shard_map(
            body,
            mesh=where,
            in_specs=(row_spec,) * 4 + (P(),),
            out_specs=(row_spec,) * 4,
            check_vma=False,
        )(query_rows, key_rows, value_rows, out_grad, block_mask)

    return run
```

```python
import functools
import math

import jax
import jax.numpy as jnp
from jax import lax
from jax.experimental import pallas as pl
from jax.experimental.pallas import tpu as pltpu
from jax.sharding import Mesh
from jax.sharding import PartitionSpec as P

HD = 128
BLOCK = 128
GROUP = 4
SCALE = 1.0 / math.sqrt(HD)
SCALE_LOG2 = SCALE * math.log2(math.e)
MASKED = -1e30
VMEM_BYTES = 12 * 1024 * 1024

CONFIG = {'groups': [['k', 'q', 'g'], ['v']], 'vmode': 1, 'outs': [['att', 'dq'], ['dk', 'dv']], 'opts': ['b6', 'b7', 'sumv', 'big', 'b8', 'gate'], 'cost': {'fs': 2, 'nv': 2, 'fv': 2, 'nk': 4, 'pick1': 0.1, 'gate': 20, 'sumv': 20}}


def partner_2(shard, axis, distance):
    return lax.ppermute(shard, axis, [(i, i ^ 1 << distance) for i in range(lax.axis_size(axis))])


def passed_along(shard, axis, by):
    peers = lax.axis_size(axis)
    pairs = [(i, i + by) for i in range(peers) if 0 <= i + by < peers]
    return lax.ppermute(shard, axis, pairs)


def widen_mask(bits):
    blocks = bits.shape[0]
    grid = jnp.broadcast_to((bits > 0)[:, None, :, None], (blocks, BLOCK, blocks, BLOCK))
    return grid.reshape(blocks * BLOCK, blocks * BLOCK)


def place_pair(mine, other, is_low, dim):
    return lax.cond(
        is_low,
        lambda pair: jnp.concatenate([pair[0], pair[1]], dim),
        lambda pair: jnp.concatenate([pair[1], pair[0]], dim),
        (mine, other),
    )


def per_device_general(query_rows, key_rows, value_rows, out_grad, block_mask):
    queries, keys_local, values_local, grads_output = (
        lax.all_to_all(query_rows, "head", split_axis=1, concat_axis=0, tiled=True),
        lax.all_to_all(key_rows, "head", split_axis=1, concat_axis=0, tiled=True),
        lax.all_to_all(value_rows, "head", split_axis=1, concat_axis=0, tiled=True),
        lax.all_to_all(out_grad, "head", split_axis=1, concat_axis=0, tiled=True),
    )
    seq_index = lax.axis_index("seq")
    group_bits = GROUP.bit_length() - 1
    rank = seq_index % GROUP
    frame_index = seq_index // GROUP
    frame_count = lax.axis_size("seq") // GROUP
    level_count = block_mask.shape[0]
    block_rows = queries.shape[0]
    frame_tokens = block_rows * GROUP
    head_count = queries.shape[1] // HD
    score_scale = 1.0 / math.sqrt(HD)
    own_pair = jnp.stack([keys_local, values_local])

    def low_bit(bit):
        return seq_index >> bit & 1 == 0

    whole_pair = own_pair
    for bit in range(group_bits):
        other = partner_2(whole_pair, "seq", bit)
        whole_pair = place_pair(whole_pair, other, low_bit(bit), 1)
    partner_list = []
    for level_index in range(level_count):
        for orient in (1, -1):
            partner_list.append(
                passed_along(whole_pair, "seq", orient * GROUP * (1 << level_index))
            )
    every_pair = jnp.concatenate([whole_pair] + partner_list, axis=1)
    keys_all, values_all = (every_pair[0], every_pair[1])
    allowed_list = [jnp.ones((block_rows, frame_tokens), bool)]
    for level_index in range(level_count):
        for orient in (1, -1):
            partner = frame_index - orient * (1 << level_index)
            inside = (partner >= 0) & (partner < frame_count)
            allowed_list.append(
                lax.dynamic_slice_in_dim(
                    widen_mask(block_mask[level_index]), rank * block_rows, block_rows, 0
                )
                & inside
            )
    allowed = jnp.concatenate(allowed_list, axis=1)

    def head_scores(query_head, keys_head):
        scores = (
            jnp.einsum("qd,kd->qk", query_head, keys_head, preferred_element_type=jnp.float32)
            * score_scale
        )
        return jnp.where(allowed, scores, -jnp.inf)

    outputs = []
    logsums = []
    for head_index in range(head_count):
        columns = slice(head_index * HD, (head_index + 1) * HD)
        scores = head_scores(queries[:, columns], keys_all[:, columns])
        peak = jnp.max(scores, axis=1, keepdims=True)
        logsum = peak + jnp.log(jnp.sum(jnp.exp(scores - peak), axis=1, keepdims=True))
        weights = jnp.exp(scores - logsum).astype(jnp.bfloat16)
        outputs.append(
            jnp.dot(weights, values_all[:, columns], preferred_element_type=jnp.float32).astype(
                jnp.bfloat16
            )
        )
        logsums.append(logsum)
    attended = jnp.concatenate(outputs, axis=1)
    query_grads = []
    key_grads = []
    value_grads = []
    for head_index in range(head_count):
        columns = slice(head_index * HD, (head_index + 1) * HD)
        query_head = queries[:, columns]
        grad_head = grads_output[:, columns]
        scores = head_scores(query_head, keys_all[:, columns])
        probability = jnp.exp(scores - logsums[head_index])
        weights = probability.astype(jnp.bfloat16)
        grad_weights = jnp.einsum(
            "qd,kd->qk", grad_head, values_all[:, columns], preferred_element_type=jnp.float32
        )
        delta_row = jnp.sum(
            grad_head.astype(jnp.float32) * attended[:, columns].astype(jnp.float32),
            axis=1,
            keepdims=True,
        )
        grad_scores = (probability * (grad_weights - delta_row) * score_scale).astype(jnp.bfloat16)
        query_grads.append(
            jnp.dot(grad_scores, keys_all[:, columns], preferred_element_type=jnp.float32).astype(
                jnp.bfloat16
            )
        )
        key_grads.append(
            jnp.einsum(
                "qk,qd->kd", grad_scores, query_head, preferred_element_type=jnp.float32
            ).astype(jnp.bfloat16)
        )
        value_grads.append(
            jnp.einsum("qk,qd->kd", weights, grad_head, preferred_element_type=jnp.float32).astype(
                jnp.bfloat16
            )
        )
    grad_query = jnp.concatenate(query_grads, axis=1)
    grad_pair = jnp.stack(
        [jnp.concatenate(key_grads, axis=1), jnp.concatenate(value_grads, axis=1)]
    )
    total = grad_pair[:, :frame_tokens].astype(jnp.float32)
    piece_index = 1
    for level_index in range(level_count):
        for orient in (1, -1):
            piece = grad_pair[:, piece_index * frame_tokens : (piece_index + 1) * frame_tokens]
            returned = passed_along(piece, "seq", -orient * GROUP * (1 << level_index))
            total = total + returned.astype(jnp.float32)
            piece_index += 1
    for bit in reversed(range(group_bits)):
        half = total.shape[1] // 2
        first_half = total[:, :half]
        second_half = total[:, half:]
        is_low = low_bit(bit)
        outgoing = jnp.where(is_low, second_half, first_half)
        staying = jnp.where(is_low, first_half, second_half)
        total = staying + partner_2(outgoing, "seq", bit)
    grad_keys = total[0].astype(jnp.bfloat16)
    grad_values = total[1].astype(jnp.bfloat16)
    return (
        lax.all_to_all(attended, "head", split_axis=0, concat_axis=1, tiled=True),
        lax.all_to_all(grad_query, "head", split_axis=0, concat_axis=1, tiled=True),
        lax.all_to_all(grad_keys, "head", split_axis=0, concat_axis=1, tiled=True),
        lax.all_to_all(grad_values, "head", split_axis=0, concat_axis=1, tiled=True),
    )


NT = (((1,), (1,)), ((), ()))
F32 = jnp.float32
BF16 = jnp.bfloat16


def dot(a, b):
    return jnp.dot(a, b, preferred_element_type=F32)


def dot_nt(a, b):
    return lax.dot_general(a, b, NT, preferred_element_type=F32)


def head_columns(head):
    return slice(head * HD, (head + 1) * HD)


def flat(ref, head, which=None):
    columns = head_columns(head)
    part = ref[:, :, columns] if which is None else ref[:, which, :, columns]
    return part.reshape(part.shape[0] * part.shape[1], HD)


def put(ref, head, rows, which=None):
    if which is None:
        ref[:, :, head_columns(head)] = rows.reshape(ref.shape[0], ref.shape[1], HD)
    else:
        ref[:, which, :, head_columns(head)] = rows.reshape(ref.shape[0], ref.shape[2], HD)


def bias_rows(mask_ref, level, valid, blocks):
    lane_block = lax.broadcasted_iota(jnp.int32, (1, blocks * BLOCK), 1) // BLOCK
    rows = []
    for key_block in range(blocks):
        row = jnp.zeros((1, blocks * BLOCK), F32)
        for query_block in range(blocks):
            open_ = (mask_ref[level, query_block, key_block] > 0) & valid
            value = jnp.where(open_, 0.0, MASKED).astype(F32)
            row = jnp.where(lane_block == query_block, value, row)
        rows.append(row)
    return rows


def masked_scores(keys, queries, bias):
    scores = dot_nt(keys, queries) * SCALE_LOG2
    if bias is None:
        return scores
    blocks = len(bias)
    return jnp.concatenate(
        [scores[j * BLOCK : (j + 1) * BLOCK] + bias[j] for j in range(blocks)], axis=0
    )


def near_scores_kernel(rows, frame_ref, mask_ref, e_ref, ml_ref):
    heads, _, tokens = e_ref.shape
    blocks = tokens // BLOCK
    frame = frame_ref[0]
    inner = (frame == 1) | (frame == 2)
    bias1 = bias_rows(mask_ref, 0, frame >= 0, blocks)
    bias3 = bias_rows(mask_ref, 0, inner, blocks)
    for head in range(heads):
        queries = rows("q", head)
        slots = (("k0", None), ("k1", bias1), ("k3", bias3))
        scores = [masked_scores(rows(name, head), queries, bias) for name, bias in slots]
        peak = scores[0].max(axis=0, keepdims=True)
        for score in scores[1:]:
            peak = jnp.maximum(peak, score.max(axis=0, keepdims=True))
        total = jnp.zeros((1, tokens), F32)
        for index, score in enumerate(scores):
            e = jnp.exp2(score - peak)
            total = total + e.sum(axis=0, keepdims=True)
            e_ref[head, index * tokens : (index + 1) * tokens] = e.astype(BF16)
        ml_ref[head, 0:1] = peak
        ml_ref[head, 1:2] = total


def far_scores_kernel(rows, frame_ref, mask_ref, ml_ref, e_ref, w_ref, dv_ref):
    heads, _, tokens = e_ref.shape
    blocks = tokens // BLOCK
    frame = frame_ref[0]
    inner = (frame == 1) | (frame == 2)
    bias = bias_rows(mask_ref, 1, frame >= 0, blocks)
    for head in range(heads):
        keys = jnp.where(inner, rows("kb", head), rows("ka", head))
        scores = masked_scores(keys, rows("q", head), bias)
        peak2 = scores.max(axis=0, keepdims=True)
        e = jnp.exp2(scores - peak2)
        total2 = e.sum(axis=0, keepdims=True)
        e = e.astype(BF16)
        peak1 = ml_ref[head, 0:1]
        peak = jnp.maximum(peak1, peak2)
        near = jnp.exp2(peak1 - peak)
        far = jnp.exp2(peak2 - peak)
        inv = 1.0 / (near * ml_ref[head, 1:2] + far * total2)
        far = far * inv
        scaled = (rows("g", head).T.astype(F32) * far).astype(BF16)
        put(dv_ref, head, dot_nt(e, scaled).astype(BF16))
        e_ref[head] = e
        w_ref[head, 0:1] = near * inv
        w_ref[head, 1:2] = far


def near_values_kernel(rows, e_ref, w_ref, dv0_ref, dv1_ref, dv3_ref, acc_ref):
    heads, _, tokens = e_ref.shape
    for head in range(heads):
        scaled = (rows("g", head).T.astype(F32) * w_ref[head, 0:1]).astype(BF16)
        acc = jnp.zeros((HD, tokens), F32)
        slots = (("v0", dv0_ref), ("v1", dv1_ref), ("v3", dv3_ref))
        for index, (name, dv_ref) in enumerate(slots):
            e = e_ref[head, index * tokens : (index + 1) * tokens]
            put(dv_ref, head, dot_nt(e, scaled).astype(BF16))
            acc = acc + dot(rows(name, head).T, e)
        acc_ref[head] = acc


def far_values_kernel(rows, frame_ref, e_ref, w_ref, acc_ref, dk_ref, att_ref, delta_ref, dq_ref):
    heads = e_ref.shape[0]
    frame = frame_ref[0]
    inner = (frame == 1) | (frame == 2)
    for head in range(heads):
        keys = jnp.where(inner, rows("kb", head), rows("ka", head))
        values = jnp.where(inner, rows("vb", head), rows("va", head))
        e = e_ref[head]
        near = w_ref[head, 0:1]
        far = w_ref[head, 1:2]
        out = (acc_ref[head] * near + dot(values.T, e) * far).astype(BF16)
        put(att_ref, head, out.T)
        grads = rows("g", head).T.astype(F32)
        delta = (grads * out.astype(F32)).sum(axis=0, keepdims=True)
        delta_ref[head, 0:1] = near
        delta_ref[head, 1:2] = near * delta
        scaled = (grads * far).astype(BF16)
        ds = (e.astype(F32) * (dot(values, scaled) - far * delta)).astype(BF16)
        put(dk_ref, head, (dot(ds, rows("q", head)) * SCALE).astype(BF16))
        dq_ref[head] = dot(keys.T, ds)


def near_keys_kernel(rows, e_ref, delta_ref, dq2_ref, dk0_ref, dk1_ref, dk3_ref, dq_ref):
    heads, _, tokens = e_ref.shape
    for head in range(heads):
        queries = rows("q", head)
        near = delta_ref[head, 0:1]
        delta = delta_ref[head, 1:2]
        scaled = (rows("g", head).T.astype(F32) * near).astype(BF16)
        dq = dq2_ref[head]
        slots = (("k0", "v0", dk0_ref), ("k1", "v1", dk1_ref), ("k3", "v3", dk3_ref))
        for index, (k_name, v_name, dk_ref) in enumerate(slots):
            e = e_ref[head, index * tokens : (index + 1) * tokens]
            ds = (e.astype(F32) * (dot(rows(v_name, head), scaled) - delta)).astype(BF16)
            put(dk_ref, head, (dot(ds, queries) * SCALE).astype(BF16))
            dq = dq + dot(rows(k_name, head).T, ds)
        put(dq_ref, head, (dq * SCALE).astype(BF16).T)


def add_kernel(own_ref, other_ref, out_ref):
    out_ref[...] = (own_ref[...].astype(F32) + other_ref[...].astype(F32)).astype(BF16)


def add_inner_kernel(frame_ref, own_ref, other_ref, out_ref):
    inner = (frame_ref[0] == 1) | (frame_ref[0] == 2)

    @pl.when(inner)
    def _():
        out_ref[...] = (own_ref[...].astype(F32) + other_ref[...].astype(F32)).astype(BF16)

    @pl.when(jnp.logical_not(inner))
    def _():
        out_ref[...] = own_ref[...]


def sum_kernel(frame_ref, own_ref, edge_ref, middle_ref, out_ref):
    inner = (frame_ref[0] == 1) | (frame_ref[0] == 2)
    total = own_ref[...].astype(F32) + edge_ref[...].astype(F32)
    out_ref[...] = (total + jnp.where(inner, middle_ref[...].astype(F32), 0.0)).astype(BF16)


def collect_kernel(counts, frame_ref, *refs):
    out_ref = refs[-1]
    inner = (frame_ref[0] == 1) | (frame_ref[0] == 2)
    place = 0
    for which, count in enumerate(counts):
        parts = refs[place : place + count]
        place += count
        if count == 1:
            out_ref[:, which] = parts[0][...]
        else:
            own, edge, middle = (part[...].astype(F32) for part in parts)
            out_ref[:, which] = (own + edge + jnp.where(inner, middle, 0.0)).astype(BF16)


def pack_kernel(*refs):
    out_ref, held, sems = refs[-3:]
    copies = [
        pltpu.make_async_copy(ref, held.at[which], sems.at[which])
        for which, ref in enumerate(refs[:-3])
    ]
    for copy in copies:
        copy.start()
    peers, _, _, width = out_ref.shape
    for which, copy in enumerate(copies):
        copy.wait()
        for peer in range(peers):
            out_ref[peer, which] = held[which, :, peer * width : (peer + 1) * width]


def pack_values_kernel(frame_ref, *refs):
    out_ref, held, sems = refs[-3:]
    count = out_ref.shape[1]
    inner = (frame_ref[0] == 1) | (frame_ref[0] == 2)
    copies = [
        pltpu.make_async_copy(ref, held.at[which], sems.at[which])
        for which, ref in enumerate(refs[:-3])
    ]
    for copy in copies:
        copy.start()
    for copy in copies:
        copy.wait()
    peers, _, _, width = out_ref.shape
    for peer in range(peers):
        columns = slice(peer * width, (peer + 1) * width)
        for which in range(count - 1):
            out_ref[peer, which] = held[which, :, columns]
        out_ref[peer, count - 1] = jnp.where(
            inner, held[count, :, columns], held[count - 1, :, columns]
        )


def pass_kernel(*refs):
    pass


def pick_kernel(places, in_ref, *out_refs):
    for place, ref in zip(places, out_refs):
        ref[...] = in_ref[:, place]


def unpack_kernel(in_ref, *out_refs):
    peers, _, _, width = in_ref.shape
    for peer in range(peers):
        for which, ref in enumerate(out_refs):
            ref[:, peer * width : (peer + 1) * width] = in_ref[peer, which]


def per_device_line(query_rows, key_rows, value_rows, out_grad, block_mask):
    plane = ("rank", "head")
    peers = lax.axis_size("rank") * lax.axis_size("head")
    rows, columns = query_rows.shape
    width = columns // peers
    heads = width // HD
    tokens = peers * rows
    one = jax.ShapeDtypeStruct((peers, rows, width), BF16)
    row_type = jax.ShapeDtypeStruct((rows, columns), BF16)
    near_e = jax.ShapeDtypeStruct((heads, 3 * tokens, tokens), BF16)
    far_e = jax.ShapeDtypeStruct((heads, tokens, tokens), BF16)
    stat = jax.ShapeDtypeStruct((heads, 8, tokens), F32)
    accum = jax.ShapeDtypeStruct((heads, HD, tokens), F32)
    frame = lax.axis_index("frame").astype(jnp.int32).reshape(1)
    smem = pl.BlockSpec(memory_space=pltpu.SMEM)
    vmem = pl.BlockSpec(memory_space=pltpu.VMEM)
    found = {}

    def call(kernel, outs, work, *operands, names=()):
        several = isinstance(outs, tuple)
        arrays = []
        places = {}
        for name in names:
            array, which = found[name]
            spot = [i for i, x in enumerate(arrays) if x is array]
            if not spot:
                spot = [len(arrays)]
                arrays.append(array)
            places[name] = (spot[0], which)

        def body(*refs):
            lookup = refs[: len(arrays)]
            if not places:
                return kernel(*refs)

            def rows_of(name, head):
                index, which = places[name]
                return flat(lookup[index], head, which)

            return kernel(rows_of, *refs[len(arrays) :])

        operands = tuple(arrays) + operands
        return pl.pallas_call(
            body,
            in_specs=[smem if x.dtype == jnp.int32 else vmem for x in operands],
            out_specs=(vmem,) * len(outs) if several else vmem,
            out_shape=outs,
            compiler_params=pltpu.CompilerParams(vmem_limit_bytes=VMEM_BYTES),
            cost_estimate=pl.CostEstimate(
                flops=int(work * 1_150_000_000), bytes_accessed=1 << 16, transcendentals=0
            ),
        )(*operands)

    def later(work, *arrays):
        return pl.pallas_call(
            pass_kernel,
            in_specs=[pl.BlockSpec(memory_space=pl.ANY)] * len(arrays),
            out_specs=(pl.BlockSpec(memory_space=pl.ANY),) * len(arrays),
            out_shape=tuple(jax.ShapeDtypeStruct(x.shape, x.dtype) for x in arrays),
            input_output_aliases={i: i for i in range(len(arrays))},
            cost_estimate=pl.CostEstimate(
                flops=int(work * 1_150_000_000), bytes_accessed=1 << 16, transcendentals=0
            ),
        )(*arrays)

    def pack(work, *arrays, kernel=pack_kernel, first=(), limit=VMEM_BYTES):
        count = len(arrays) - len(first)
        return pl.pallas_call(
            kernel,
            in_specs=[smem] * len(first) + [pl.BlockSpec(memory_space=pltpu.HBM)] * len(arrays),
            out_specs=vmem,
            out_shape=packed(count),
            scratch_shapes=[
                pltpu.VMEM((len(arrays), rows, columns), BF16),
                pltpu.SemaphoreType.DMA((len(arrays),)),
            ],
            compiler_params=pltpu.CompilerParams(vmem_limit_bytes=limit),
            cost_estimate=pl.CostEstimate(
                flops=int(work * 1_150_000_000), bytes_accessed=1 << 16, transcendentals=0
            ),
        )(*first, *arrays)

    def packed(count):
        return jax.ShapeDtypeStruct((peers, count, rows, width), BF16)

    def swap(array):
        return lax.all_to_all(array, plane, 0, 0, tiled=True)

    devices = ("frame", "rank", "head")
    heads_axis = lax.axis_size("head")

    def pairs_of(partner):
        pairs = []
        for frame_ in range(4):
            for rank in range(GROUP):
                for part in range(heads_axis):
                    there = partner.get(frame_)
                    place = (frame_, rank ^ 1) if there is None else (there, rank)
                    pairs.append(
                        (
                            (frame_ * GROUP + rank) * heads_axis + part,
                            (place[0] * GROUP + place[1]) * heads_axis + part,
                        )
                    )
        return pairs

    edge = pairs_of({0: 1, 1: 0, 2: 3, 3: 2})
    middle = pairs_of({1: 2, 2: 1})

    def send(array, pairs):
        return lax.ppermute(array, devices, pairs)

    def barrier(*values):
        return lax.optimization_barrier(values)

    cost = CONFIG["cost"]
    opts = CONFIG["opts"]
    raw = {"k": key_rows, "q": query_rows, "v": value_rows, "g": out_grad}
    vmode = CONFIG["vmode"]
    if vmode > 0:
        raw["v1"], raw["v3"] = send(value_rows, edge), send(value_rows, middle)
    if vmode > 1:
        raw["va"], raw["vb"] = send(raw["v3"], edge), send(raw["v1"], middle)

    scored = []

    def near_scores():
        return call(
            near_scores_kernel, (near_e, stat), cost.get("ns", 3.5), frame, block_mask,
            names=("q", "k0", "k1", "k3"),
        )

    early = {}
    ready = {}
    for index, group in enumerate(CONFIG["groups"]):
        members = list(group)
        if "v" in members and vmode > 0:
            at = members.index("v")
            members[at:at + 1] = ["v", "v1", "v3"]
            if vmode > 1:
                members.append("v2")
        work = cost.get("pack%d" % index, 0.5)
        if "v2" in members:
            members.remove("v2")
            members.append("v2")
            buffer = pack(
                work, *[raw[m] for m in members[:-1]], raw["va"], raw["vb"],
                kernel=pack_values_kernel, first=(frame,),
            )
        else:
            buffer = early.pop(index, None)
            if buffer is None:
                buffer = pack(
                    work, *[raw[m] for m in members],
                    limit=(60 << 20) if index == 0 and "big" in opts else VMEM_BYTES,
                )
        landed = swap(buffer)
        if "b8" in opts and index == 0 and vmode == 1:
            later_index = [i for i, g in enumerate(CONFIG["groups"]) if "v" in g][0]
            early[later_index] = pack(
                cost.get("pack%d" % later_index, 0.5),
                *[raw[m] for m in sum([["v", "v1", "v3"] if x == "v" else [x] for x in CONFIG["groups"][later_index]], [])],
            )
            landed, early[later_index] = barrier(landed, early[later_index])
        if "b7" in opts and "v" in members and "k0" in found and "q" in found:
            e_near, ml = near_scores()
            landed, ml = barrier(landed, ml)
            scored.append((e_near, ml))
        for place, m in enumerate(members):
            ready[m] = (landed, place)
        want = [m for m in members if m == "k" or (m == "v" and vmode == 0) or (m in ("v1", "v3") and vmode == 1)]
        if want:
            if len(members) == 1:
                alone = (landed.reshape(one.shape),)
            else:
                alone = call(
                    functools.partial(pick_kernel, tuple(members.index(m) for m in want)),
                    (one,) * len(want), cost.get("pick%d" % index, 0.2), landed,
                )
            for m, array in zip(want, alone):
                ready[m] = (array, None)
        if "k" in members:
            k0 = ready["k"][0]
            k1, k3 = send(k0, edge), send(k0, middle)
            if "gate" in opts:
                k1, k3 = later(cost.get("gate", 20), k1, k3)
            found.update(k0=(k0, None), k1=(k1, None), k3=(k3, None))
            found.update(ka=(send(k3, edge), None), kb=(send(k1, middle), None))
        if "v" in members:
            if vmode == 0:
                v0 = ready["v"][0]
                v1, v3 = send(v0, edge), send(v0, middle)
                found.update(v0=(v0, None), v1=(v1, None), v3=(v3, None))
                found.update(va=(send(v3, edge), None), vb=(send(v1, middle), None))
            else:
                found.update(v0=(landed, members.index("v")), v1=ready["v1"], v3=ready["v3"])
                if vmode == 1:
                    v1, v3 = ready["v1"][0], ready["v3"][0]
                    found.update(va=(send(v3, edge), None), vb=(send(v1, middle), None))
                else:
                    found.update(va=ready["v2"], vb=ready["v2"])
        for m in ("q", "g"):
            if m in members:
                found[m] = ready[m]

    if not scored:
        scored.append(near_scores())

    def sums(name, first, third, from_edge, from_middle):
        work = cost.get("add" + name, 0.2)
        return (
            call(add_inner_kernel, one, work, frame, first, from_middle),
            call(add_kernel, one, work, third, from_edge),
        )

    e_near, ml = scored[0]
    if "gns" in opts:
        (ml,) = later(cost.get("gns", 10), ml)
    e_far, w, dv2 = call(
        far_scores_kernel, (far_e, stat, one), cost.get("fs", 2.5), frame, block_mask, ml,
        names=("q", "g", "ka", "kb"),
    )
    dv_edge, dv_middle = send(dv2, edge), send(dv2, middle)
    dv0, dv1, dv3, acc = call(
        near_values_kernel, (one, one, one, accum), cost.get("nv", 2), e_near, w,
        names=("g", "v0", "v1", "v3"),
    )
    dk2, att, delta, dq2 = call(
        far_values_kernel, (one, one, stat, accum), cost.get("fv", 2.5), frame, e_far, w, acc,
        names=("q", "g", "ka", "kb", "va", "vb"),
    )
    dk_edge, dk_middle = send(dk2, edge), send(dk2, middle)
    dk0, dk1, dk3, dq = call(
        near_keys_kernel, (one, one, one, one), cost.get("nk", 3.5), e_near, delta, dq2,
        names=("q", "g", "k0", "k1", "k3", "v0", "v1", "v3"),
    )
    if "b6" in opts:
        dq, dv1, dv3 = barrier(dq, dv1, dv3)
    dv_first, dv_third = sums("v", dv1, dv3, dv_edge, dv_middle)
    dv_over = send(dv_first, edge), send(dv_third, middle)
    if "gdv" in opts:
        dv_over = later(cost.get("gdv", 20), *dv_over)
    dk_first, dk_third = sums("k", dk1, dk3, dk_edge, dk_middle)
    dk_over = send(dk_first, edge), send(dk_third, middle)

    if "b4" in opts:
        att, dv_first, dv_third = barrier(att, dv_first, dv_third)
    if "b5" in opts:
        dq, dv_first, dv_third = barrier(dq, dv_first, dv_third)
    parts = {"att": (att,), "dq": (dq,), "dk": (dk0, *dk_over), "dv": (dv0, *dv_over)}
    if "sumv" in opts:
        parts["dv"] = (call(sum_kernel, one, cost.get("sumv", 20), frame, *parts["dv"]),)
    results = {}
    previous = None
    for index, group in enumerate(CONFIG["outs"]):
        operands = [parts[m] for m in group]
        if previous is not None and "b3" in opts:
            first, previous = barrier(operands[0][0], previous)
            operands[0] = (first,) + tuple(operands[0][1:])
            previous_outs = call(
                unpack_kernel, (row_type,) * len(previous_group), 0.5, previous
            )
            results.update(zip(previous_group, previous_outs))
        counts = tuple(len(p) for p in operands)
        buffer = call(
            functools.partial(collect_kernel, counts), packed(len(group)),
            cost.get("collect%d" % index, 0.5), frame, *[x for p in operands for x in p],
        )
        previous, previous_group = swap(buffer), group
        if "b3" not in opts or index == len(CONFIG["outs"]) - 1:
            outs = call(unpack_kernel, (row_type,) * len(group), 0.5, previous)
            results.update(zip(group, outs))
    return results["att"], results["dq"], results["dk"], results["dv"]


def solution(mesh):
    seq, head = mesh.shape["seq"], mesh.shape["head"]
    frames = seq // GROUP
    line = Mesh(mesh.devices.reshape(frames, GROUP, head), ("frame", "rank", "head"))

    def run(query_rows, key_rows, value_rows, out_grad, block_mask):
        heads = query_rows.shape[1] // HD
        tokens = query_rows.shape[0] // frames
        fits = (
            frames == 4
            and block_mask.shape[0] == 2
            and heads % (GROUP * head) == 0
            and tokens == block_mask.shape[1] * BLOCK
            and tokens // (GROUP * head) % 16 == 0
        )
        if fits:
            body, where, axes = per_device_line, line, ("frame", "rank", "head")
        else:
            body, where, axes = per_device_general, mesh, ("seq", "head")
        row_spec = P(axes, None)
        return jax.shard_map(
            body,
            mesh=where,
            in_specs=(row_spec,) * 4 + (P(),),
            out_specs=(row_spec,) * 4,
            check_vma=False,
        )(query_rows, key_rows, value_rows, out_grad, block_mask)

    return run
```

```python
import functools
import math

import jax
import jax.numpy as jnp
from jax import lax
from jax.experimental import pallas as pl
from jax.experimental.pallas import tpu as pltpu
from jax.sharding import Mesh
from jax.sharding import PartitionSpec as P

HD = 128
BLOCK = 128
GROUP = 4
SCALE = 1.0 / math.sqrt(HD)
SCALE_LOG2 = SCALE * math.log2(math.e)
MASKED = -1e30
VMEM_BYTES = 12 * 1024 * 1024
FIRST_PACK_BYTES = 60 * 1024 * 1024

FLOPS_PER_US = 1_150_000_000
SECOND_HOP_WORK = 20
PICK_WORK = 20
SUM_WORK = 20


def partner_2(shard, axis, distance):
    return lax.ppermute(shard, axis, [(i, i ^ 1 << distance) for i in range(lax.axis_size(axis))])


def passed_along(shard, axis, by):
    peers = lax.axis_size(axis)
    pairs = [(i, i + by) for i in range(peers) if 0 <= i + by < peers]
    return lax.ppermute(shard, axis, pairs)


def widen_mask(bits):
    blocks = bits.shape[0]
    grid = jnp.broadcast_to((bits > 0)[:, None, :, None], (blocks, BLOCK, blocks, BLOCK))
    return grid.reshape(blocks * BLOCK, blocks * BLOCK)


def place_pair(mine, other, is_low, dim):
    return lax.cond(
        is_low,
        lambda pair: jnp.concatenate([pair[0], pair[1]], dim),
        lambda pair: jnp.concatenate([pair[1], pair[0]], dim),
        (mine, other),
    )


def per_device_general(query_rows, key_rows, value_rows, out_grad, block_mask):
    queries, keys_local, values_local, grads_output = (
        lax.all_to_all(query_rows, "head", split_axis=1, concat_axis=0, tiled=True),
        lax.all_to_all(key_rows, "head", split_axis=1, concat_axis=0, tiled=True),
        lax.all_to_all(value_rows, "head", split_axis=1, concat_axis=0, tiled=True),
        lax.all_to_all(out_grad, "head", split_axis=1, concat_axis=0, tiled=True),
    )
    seq_index = lax.axis_index("seq")
    group_bits = GROUP.bit_length() - 1
    rank = seq_index % GROUP
    frame_index = seq_index // GROUP
    frame_count = lax.axis_size("seq") // GROUP
    level_count = block_mask.shape[0]
    block_rows = queries.shape[0]
    frame_tokens = block_rows * GROUP
    head_count = queries.shape[1] // HD
    score_scale = 1.0 / math.sqrt(HD)
    own_pair = jnp.stack([keys_local, values_local])

    def low_bit(bit):
        return seq_index >> bit & 1 == 0

    whole_pair = own_pair
    for bit in range(group_bits):
        other = partner_2(whole_pair, "seq", bit)
        whole_pair = place_pair(whole_pair, other, low_bit(bit), 1)
    partner_list = []
    for level_index in range(level_count):
        for orient in (1, -1):
            partner_list.append(
                passed_along(whole_pair, "seq", orient * GROUP * (1 << level_index))
            )
    every_pair = jnp.concatenate([whole_pair] + partner_list, axis=1)
    keys_all, values_all = (every_pair[0], every_pair[1])
    allowed_list = [jnp.ones((block_rows, frame_tokens), bool)]
    for level_index in range(level_count):
        for orient in (1, -1):
            partner = frame_index - orient * (1 << level_index)
            inside = (partner >= 0) & (partner < frame_count)
            allowed_list.append(
                lax.dynamic_slice_in_dim(
                    widen_mask(block_mask[level_index]), rank * block_rows, block_rows, 0
                )
                & inside
            )
    allowed = jnp.concatenate(allowed_list, axis=1)

    def head_scores(query_head, keys_head):
        scores = (
            jnp.einsum("qd,kd->qk", query_head, keys_head, preferred_element_type=jnp.float32)
            * score_scale
        )
        return jnp.where(allowed, scores, -jnp.inf)

    outputs = []
    logsums = []
    for head_index in range(head_count):
        columns = slice(head_index * HD, (head_index + 1) * HD)
        scores = head_scores(queries[:, columns], keys_all[:, columns])
        peak = jnp.max(scores, axis=1, keepdims=True)
        logsum = peak + jnp.log(jnp.sum(jnp.exp(scores - peak), axis=1, keepdims=True))
        weights = jnp.exp(scores - logsum).astype(jnp.bfloat16)
        outputs.append(
            jnp.dot(weights, values_all[:, columns], preferred_element_type=jnp.float32).astype(
                jnp.bfloat16
            )
        )
        logsums.append(logsum)
    attended = jnp.concatenate(outputs, axis=1)
    query_grads = []
    key_grads = []
    value_grads = []
    for head_index in range(head_count):
        columns = slice(head_index * HD, (head_index + 1) * HD)
        query_head = queries[:, columns]
        grad_head = grads_output[:, columns]
        scores = head_scores(query_head, keys_all[:, columns])
        probability = jnp.exp(scores - logsums[head_index])
        weights = probability.astype(jnp.bfloat16)
        grad_weights = jnp.einsum(
            "qd,kd->qk", grad_head, values_all[:, columns], preferred_element_type=jnp.float32
        )
        delta_row = jnp.sum(
            grad_head.astype(jnp.float32) * attended[:, columns].astype(jnp.float32),
            axis=1,
            keepdims=True,
        )
        grad_scores = (probability * (grad_weights - delta_row) * score_scale).astype(jnp.bfloat16)
        query_grads.append(
            jnp.dot(grad_scores, keys_all[:, columns], preferred_element_type=jnp.float32).astype(
                jnp.bfloat16
            )
        )
        key_grads.append(
            jnp.einsum(
                "qk,qd->kd", grad_scores, query_head, preferred_element_type=jnp.float32
            ).astype(jnp.bfloat16)
        )
        value_grads.append(
            jnp.einsum("qk,qd->kd", weights, grad_head, preferred_element_type=jnp.float32).astype(
                jnp.bfloat16
            )
        )
    grad_query = jnp.concatenate(query_grads, axis=1)
    grad_pair = jnp.stack(
        [jnp.concatenate(key_grads, axis=1), jnp.concatenate(value_grads, axis=1)]
    )
    total = grad_pair[:, :frame_tokens].astype(jnp.float32)
    piece_index = 1
    for level_index in range(level_count):
        for orient in (1, -1):
            piece = grad_pair[:, piece_index * frame_tokens : (piece_index + 1) * frame_tokens]
            returned = passed_along(piece, "seq", -orient * GROUP * (1 << level_index))
            total = total + returned.astype(jnp.float32)
            piece_index += 1
    for bit in reversed(range(group_bits)):
        half = total.shape[1] // 2
        first_half = total[:, :half]
        second_half = total[:, half:]
        is_low = low_bit(bit)
        outgoing = jnp.where(is_low, second_half, first_half)
        staying = jnp.where(is_low, first_half, second_half)
        total = staying + partner_2(outgoing, "seq", bit)
    grad_keys = total[0].astype(jnp.bfloat16)
    grad_values = total[1].astype(jnp.bfloat16)
    return (
        lax.all_to_all(attended, "head", split_axis=0, concat_axis=1, tiled=True),
        lax.all_to_all(grad_query, "head", split_axis=0, concat_axis=1, tiled=True),
        lax.all_to_all(grad_keys, "head", split_axis=0, concat_axis=1, tiled=True),
        lax.all_to_all(grad_values, "head", split_axis=0, concat_axis=1, tiled=True),
    )


NT = (((1,), (1,)), ((), ()))
F32 = jnp.float32
BF16 = jnp.bfloat16


def dot(a, b):
    return jnp.dot(a, b, preferred_element_type=F32)


def dot_nt(a, b):
    return lax.dot_general(a, b, NT, preferred_element_type=F32)


def head_columns(head):
    return slice(head * HD, (head + 1) * HD)


def flat(ref, head, which=None):
    columns = head_columns(head)
    part = ref[:, :, columns] if which is None else ref[:, which, :, columns]
    return part.reshape(part.shape[0] * part.shape[1], HD)


def put(ref, head, rows, which=None):
    if which is None:
        ref[:, :, head_columns(head)] = rows.reshape(ref.shape[0], ref.shape[1], HD)
    else:
        ref[:, which, :, head_columns(head)] = rows.reshape(ref.shape[0], ref.shape[2], HD)


def bias_rows(mask_ref, level, valid, blocks):
    lane_block = lax.broadcasted_iota(jnp.int32, (1, blocks * BLOCK), 1) // BLOCK
    rows = []
    for key_block in range(blocks):
        row = jnp.zeros((1, blocks * BLOCK), F32)
        for query_block in range(blocks):
            open_ = (mask_ref[level, query_block, key_block] > 0) & valid
            value = jnp.where(open_, 0.0, MASKED).astype(F32)
            row = jnp.where(lane_block == query_block, value, row)
        rows.append(row)
    return rows


def masked_scores(keys, queries, bias):
    scores = dot_nt(keys, queries) * SCALE_LOG2
    if bias is None:
        return scores
    blocks = len(bias)
    return jnp.concatenate(
        [scores[j * BLOCK : (j + 1) * BLOCK] + bias[j] for j in range(blocks)], axis=0
    )


def near_scores_kernel(rows, frame_ref, mask_ref, e_ref, ml_ref):
    heads, _, tokens = e_ref.shape
    blocks = tokens // BLOCK
    frame = frame_ref[0]
    inner = (frame == 1) | (frame == 2)
    bias1 = bias_rows(mask_ref, 0, frame >= 0, blocks)
    bias3 = bias_rows(mask_ref, 0, inner, blocks)
    for head in range(heads):
        queries = rows("q", head)
        slots = (("k0", None), ("k1", bias1), ("k3", bias3))
        scores = [masked_scores(rows(name, head), queries, bias) for name, bias in slots]
        peak = scores[0].max(axis=0, keepdims=True)
        for score in scores[1:]:
            peak = jnp.maximum(peak, score.max(axis=0, keepdims=True))
        total = jnp.zeros((1, tokens), F32)
        for index, score in enumerate(scores):
            e = jnp.exp2(score - peak)
            total = total + e.sum(axis=0, keepdims=True)
            e_ref[head, index * tokens : (index + 1) * tokens] = e.astype(BF16)
        ml_ref[head, 0:1] = peak
        ml_ref[head, 1:2] = total


def far_scores_kernel(rows, frame_ref, mask_ref, ml_ref, p_ref, w_ref, dv_ref, k2_ref):
    heads, _, tokens = p_ref.shape
    blocks = tokens // BLOCK
    frame = frame_ref[0]
    inner = (frame == 1) | (frame == 2)
    bias = bias_rows(mask_ref, 1, frame >= 0, blocks)
    for head in range(heads):
        keys = jnp.where(inner, rows("kb", head), rows("ka", head))
        put(k2_ref, head, keys)
        scores = masked_scores(keys, rows("q", head), bias)
        peak2 = scores.max(axis=0, keepdims=True)
        e = jnp.exp2(scores - peak2)
        total2 = e.sum(axis=0, keepdims=True)
        peak1 = ml_ref[head, 0:1]
        peak = jnp.maximum(peak1, peak2)
        near = jnp.exp2(peak1 - peak)
        far = jnp.exp2(peak2 - peak)
        inv = 1.0 / (near * ml_ref[head, 1:2] + far * total2)
        weights = (e * (far * inv)).astype(BF16)
        put(dv_ref, head, dot(weights, rows("g", head)).astype(BF16))
        p_ref[head] = weights
        w_ref[head, 0:1] = near * inv


def near_weights(e_ref, w_ref, head, index):
    tokens = e_ref.shape[2]
    e = e_ref[head, index * tokens : (index + 1) * tokens]
    return e * w_ref[head, 0:1].astype(BF16)


def near_values_kernel(rows, e_ref, w_ref, dv0_ref, dv1_ref, dv3_ref, acc_ref):
    heads, _, tokens = e_ref.shape
    for head in range(heads):
        grads = rows("g", head)
        acc = jnp.zeros((HD, tokens), F32)
        slots = (("v0", dv0_ref), ("v1", dv1_ref), ("v3", dv3_ref))
        for index, (name, dv_ref) in enumerate(slots):
            weights = near_weights(e_ref, w_ref, head, index)
            put(dv_ref, head, dot(weights, grads).astype(BF16))
            acc = acc + dot(rows(name, head).T, weights)
        acc_ref[head] = acc


def far_values_kernel(rows, frame_ref, p_ref, acc_ref, dk_ref, att_ref, delta_ref, dq_ref):
    heads = p_ref.shape[0]
    frame = frame_ref[0]
    inner = (frame == 1) | (frame == 2)
    for head in range(heads):
        keys = rows("k2", head)
        values = jnp.where(inner, rows("vb", head), rows("va", head))
        weights = p_ref[head]
        out = (acc_ref[head] + dot(values.T, weights)).astype(BF16)
        put(att_ref, head, out.T)
        grads = rows("g", head).T
        delta = (grads.astype(F32) * out.astype(F32)).sum(axis=0, keepdims=True)
        delta_ref[head, 0:1] = delta
        ds = (weights.astype(F32) * (dot(values, grads) - delta)).astype(BF16)
        put(dk_ref, head, (dot(ds, rows("q", head)) * SCALE).astype(BF16))
        dq_ref[head] = dot(keys.T, ds)


def near_keys_kernel(rows, e_ref, w_ref, delta_ref, dq2_ref, dk0_ref, dk1_ref, dk3_ref, dq_ref):
    for head in range(e_ref.shape[0]):
        queries = rows("q", head)
        grads = rows("g", head).T
        delta = delta_ref[head, 0:1]
        dq = dq2_ref[head]
        slots = (("k0", "v0", dk0_ref), ("k1", "v1", dk1_ref), ("k3", "v3", dk3_ref))
        for index, (k_name, v_name, dk_ref) in enumerate(slots):
            weights = near_weights(e_ref, w_ref, head, index).astype(F32)
            ds = (weights * (dot(rows(v_name, head), grads) - delta)).astype(BF16)
            put(dk_ref, head, (dot(ds, queries) * SCALE).astype(BF16))
            dq = dq + dot(rows(k_name, head).T, ds)
        put(dq_ref, head, (dq * SCALE).astype(BF16).T)


def add_both_kernel(frame_ref, first_ref, middle_ref, third_ref, edge_ref, first_out, third_out):
    inner = (frame_ref[0] == 1) | (frame_ref[0] == 2)
    third_out[...] = (third_ref[...].astype(F32) + edge_ref[...].astype(F32)).astype(BF16)

    @pl.when(inner)
    def _():
        first_out[...] = (first_ref[...].astype(F32) + middle_ref[...].astype(F32)).astype(BF16)

    @pl.when(jnp.logical_not(inner))
    def _():
        first_out[...] = first_ref[...]


def sum_kernel(frame_ref, own_ref, edge_ref, middle_ref, out_ref):
    inner = (frame_ref[0] == 1) | (frame_ref[0] == 2)
    total = own_ref[...].astype(F32) + edge_ref[...].astype(F32)
    out_ref[...] = (total + jnp.where(inner, middle_ref[...].astype(F32), 0.0)).astype(BF16)


def pair_kernel(first_ref, second_ref, out_ref):
    out_ref[:, 0] = first_ref[...]
    out_ref[:, 1] = second_ref[...]


def last_kernel(frame_ref, own_ref, edge_ref, middle_ref, second_ref, out_ref):
    inner = (frame_ref[0] == 1) | (frame_ref[0] == 2)
    total = own_ref[...].astype(F32) + edge_ref[...].astype(F32)
    out_ref[:, 0] = (total + jnp.where(inner, middle_ref[...].astype(F32), 0.0)).astype(BF16)
    out_ref[:, 1] = second_ref[...]


def pack_kernel(*refs):
    out_ref, held, packed, sems, out_sems = refs[-5:]
    copies = [
        pltpu.make_async_copy(ref, held.at[which], sems.at[which])
        for which, ref in enumerate(refs[:-5])
    ]
    for copy in copies:
        copy.start()
    peers, _, _, width = out_ref.shape
    leaving = []
    for which, copy in enumerate(copies):
        copy.wait()
        for peer in range(peers):
            packed[which, peer] = held[which, :, peer * width : (peer + 1) * width]
        leaving.append(
            pltpu.make_async_copy(packed.at[which], out_ref.at[:, which], out_sems.at[which])
        )
        leaving[-1].start()
    for copy in leaving:
        copy.wait()


def pass_kernel(*refs):
    pass


def pick_kernel(places, in_ref, *out_refs):
    for place, ref in zip(places, out_refs):
        ref[...] = in_ref[:, place]


def unpack_kernel(in_ref, *out_refs):
    peers, _, _, width = in_ref.shape
    for peer in range(peers):
        for which, ref in enumerate(out_refs):
            ref[:, peer * width : (peer + 1) * width] = in_ref[peer, which]


def per_device_line(query_rows, key_rows, value_rows, out_grad, block_mask):
    plane = ("rank", "head")
    devices = ("frame", "rank", "head")
    head_parts = lax.axis_size("head")
    peers = lax.axis_size("rank") * head_parts
    rows, columns = query_rows.shape
    width = columns // peers
    heads = width // HD
    tokens = peers * rows
    one = jax.ShapeDtypeStruct((peers, rows, width), BF16)
    row_type = jax.ShapeDtypeStruct((rows, columns), BF16)
    near_e = jax.ShapeDtypeStruct((heads, 3 * tokens, tokens), BF16)
    far_e = jax.ShapeDtypeStruct((heads, tokens, tokens), BF16)
    stat = jax.ShapeDtypeStruct((heads, 8, tokens), F32)
    accum = jax.ShapeDtypeStruct((heads, HD, tokens), F32)
    frame = lax.axis_index("frame").astype(jnp.int32).reshape(1)
    smem = pl.BlockSpec(memory_space=pltpu.SMEM)
    vmem = pl.BlockSpec(memory_space=pltpu.VMEM)
    anywhere = pl.BlockSpec(memory_space=pl.ANY)
    found = {}

    def estimate(work):
        return pl.CostEstimate(
            flops=int(work * FLOPS_PER_US), bytes_accessed=1 << 16, transcendentals=0
        )

    def call(kernel, outs, work, *operands, names=()):
        several = isinstance(outs, tuple)
        arrays = []
        places = {}
        for name in names:
            array, which = found[name]
            spot = [i for i, x in enumerate(arrays) if x is array]
            if not spot:
                spot = [len(arrays)]
                arrays.append(array)
            places[name] = (spot[0], which)

        def body(*refs):
            lookup = refs[: len(arrays)]
            if not places:
                return kernel(*refs)

            def rows_of(name, head):
                index, which = places[name]
                return flat(lookup[index], head, which)

            return kernel(rows_of, *refs[len(arrays) :])

        operands = tuple(arrays) + operands
        return pl.pallas_call(
            body,
            in_specs=[smem if x.dtype == jnp.int32 else vmem for x in operands],
            out_specs=(vmem,) * len(outs) if several else vmem,
            out_shape=outs,
            compiler_params=pltpu.CompilerParams(vmem_limit_bytes=VMEM_BYTES),
            cost_estimate=estimate(work),
        )(*operands)

    def packed(count):
        return jax.ShapeDtypeStruct((peers, count, rows, width), BF16)

    def pack(*arrays, limit=VMEM_BYTES):
        count = len(arrays)
        return pl.pallas_call(
            pack_kernel,
            in_specs=[anywhere] * count,
            out_specs=anywhere,
            out_shape=packed(count),
            scratch_shapes=[
                pltpu.VMEM((count, rows, columns), BF16),
                pltpu.VMEM((count, peers, rows, width), BF16),
                pltpu.SemaphoreType.DMA((count,)),
                pltpu.SemaphoreType.DMA((count,)),
            ],
            compiler_params=pltpu.CompilerParams(vmem_limit_bytes=limit),
            cost_estimate=estimate(0.5),
        )(*arrays)

    def pick(landed, *places):
        kernel = functools.partial(pick_kernel, places)
        return call(kernel, (one,) * len(places), PICK_WORK, landed)

    def later(work, *arrays):
        return pl.pallas_call(
            pass_kernel,
            in_specs=[anywhere] * len(arrays),
            out_specs=(anywhere,) * len(arrays),
            out_shape=tuple(jax.ShapeDtypeStruct(x.shape, x.dtype) for x in arrays),
            input_output_aliases={i: i for i in range(len(arrays))},
            cost_estimate=estimate(work),
        )(*arrays)

    def swap(array):
        return lax.all_to_all(array, plane, 0, 0, tiled=True)

    def leave(pair):
        return call(unpack_kernel, (row_type, row_type), 0.5, swap(pair))

    def barrier(*values):
        return lax.optimization_barrier(values)

    def pairs_of(partner):
        pairs = []
        for frame_ in range(4):
            for rank in range(GROUP):
                for part in range(head_parts):
                    there = partner.get(frame_)
                    place = (frame_, rank ^ 1) if there is None else (there, rank)
                    pairs.append(
                        (
                            (frame_ * GROUP + rank) * head_parts + part,
                            (place[0] * GROUP + place[1]) * head_parts + part,
                        )
                    )
        return pairs

    edge = pairs_of({0: 1, 1: 0, 2: 3, 3: 2})
    middle = pairs_of({1: 2, 2: 1})

    def send(array, pairs):
        return lax.ppermute(array, devices, pairs)

    def sums(first, third, from_edge, from_middle):
        return call(
            add_both_kernel, (one, one), 0.2, frame, first, from_middle, third, from_edge
        )

    v1_rows, v3_rows = send(value_rows, edge), send(value_rows, middle)
    kqg = swap(pack(key_rows, query_rows, out_grad, limit=FIRST_PACK_BYTES))
    values = pack(value_rows, v1_rows, v3_rows)
    kqg, values = barrier(kqg, values)
    (k0,) = pick(kqg, 0)
    k1, k3 = send(k0, edge), send(k0, middle)
    k1_on, k3_on = later(SECOND_HOP_WORK, k1, k3)
    ka, kb = send(k3_on, edge), send(k1_on, middle)
    for name, array in (("k0", k0), ("k1", k1), ("k3", k3), ("ka", ka), ("kb", kb)):
        found[name] = (array, None)
    found.update(q=(kqg, 1), g=(kqg, 2))
    e_near, ml = call(
        near_scores_kernel, (near_e, stat), 3.5, frame, block_mask,
        names=("q", "k0", "k1", "k3"),
    )
    values, ml = barrier(swap(values), ml)
    v1, v3 = pick(values, 1, 2)
    found.update(v0=(values, 0), v1=(values, 1), v3=(values, 2))
    found.update(va=(send(v3, edge), None), vb=(send(v1, middle), None))

    p_far, w, dv2, k2 = call(
        far_scores_kernel, (far_e, stat, one, one), 2, frame, block_mask, ml,
        names=("q", "g", "ka", "kb"),
    )
    found["k2"] = (k2, None)
    dv_edge, dv_middle = send(dv2, edge), send(dv2, middle)
    dv0, dv1, dv3, acc = call(
        near_values_kernel, (one, one, one, accum), 2, e_near, w,
        names=("g", "v0", "v1", "v3"),
    )
    dk2, att, delta, dq2 = call(
        far_values_kernel, (one, one, stat, accum), 2, frame, p_far, acc,
        names=("q", "g", "k2", "va", "vb"),
    )
    dk_edge, dk_middle = send(dk2, edge), send(dk2, middle)
    dk0, dk1, dk3, dq = call(
        near_keys_kernel, (one, one, one, one), 4, e_near, w, delta, dq2,
        names=("q", "g", "k0", "k1", "k3", "v0", "v1", "v3"),
    )
    dq, dv1, dv3 = barrier(dq, dv1, dv3)
    dv_first, dv_third = sums(dv1, dv3, dv_edge, dv_middle)
    dv_over = send(dv_first, edge), send(dv_third, middle)
    dk_first, dk_third = sums(dk1, dk3, dk_edge, dk_middle)
    dk_over = send(dk_first, edge), send(dk_third, middle)
    attended, grad_query = leave(call(pair_kernel, packed(2), 0.5, att, dq))
    dv = call(sum_kernel, one, SUM_WORK, frame, dv0, *dv_over)
    grad_keys, grad_values = leave(
        call(last_kernel, packed(2), 0.5, frame, dk0, *dk_over, dv)
    )
    return attended, grad_query, grad_keys, grad_values


def solution(mesh):
    seq, head = mesh.shape["seq"], mesh.shape["head"]
    frames = seq // GROUP
    line = Mesh(mesh.devices.reshape(frames, GROUP, head), ("frame", "rank", "head"))

    def run(query_rows, key_rows, value_rows, out_grad, block_mask):
        heads = query_rows.shape[1] // HD
        tokens = query_rows.shape[0] // frames
        fits = (
            frames == 4
            and block_mask.shape[0] == 2
            and heads % (GROUP * head) == 0
            and tokens == block_mask.shape[1] * BLOCK
            and tokens // (GROUP * head) % 16 == 0
        )
        if fits:
            body, where, axes = per_device_line, line, ("frame", "rank", "head")
        else:
            body, where, axes = per_device_general, mesh, ("seq", "head")
        row_spec = P(axes, None)
        return jax.shard_map(
            body,
            mesh=where,
            in_specs=(row_spec,) * 4 + (P(),),
            out_specs=(row_spec,) * 4,
            check_vma=False,
        )(query_rows, key_rows, value_rows, out_grad, block_mask)

    return run
```

```python
import functools
import math

import jax
import jax.numpy as jnp
from jax import lax
from jax.experimental import pallas as pl
from jax.experimental.pallas import tpu as pltpu
from jax.sharding import Mesh
from jax.sharding import PartitionSpec as P

HD = 128
BLOCK = 128
GROUP = 4
SCALE = 1.0 / math.sqrt(HD)
SCALE_LOG2 = SCALE * math.log2(math.e)
MASKED = -1e30
VMEM_BYTES = 12 * 1024 * 1024
FIRST_PACK_BYTES = 60 * 1024 * 1024

FLOPS_PER_US = 1_150_000_000
PACK_VALUES_WORK = 40
PICK_WORK = 20
SUM_WORK = 20


def partner_2(shard, axis, distance):
    return lax.ppermute(shard, axis, [(i, i ^ 1 << distance) for i in range(lax.axis_size(axis))])


def passed_along(shard, axis, by):
    peers = lax.axis_size(axis)
    pairs = [(i, i + by) for i in range(peers) if 0 <= i + by < peers]
    return lax.ppermute(shard, axis, pairs)


def widen_mask(bits):
    blocks = bits.shape[0]
    grid = jnp.broadcast_to((bits > 0)[:, None, :, None], (blocks, BLOCK, blocks, BLOCK))
    return grid.reshape(blocks * BLOCK, blocks * BLOCK)


def place_pair(mine, other, is_low, dim):
    return lax.cond(
        is_low,
        lambda pair: jnp.concatenate([pair[0], pair[1]], dim),
        lambda pair: jnp.concatenate([pair[1], pair[0]], dim),
        (mine, other),
    )


def per_device_general(query_rows, key_rows, value_rows, out_grad, block_mask):
    queries, keys_local, values_local, grads_output = (
        lax.all_to_all(query_rows, "head", split_axis=1, concat_axis=0, tiled=True),
        lax.all_to_all(key_rows, "head", split_axis=1, concat_axis=0, tiled=True),
        lax.all_to_all(value_rows, "head", split_axis=1, concat_axis=0, tiled=True),
        lax.all_to_all(out_grad, "head", split_axis=1, concat_axis=0, tiled=True),
    )
    seq_index = lax.axis_index("seq")
    group_bits = GROUP.bit_length() - 1
    rank = seq_index % GROUP
    frame_index = seq_index // GROUP
    frame_count = lax.axis_size("seq") // GROUP
    level_count = block_mask.shape[0]
    block_rows = queries.shape[0]
    frame_tokens = block_rows * GROUP
    head_count = queries.shape[1] // HD
    score_scale = 1.0 / math.sqrt(HD)
    own_pair = jnp.stack([keys_local, values_local])

    def low_bit(bit):
        return seq_index >> bit & 1 == 0

    whole_pair = own_pair
    for bit in range(group_bits):
        other = partner_2(whole_pair, "seq", bit)
        whole_pair = place_pair(whole_pair, other, low_bit(bit), 1)
    partner_list = []
    for level_index in range(level_count):
        for orient in (1, -1):
            partner_list.append(
                passed_along(whole_pair, "seq", orient * GROUP * (1 << level_index))
            )
    every_pair = jnp.concatenate([whole_pair] + partner_list, axis=1)
    keys_all, values_all = (every_pair[0], every_pair[1])
    allowed_list = [jnp.ones((block_rows, frame_tokens), bool)]
    for level_index in range(level_count):
        for orient in (1, -1):
            partner = frame_index - orient * (1 << level_index)
            inside = (partner >= 0) & (partner < frame_count)
            allowed_list.append(
                lax.dynamic_slice_in_dim(
                    widen_mask(block_mask[level_index]), rank * block_rows, block_rows, 0
                )
                & inside
            )
    allowed = jnp.concatenate(allowed_list, axis=1)

    def head_scores(query_head, keys_head):
        scores = (
            jnp.einsum("qd,kd->qk", query_head, keys_head, preferred_element_type=jnp.float32)
            * score_scale
        )
        return jnp.where(allowed, scores, -jnp.inf)

    outputs = []
    logsums = []
    for head_index in range(head_count):
        columns = slice(head_index * HD, (head_index + 1) * HD)
        scores = head_scores(queries[:, columns], keys_all[:, columns])
        peak = jnp.max(scores, axis=1, keepdims=True)
        logsum = peak + jnp.log(jnp.sum(jnp.exp(scores - peak), axis=1, keepdims=True))
        weights = jnp.exp(scores - logsum).astype(jnp.bfloat16)
        outputs.append(
            jnp.dot(weights, values_all[:, columns], preferred_element_type=jnp.float32).astype(
                jnp.bfloat16
            )
        )
        logsums.append(logsum)
    attended = jnp.concatenate(outputs, axis=1)
    query_grads = []
    key_grads = []
    value_grads = []
    for head_index in range(head_count):
        columns = slice(head_index * HD, (head_index + 1) * HD)
        query_head = queries[:, columns]
        grad_head = grads_output[:, columns]
        scores = head_scores(query_head, keys_all[:, columns])
        probability = jnp.exp(scores - logsums[head_index])
        weights = probability.astype(jnp.bfloat16)
        grad_weights = jnp.einsum(
            "qd,kd->qk", grad_head, values_all[:, columns], preferred_element_type=jnp.float32
        )
        delta_row = jnp.sum(
            grad_head.astype(jnp.float32) * attended[:, columns].astype(jnp.float32),
            axis=1,
            keepdims=True,
        )
        grad_scores = (probability * (grad_weights - delta_row) * score_scale).astype(jnp.bfloat16)
        query_grads.append(
            jnp.dot(grad_scores, keys_all[:, columns], preferred_element_type=jnp.float32).astype(
                jnp.bfloat16
            )
        )
        key_grads.append(
            jnp.einsum(
                "qk,qd->kd", grad_scores, query_head, preferred_element_type=jnp.float32
            ).astype(jnp.bfloat16)
        )
        value_grads.append(
            jnp.einsum("qk,qd->kd", weights, grad_head, preferred_element_type=jnp.float32).astype(
                jnp.bfloat16
            )
        )
    grad_query = jnp.concatenate(query_grads, axis=1)
    grad_pair = jnp.stack(
        [jnp.concatenate(key_grads, axis=1), jnp.concatenate(value_grads, axis=1)]
    )
    total = grad_pair[:, :frame_tokens].astype(jnp.float32)
    piece_index = 1
    for level_index in range(level_count):
        for orient in (1, -1):
            piece = grad_pair[:, piece_index * frame_tokens : (piece_index + 1) * frame_tokens]
            returned = passed_along(piece, "seq", -orient * GROUP * (1 << level_index))
            total = total + returned.astype(jnp.float32)
            piece_index += 1
    for bit in reversed(range(group_bits)):
        half = total.shape[1] // 2
        first_half = total[:, :half]
        second_half = total[:, half:]
        is_low = low_bit(bit)
        outgoing = jnp.where(is_low, second_half, first_half)
        staying = jnp.where(is_low, first_half, second_half)
        total = staying + partner_2(outgoing, "seq", bit)
    grad_keys = total[0].astype(jnp.bfloat16)
    grad_values = total[1].astype(jnp.bfloat16)
    return (
        lax.all_to_all(attended, "head", split_axis=0, concat_axis=1, tiled=True),
        lax.all_to_all(grad_query, "head", split_axis=0, concat_axis=1, tiled=True),
        lax.all_to_all(grad_keys, "head", split_axis=0, concat_axis=1, tiled=True),
        lax.all_to_all(grad_values, "head", split_axis=0, concat_axis=1, tiled=True),
    )


NT = (((1,), (1,)), ((), ()))
F32 = jnp.float32
BF16 = jnp.bfloat16


def dot(a, b):
    return jnp.dot(a, b, preferred_element_type=F32)


def dot_nt(a, b):
    return lax.dot_general(a, b, NT, preferred_element_type=F32)


def head_columns(head):
    return slice(head * HD, (head + 1) * HD)


def flat(ref, head, which=None):
    columns = head_columns(head)
    part = ref[:, :, columns] if which is None else ref[:, which, :, columns]
    return part.reshape(part.shape[0] * part.shape[1], HD)


def put(ref, head, rows, which=None):
    if which is None:
        ref[:, :, head_columns(head)] = rows.reshape(ref.shape[0], ref.shape[1], HD)
    else:
        ref[:, which, :, head_columns(head)] = rows.reshape(ref.shape[0], ref.shape[2], HD)


def bias_rows(mask_ref, level, valid, blocks):
    lane_block = lax.broadcasted_iota(jnp.int32, (1, blocks * BLOCK), 1) // BLOCK
    rows = []
    for key_block in range(blocks):
        row = jnp.zeros((1, blocks * BLOCK), F32)
        for query_block in range(blocks):
            open_ = (mask_ref[level, query_block, key_block] > 0) & valid
            value = jnp.where(open_, 0.0, MASKED).astype(F32)
            row = jnp.where(lane_block == query_block, value, row)
        rows.append(row)
    return rows


def masked_scores(keys, queries, bias):
    scores = dot_nt(keys, queries) * SCALE_LOG2
    if bias is None:
        return scores
    blocks = len(bias)
    return jnp.concatenate(
        [scores[j * BLOCK : (j + 1) * BLOCK] + bias[j] for j in range(blocks)], axis=0
    )


def near_scores_kernel(rows, frame_ref, mask_ref, e_ref, ml_ref):
    heads, _, tokens = e_ref.shape
    blocks = tokens // BLOCK
    frame = frame_ref[0]
    inner = (frame == 1) | (frame == 2)
    bias1 = bias_rows(mask_ref, 0, frame >= 0, blocks)
    bias3 = bias_rows(mask_ref, 0, inner, blocks)
    for head in range(heads):
        queries = rows("q", head)
        slots = (("k0", None), ("k1", bias1), ("k3", bias3))
        scores = [masked_scores(rows(name, head), queries, bias) for name, bias in slots]
        peak = scores[0].max(axis=0, keepdims=True)
        for score in scores[1:]:
            peak = jnp.maximum(peak, score.max(axis=0, keepdims=True))
        total = jnp.zeros((1, tokens), F32)
        for index, score in enumerate(scores):
            e = jnp.exp2(score - peak)
            total = total + e.sum(axis=0, keepdims=True)
            e_ref[head, index * tokens : (index + 1) * tokens] = e.astype(BF16)
        ml_ref[head, 0:1] = peak
        ml_ref[head, 1:2] = total


def far_scores_kernel(rows, frame_ref, mask_ref, ml_ref, p_ref, w_ref, dv_ref, k2_ref):
    heads, _, tokens = p_ref.shape
    blocks = tokens // BLOCK
    frame = frame_ref[0]
    inner = (frame == 1) | (frame == 2)
    bias = bias_rows(mask_ref, 1, frame >= 0, blocks)
    for head in range(heads):
        keys = jnp.where(inner, rows("kb", head), rows("ka", head))
        put(k2_ref, head, keys)
        scores = masked_scores(keys, rows("q", head), bias)
        peak2 = scores.max(axis=0, keepdims=True)
        e = jnp.exp2(scores - peak2)
        total2 = e.sum(axis=0, keepdims=True)
        peak1 = ml_ref[head, 0:1]
        peak = jnp.maximum(peak1, peak2)
        near = jnp.exp2(peak1 - peak)
        far = jnp.exp2(peak2 - peak)
        inv = 1.0 / (near * ml_ref[head, 1:2] + far * total2)
        weights = (e * (far * inv)).astype(BF16)
        put(dv_ref, head, dot(weights, rows("g", head)).astype(BF16))
        p_ref[head] = weights
        w_ref[head, 0:1] = near * inv


def near_weights(e_ref, w_ref, head, index):
    tokens = e_ref.shape[2]
    e = e_ref[head, index * tokens : (index + 1) * tokens]
    return e * w_ref[head, 0:1].astype(BF16)


def near_values_kernel(rows, e_ref, w_ref, dv0_ref, dv1_ref, dv3_ref, acc_ref):
    heads, _, tokens = e_ref.shape
    for head in range(heads):
        grads = rows("g", head)
        acc = jnp.zeros((HD, tokens), F32)
        slots = (("v0", dv0_ref), ("v1", dv1_ref), ("v3", dv3_ref))
        for index, (name, dv_ref) in enumerate(slots):
            weights = near_weights(e_ref, w_ref, head, index)
            put(dv_ref, head, dot(weights, grads).astype(BF16))
            acc = acc + dot(rows(name, head).T, weights)
        acc_ref[head] = acc


def far_values_kernel(rows, frame_ref, p_ref, acc_ref, dk_ref, att_ref, delta_ref, dq_ref):
    heads = p_ref.shape[0]
    frame = frame_ref[0]
    inner = (frame == 1) | (frame == 2)
    for head in range(heads):
        keys = rows("k2", head)
        values = jnp.where(inner, rows("vb", head), rows("va", head))
        weights = p_ref[head]
        out = (acc_ref[head] + dot(values.T, weights)).astype(BF16)
        put(att_ref, head, out.T)
        grads = rows("g", head).T
        delta = (grads.astype(F32) * out.astype(F32)).sum(axis=0, keepdims=True)
        delta_ref[head, 0:1] = delta
        ds = (weights.astype(F32) * (dot(values, grads) - delta)).astype(BF16)
        put(dk_ref, head, (dot(ds, rows("q", head)) * SCALE).astype(BF16))
        dq_ref[head] = dot(keys.T, ds)


def near_keys_kernel(rows, e_ref, w_ref, delta_ref, dq2_ref, dk0_ref, dk1_ref, dk3_ref, dq_ref):
    for head in range(e_ref.shape[0]):
        queries = rows("q", head)
        grads = rows("g", head).T
        delta = delta_ref[head, 0:1]
        dq = dq2_ref[head]
        slots = (("k0", "v0", dk0_ref), ("k1", "v1", dk1_ref), ("k3", "v3", dk3_ref))
        for index, (k_name, v_name, dk_ref) in enumerate(slots):
            weights = near_weights(e_ref, w_ref, head, index).astype(F32)
            ds = (weights * (dot(rows(v_name, head), grads) - delta)).astype(BF16)
            put(dk_ref, head, (dot(ds, queries) * SCALE).astype(BF16))
            dq = dq + dot(rows(k_name, head).T, ds)
        put(dq_ref, head, (dq * SCALE).astype(BF16).T)


def add_both_kernel(frame_ref, first_ref, middle_ref, third_ref, edge_ref, first_out, third_out):
    inner = (frame_ref[0] == 1) | (frame_ref[0] == 2)
    third_out[...] = (third_ref[...].astype(F32) + edge_ref[...].astype(F32)).astype(BF16)

    @pl.when(inner)
    def _():
        first_out[...] = (first_ref[...].astype(F32) + middle_ref[...].astype(F32)).astype(BF16)

    @pl.when(jnp.logical_not(inner))
    def _():
        first_out[...] = first_ref[...]


def sum_kernel(frame_ref, own_ref, edge_ref, middle_ref, out_ref):
    inner = (frame_ref[0] == 1) | (frame_ref[0] == 2)
    total = own_ref[...].astype(F32) + edge_ref[...].astype(F32)
    out_ref[...] = (total + jnp.where(inner, middle_ref[...].astype(F32), 0.0)).astype(BF16)


def pair_kernel(first_ref, second_ref, out_ref):
    out_ref[:, 0] = first_ref[...]
    out_ref[:, 1] = second_ref[...]


def last_kernel(frame_ref, own_ref, edge_ref, middle_ref, second_ref, out_ref):
    inner = (frame_ref[0] == 1) | (frame_ref[0] == 2)
    total = own_ref[...].astype(F32) + edge_ref[...].astype(F32)
    out_ref[:, 0] = (total + jnp.where(inner, middle_ref[...].astype(F32), 0.0)).astype(BF16)
    out_ref[:, 1] = second_ref[...]


def pack_kernel(*refs):
    out_ref, held, packed, sems, out_sems = refs[-5:]
    copies = [
        pltpu.make_async_copy(ref, held.at[which], sems.at[which])
        for which, ref in enumerate(refs[:-5])
    ]
    for copy in copies:
        copy.start()
    peers, _, _, width = out_ref.shape
    leaving = []
    for which, copy in enumerate(copies):
        copy.wait()
        for peer in range(peers):
            packed[which, peer] = held[which, :, peer * width : (peer + 1) * width]
        leaving.append(
            pltpu.make_async_copy(packed.at[which], out_ref.at[:, which], out_sems.at[which])
        )
        leaving[-1].start()
    for copy in leaving:
        copy.wait()


def pick_kernel(places, in_ref, *out_refs):
    for place, ref in zip(places, out_refs):
        ref[...] = in_ref[:, place]


def unpack_kernel(in_ref, *out_refs):
    peers, _, _, width = in_ref.shape
    for peer in range(peers):
        for which, ref in enumerate(out_refs):
            ref[:, peer * width : (peer + 1) * width] = in_ref[peer, which]


def per_device_line(query_rows, key_rows, value_rows, out_grad, block_mask):
    plane = ("rank", "head")
    devices = ("frame", "rank", "head")
    head_parts = lax.axis_size("head")
    peers = lax.axis_size("rank") * head_parts
    rows, columns = query_rows.shape
    width = columns // peers
    heads = width // HD
    tokens = peers * rows
    one = jax.ShapeDtypeStruct((peers, rows, width), BF16)
    row_type = jax.ShapeDtypeStruct((rows, columns), BF16)
    near_e = jax.ShapeDtypeStruct((heads, 3 * tokens, tokens), BF16)
    far_e = jax.ShapeDtypeStruct((heads, tokens, tokens), BF16)
    stat = jax.ShapeDtypeStruct((heads, 8, tokens), F32)
    accum = jax.ShapeDtypeStruct((heads, HD, tokens), F32)
    frame = lax.axis_index("frame").astype(jnp.int32).reshape(1)
    smem = pl.BlockSpec(memory_space=pltpu.SMEM)
    vmem = pl.BlockSpec(memory_space=pltpu.VMEM)
    anywhere = pl.BlockSpec(memory_space=pl.ANY)
    found = {}

    def estimate(work):
        return pl.CostEstimate(
            flops=int(work * FLOPS_PER_US), bytes_accessed=1 << 16, transcendentals=0
        )

    def call(kernel, outs, work, *operands, names=()):
        several = isinstance(outs, tuple)
        arrays = []
        places = {}
        for name in names:
            array, which = found[name]
            spot = [i for i, x in enumerate(arrays) if x is array]
            if not spot:
                spot = [len(arrays)]
                arrays.append(array)
            places[name] = (spot[0], which)

        def body(*refs):
            lookup = refs[: len(arrays)]
            if not places:
                return kernel(*refs)

            def rows_of(name, head):
                index, which = places[name]
                return flat(lookup[index], head, which)

            return kernel(rows_of, *refs[len(arrays) :])

        operands = tuple(arrays) + operands
        return pl.pallas_call(
            body,
            in_specs=[smem if x.dtype == jnp.int32 else vmem for x in operands],
            out_specs=(vmem,) * len(outs) if several else vmem,
            out_shape=outs,
            compiler_params=pltpu.CompilerParams(vmem_limit_bytes=VMEM_BYTES),
            cost_estimate=estimate(work),
        )(*operands)

    def packed(count):
        return jax.ShapeDtypeStruct((peers, count, rows, width), BF16)

    def pack(*arrays, limit=VMEM_BYTES, work=0.5):
        count = len(arrays)
        return pl.pallas_call(
            pack_kernel,
            in_specs=[anywhere] * count,
            out_specs=anywhere,
            out_shape=packed(count),
            scratch_shapes=[
                pltpu.VMEM((count, rows, columns), BF16),
                pltpu.VMEM((count, peers, rows, width), BF16),
                pltpu.SemaphoreType.DMA((count,)),
                pltpu.SemaphoreType.DMA((count,)),
            ],
            compiler_params=pltpu.CompilerParams(vmem_limit_bytes=limit),
            cost_estimate=estimate(work),
        )(*arrays)

    def pick(landed, *places):
        kernel = functools.partial(pick_kernel, places)
        return call(kernel, (one,) * len(places), PICK_WORK, landed)

    def swap(array):
        return lax.all_to_all(array, plane, 0, 0, tiled=True)

    def leave(pair):
        return call(unpack_kernel, (row_type, row_type), 0.5, swap(pair))

    def barrier(*values):
        return lax.optimization_barrier(values)

    def pairs_of(partner):
        pairs = []
        for frame_ in range(4):
            for rank in range(GROUP):
                for part in range(head_parts):
                    there = partner.get(frame_)
                    place = (frame_, rank ^ 1) if there is None else (there, rank)
                    pairs.append(
                        (
                            (frame_ * GROUP + rank) * head_parts + part,
                            (place[0] * GROUP + place[1]) * head_parts + part,
                        )
                    )
        return pairs

    edge = pairs_of({0: 1, 1: 0, 2: 3, 3: 2})
    middle = pairs_of({1: 2, 2: 1})

    def send(array, pairs):
        return lax.ppermute(array, devices, pairs)

    def sums(first, third, from_edge, from_middle):
        return call(
            add_both_kernel, (one, one), 0.2, frame, first, from_middle, third, from_edge
        )

    v1_rows, v3_rows = send(value_rows, edge), send(value_rows, middle)
    kq = swap(pack(key_rows, query_rows, limit=FIRST_PACK_BYTES))
    values = pack(value_rows, v1_rows, v3_rows, out_grad, work=PACK_VALUES_WORK)
    kq, values = barrier(kq, values)
    (k0,) = pick(kq, 0)
    k1, k3 = send(k0, edge), send(k0, middle)
    ka, kb = send(k3, edge), send(k1, middle)
    for name, array in (("k0", k0), ("k1", k1), ("k3", k3), ("ka", ka), ("kb", kb)):
        found[name] = (array, None)
    found.update(q=(kq, 1))
    values = swap(values)
    v1, v3 = pick(values, 1, 2)
    found.update(g=(values, 3), v0=(values, 0), v1=(values, 1), v3=(values, 2))
    found.update(va=(send(v3, edge), None), vb=(send(v1, middle), None))
    k0, v1 = barrier(k0, v1)
    found["k0"] = (k0, None)
    e_near, ml = call(
        near_scores_kernel, (near_e, stat), 3.5, frame, block_mask,
        names=("q", "k0", "k1", "k3"),
    )

    p_far, w, dv2, k2 = call(
        far_scores_kernel, (far_e, stat, one, one), 10, frame, block_mask, ml,
        names=("q", "g", "ka", "kb"),
    )
    found["k2"] = (k2, None)
    dv_edge, dv_middle = send(dv2, edge), send(dv2, middle)
    dv0, dv1, dv3, acc = call(
        near_values_kernel, (one, one, one, accum), 2, e_near, w,
        names=("g", "v0", "v1", "v3"),
    )
    dk2, att, delta, dq2 = call(
        far_values_kernel, (one, one, stat, accum), 2, frame, p_far, acc,
        names=("q", "g", "k2", "va", "vb"),
    )
    dk_edge, dk_middle = send(dk2, edge), send(dk2, middle)
    dk0, dk1, dk3, dq = call(
        near_keys_kernel, (one, one, one, one), 4, e_near, w, delta, dq2,
        names=("q", "g", "k0", "k1", "k3", "v0", "v1", "v3"),
    )
    dq, dv1, dv3 = barrier(dq, dv1, dv3)
    dv_first, dv_third = sums(dv1, dv3, dv_edge, dv_middle)
    dv_over = send(dv_first, edge), send(dv_third, middle)
    dk_first, dk_third = sums(dk1, dk3, dk_edge, dk_middle)
    dk_over = send(dk_first, edge), send(dk_third, middle)
    attended, grad_query = leave(call(pair_kernel, packed(2), 0.5, att, dq))
    dv = call(sum_kernel, one, SUM_WORK, frame, dv0, *dv_over)
    grad_keys, grad_values = leave(
        call(last_kernel, packed(2), 0.5, frame, dk0, *dk_over, dv)
    )
    return attended, grad_query, grad_keys, grad_values


def solution(mesh):
    seq, head = mesh.shape["seq"], mesh.shape["head"]
    frames = seq // GROUP
    line = Mesh(mesh.devices.reshape(frames, GROUP, head), ("frame", "rank", "head"))

    def run(query_rows, key_rows, value_rows, out_grad, block_mask):
        heads = query_rows.shape[1] // HD
        tokens = query_rows.shape[0] // frames
        fits = (
            frames == 4
            and block_mask.shape[0] == 2
            and heads % (GROUP * head) == 0
            and tokens == block_mask.shape[1] * BLOCK
            and tokens // (GROUP * head) % 16 == 0
        )
        if fits:
            body, where, axes = per_device_line, line, ("frame", "rank", "head")
        else:
            body, where, axes = per_device_general, mesh, ("seq", "head")
        row_spec = P(axes, None)
        return jax.shard_map(
            body,
            mesh=where,
            in_specs=(row_spec,) * 4 + (P(),),
            out_specs=(row_spec,) * 4,
            check_vma=False,
        )(query_rows, key_rows, value_rows, out_grad, block_mask)

    return run
```

```python
import functools
import math

import jax
import jax.numpy as jnp
from jax import lax
from jax.experimental import pallas as pl
from jax.experimental.pallas import tpu as pltpu
from jax.sharding import Mesh
from jax.sharding import PartitionSpec as P

HD = 128
BLOCK = 128
GROUP = 4
SCALE = 1.0 / math.sqrt(HD)
SCALE_LOG2 = SCALE * math.log2(math.e)
MASKED = -1e30
VMEM_BYTES = 12 * 1024 * 1024
FIRST_PACK_BYTES = 60 * 1024 * 1024

FLOPS_PER_US = 1_150_000_000
SECOND_HOP_WORK = 20
PICK_WORK = 20
SUM_WORK = 20


def partner_2(shard, axis, distance):
    return lax.ppermute(shard, axis, [(i, i ^ 1 << distance) for i in range(lax.axis_size(axis))])


def passed_along(shard, axis, by):
    peers = lax.axis_size(axis)
    pairs = [(i, i + by) for i in range(peers) if 0 <= i + by < peers]
    return lax.ppermute(shard, axis, pairs)


def widen_mask(bits):
    blocks = bits.shape[0]
    grid = jnp.broadcast_to((bits > 0)[:, None, :, None], (blocks, BLOCK, blocks, BLOCK))
    return grid.reshape(blocks * BLOCK, blocks * BLOCK)


def place_pair(mine, other, is_low, dim):
    return lax.cond(
        is_low,
        lambda pair: jnp.concatenate([pair[0], pair[1]], dim),
        lambda pair: jnp.concatenate([pair[1], pair[0]], dim),
        (mine, other),
    )


def per_device_general(query_rows, key_rows, value_rows, out_grad, block_mask):
    queries, keys_local, values_local, grads_output = (
        lax.all_to_all(query_rows, "head", split_axis=1, concat_axis=0, tiled=True),
        lax.all_to_all(key_rows, "head", split_axis=1, concat_axis=0, tiled=True),
        lax.all_to_all(value_rows, "head", split_axis=1, concat_axis=0, tiled=True),
        lax.all_to_all(out_grad, "head", split_axis=1, concat_axis=0, tiled=True),
    )
    seq_index = lax.axis_index("seq")
    group_bits = GROUP.bit_length() - 1
    rank = seq_index % GROUP
    frame_index = seq_index // GROUP
    frame_count = lax.axis_size("seq") // GROUP
    level_count = block_mask.shape[0]
    block_rows = queries.shape[0]
    frame_tokens = block_rows * GROUP
    head_count = queries.shape[1] // HD
    score_scale = 1.0 / math.sqrt(HD)
    own_pair = jnp.stack([keys_local, values_local])

    def low_bit(bit):
        return seq_index >> bit & 1 == 0

    whole_pair = own_pair
    for bit in range(group_bits):
        other = partner_2(whole_pair, "seq", bit)
        whole_pair = place_pair(whole_pair, other, low_bit(bit), 1)
    partner_list = []
    for level_index in range(level_count):
        for orient in (1, -1):
            partner_list.append(
                passed_along(whole_pair, "seq", orient * GROUP * (1 << level_index))
            )
    every_pair = jnp.concatenate([whole_pair] + partner_list, axis=1)
    keys_all, values_all = (every_pair[0], every_pair[1])
    allowed_list = [jnp.ones((block_rows, frame_tokens), bool)]
    for level_index in range(level_count):
        for orient in (1, -1):
            partner = frame_index - orient * (1 << level_index)
            inside = (partner >= 0) & (partner < frame_count)
            allowed_list.append(
                lax.dynamic_slice_in_dim(
                    widen_mask(block_mask[level_index]), rank * block_rows, block_rows, 0
                )
                & inside
            )
    allowed = jnp.concatenate(allowed_list, axis=1)

    def head_scores(query_head, keys_head):
        scores = (
            jnp.einsum("qd,kd->qk", query_head, keys_head, preferred_element_type=jnp.float32)
            * score_scale
        )
        return jnp.where(allowed, scores, -jnp.inf)

    outputs = []
    logsums = []
    for head_index in range(head_count):
        columns = slice(head_index * HD, (head_index + 1) * HD)
        scores = head_scores(queries[:, columns], keys_all[:, columns])
        peak = jnp.max(scores, axis=1, keepdims=True)
        logsum = peak + jnp.log(jnp.sum(jnp.exp(scores - peak), axis=1, keepdims=True))
        weights = jnp.exp(scores - logsum).astype(jnp.bfloat16)
        outputs.append(
            jnp.dot(weights, values_all[:, columns], preferred_element_type=jnp.float32).astype(
                jnp.bfloat16
            )
        )
        logsums.append(logsum)
    attended = jnp.concatenate(outputs, axis=1)
    query_grads = []
    key_grads = []
    value_grads = []
    for head_index in range(head_count):
        columns = slice(head_index * HD, (head_index + 1) * HD)
        query_head = queries[:, columns]
        grad_head = grads_output[:, columns]
        scores = head_scores(query_head, keys_all[:, columns])
        probability = jnp.exp(scores - logsums[head_index])
        weights = probability.astype(jnp.bfloat16)
        grad_weights = jnp.einsum(
            "qd,kd->qk", grad_head, values_all[:, columns], preferred_element_type=jnp.float32
        )
        delta_row = jnp.sum(
            grad_head.astype(jnp.float32) * attended[:, columns].astype(jnp.float32),
            axis=1,
            keepdims=True,
        )
        grad_scores = (probability * (grad_weights - delta_row) * score_scale).astype(jnp.bfloat16)
        query_grads.append(
            jnp.dot(grad_scores, keys_all[:, columns], preferred_element_type=jnp.float32).astype(
                jnp.bfloat16
            )
        )
        key_grads.append(
            jnp.einsum(
                "qk,qd->kd", grad_scores, query_head, preferred_element_type=jnp.float32
            ).astype(jnp.bfloat16)
        )
        value_grads.append(
            jnp.einsum("qk,qd->kd", weights, grad_head, preferred_element_type=jnp.float32).astype(
                jnp.bfloat16
            )
        )
    grad_query = jnp.concatenate(query_grads, axis=1)
    grad_pair = jnp.stack(
        [jnp.concatenate(key_grads, axis=1), jnp.concatenate(value_grads, axis=1)]
    )
    total = grad_pair[:, :frame_tokens].astype(jnp.float32)
    piece_index = 1
    for level_index in range(level_count):
        for orient in (1, -1):
            piece = grad_pair[:, piece_index * frame_tokens : (piece_index + 1) * frame_tokens]
            returned = passed_along(piece, "seq", -orient * GROUP * (1 << level_index))
            total = total + returned.astype(jnp.float32)
            piece_index += 1
    for bit in reversed(range(group_bits)):
        half = total.shape[1] // 2
        first_half = total[:, :half]
        second_half = total[:, half:]
        is_low = low_bit(bit)
        outgoing = jnp.where(is_low, second_half, first_half)
        staying = jnp.where(is_low, first_half, second_half)
        total = staying + partner_2(outgoing, "seq", bit)
    grad_keys = total[0].astype(jnp.bfloat16)
    grad_values = total[1].astype(jnp.bfloat16)
    return (
        lax.all_to_all(attended, "head", split_axis=0, concat_axis=1, tiled=True),
        lax.all_to_all(grad_query, "head", split_axis=0, concat_axis=1, tiled=True),
        lax.all_to_all(grad_keys, "head", split_axis=0, concat_axis=1, tiled=True),
        lax.all_to_all(grad_values, "head", split_axis=0, concat_axis=1, tiled=True),
    )


NT = (((1,), (1,)), ((), ()))
F32 = jnp.float32
BF16 = jnp.bfloat16


def dot(a, b):
    return jnp.dot(a, b, preferred_element_type=F32)


def dot_nt(a, b):
    return lax.dot_general(a, b, NT, preferred_element_type=F32)


def head_columns(head):
    return slice(head * HD, (head + 1) * HD)


def flat(ref, head, which=None):
    columns = head_columns(head)
    part = ref[:, :, columns] if which is None else ref[:, which, :, columns]
    return part.reshape(part.shape[0] * part.shape[1], HD)


def put(ref, head, rows, which=None):
    if which is None:
        ref[:, :, head_columns(head)] = rows.reshape(ref.shape[0], ref.shape[1], HD)
    else:
        ref[:, which, :, head_columns(head)] = rows.reshape(ref.shape[0], ref.shape[2], HD)


def bias_rows(mask_ref, level, valid, blocks):
    lane_block = lax.broadcasted_iota(jnp.int32, (1, blocks * BLOCK), 1) // BLOCK
    rows = []
    for key_block in range(blocks):
        row = jnp.zeros((1, blocks * BLOCK), F32)
        for query_block in range(blocks):
            open_ = (mask_ref[level, query_block, key_block] > 0) & valid
            value = jnp.where(open_, 0.0, MASKED).astype(F32)
            row = jnp.where(lane_block == query_block, value, row)
        rows.append(row)
    return rows


def masked_scores(keys, queries, bias):
    scores = dot_nt(keys, queries) * SCALE_LOG2
    if bias is None:
        return scores
    blocks = len(bias)
    return jnp.concatenate(
        [scores[j * BLOCK : (j + 1) * BLOCK] + bias[j] for j in range(blocks)], axis=0
    )


def near_scores_kernel(rows, frame_ref, mask_ref, e_ref, ml_ref):
    heads, _, tokens = e_ref.shape
    blocks = tokens // BLOCK
    frame = frame_ref[0]
    inner = (frame == 1) | (frame == 2)
    bias1 = bias_rows(mask_ref, 0, frame >= 0, blocks)
    bias3 = bias_rows(mask_ref, 0, inner, blocks)
    for head in range(heads):
        queries = rows("q", head)
        slots = (("k0", None), ("k1", bias1), ("k3", bias3))
        scores = [masked_scores(rows(name, head), queries, bias) for name, bias in slots]
        peak = scores[0].max(axis=0, keepdims=True)
        for score in scores[1:]:
            peak = jnp.maximum(peak, score.max(axis=0, keepdims=True))
        total = jnp.zeros((1, tokens), F32)
        for index, score in enumerate(scores):
            e = jnp.exp2(score - peak)
            total = total + e.sum(axis=0, keepdims=True)
            e_ref[head, index * tokens : (index + 1) * tokens] = e.astype(BF16)
        ml_ref[head, 0:1] = peak
        ml_ref[head, 1:2] = total


def far_scores_kernel(rows, frame_ref, mask_ref, ml_ref, p_ref, w_ref, dv_ref, k2_ref):
    heads, _, tokens = p_ref.shape
    blocks = tokens // BLOCK
    frame = frame_ref[0]
    inner = (frame == 1) | (frame == 2)
    bias = bias_rows(mask_ref, 1, frame >= 0, blocks)
    for head in range(heads):
        keys = jnp.where(inner, rows("kb", head), rows("ka", head))
        put(k2_ref, head, keys)
        scores = masked_scores(keys, rows("q", head), bias)
        peak2 = scores.max(axis=0, keepdims=True)
        e = jnp.exp2(scores - peak2)
        total2 = e.sum(axis=0, keepdims=True)
        peak1 = ml_ref[head, 0:1]
        peak = jnp.maximum(peak1, peak2)
        near = jnp.exp2(peak1 - peak)
        far = jnp.exp2(peak2 - peak)
        inv = 1.0 / (near * ml_ref[head, 1:2] + far * total2)
        weights = (e * (far * inv)).astype(BF16)
        put(dv_ref, head, dot(weights, rows("g", head)).astype(BF16))
        p_ref[head] = weights
        w_ref[head, 0:1] = near * inv


def near_weights(e_ref, w_ref, head, index):
    tokens = e_ref.shape[2]
    e = e_ref[head, index * tokens : (index + 1) * tokens]
    return e * w_ref[head, 0:1].astype(BF16)


def near_values_kernel(rows, e_ref, w_ref, dv0_ref, dv1_ref, dv3_ref, acc_ref):
    heads, _, tokens = e_ref.shape
    for head in range(heads):
        grads = rows("g", head)
        acc = jnp.zeros((HD, tokens), F32)
        slots = (("v0", dv0_ref), ("v1", dv1_ref), ("v3", dv3_ref))
        for index, (name, dv_ref) in enumerate(slots):
            weights = near_weights(e_ref, w_ref, head, index)
            put(dv_ref, head, dot(weights, grads).astype(BF16))
            acc = acc + dot(rows(name, head).T, weights)
        acc_ref[head] = acc


def far_values_kernel(rows, frame_ref, p_ref, acc_ref, dk_ref, att_ref, delta_ref, dq_ref):
    heads = p_ref.shape[0]
    frame = frame_ref[0]
    inner = (frame == 1) | (frame == 2)
    for head in range(heads):
        keys = rows("k2", head)
        values = jnp.where(inner, rows("vb", head), rows("va", head))
        weights = p_ref[head]
        out = (acc_ref[head] + dot(values.T, weights)).astype(BF16)
        put(att_ref, head, out.T)
        grads = rows("g", head).T
        delta = (grads.astype(F32) * out.astype(F32)).sum(axis=0, keepdims=True)
        delta_ref[head, 0:1] = delta
        ds = (weights.astype(F32) * (dot(values, grads) - delta)).astype(BF16)
        put(dk_ref, head, (dot(ds, rows("q", head)) * SCALE).astype(BF16))
        dq_ref[head] = dot(keys.T, ds)


def near_keys_kernel(
    rows, e_ref, w_ref, delta_ref, dq2_ref, att_ref, dk0_ref, dk1_ref, dk3_ref, pair_ref
):
    pair_ref[:, 0] = att_ref[...]
    for head in range(e_ref.shape[0]):
        queries = rows("q", head)
        grads = rows("g", head).T
        delta = delta_ref[head, 0:1]
        dq = dq2_ref[head]
        slots = (("k0", "v0", dk0_ref), ("k1", "v1", dk1_ref), ("k3", "v3", dk3_ref))
        for index, (k_name, v_name, dk_ref) in enumerate(slots):
            weights = near_weights(e_ref, w_ref, head, index).astype(F32)
            ds = (weights * (dot(rows(v_name, head), grads) - delta)).astype(BF16)
            put(dk_ref, head, (dot(ds, queries) * SCALE).astype(BF16))
            dq = dq + dot(rows(k_name, head).T, ds)
        put(pair_ref, head, (dq * SCALE).astype(BF16).T, 1)


def add_both_kernel(frame_ref, first_ref, middle_ref, third_ref, edge_ref, first_out, third_out):
    inner = (frame_ref[0] == 1) | (frame_ref[0] == 2)
    third_out[...] = (third_ref[...].astype(F32) + edge_ref[...].astype(F32)).astype(BF16)

    @pl.when(inner)
    def _():
        first_out[...] = (first_ref[...].astype(F32) + middle_ref[...].astype(F32)).astype(BF16)

    @pl.when(jnp.logical_not(inner))
    def _():
        first_out[...] = first_ref[...]


def sum_kernel(frame_ref, own_ref, edge_ref, middle_ref, out_ref):
    inner = (frame_ref[0] == 1) | (frame_ref[0] == 2)
    total = own_ref[...].astype(F32) + edge_ref[...].astype(F32)
    out_ref[...] = (total + jnp.where(inner, middle_ref[...].astype(F32), 0.0)).astype(BF16)


def last_kernel(frame_ref, own_ref, edge_ref, middle_ref, second_ref, out_ref):
    inner = (frame_ref[0] == 1) | (frame_ref[0] == 2)
    total = own_ref[...].astype(F32) + edge_ref[...].astype(F32)
    out_ref[:, 0] = (total + jnp.where(inner, middle_ref[...].astype(F32), 0.0)).astype(BF16)
    out_ref[:, 1] = second_ref[...]


def pack_kernel(*refs):
    out_ref, held, packed, sems, out_sems = refs[-5:]
    copies = [
        pltpu.make_async_copy(ref, held.at[which], sems.at[which])
        for which, ref in enumerate(refs[:-5])
    ]
    for copy in copies:
        copy.start()
    peers, _, _, width = out_ref.shape
    leaving = []
    for which, copy in enumerate(copies):
        copy.wait()
        for peer in range(peers):
            packed[which, peer] = held[which, :, peer * width : (peer + 1) * width]
        leaving.append(
            pltpu.make_async_copy(packed.at[which], out_ref.at[:, which], out_sems.at[which])
        )
        leaving[-1].start()
    for copy in leaving:
        copy.wait()


def pass_kernel(*refs):
    pass


def pick_kernel(places, in_ref, *out_refs):
    for place, ref in zip(places, out_refs):
        ref[...] = in_ref[:, place]


def unpack_kernel(in_ref, *out_refs):
    peers, _, _, width = in_ref.shape
    for peer in range(peers):
        for which, ref in enumerate(out_refs):
            ref[:, peer * width : (peer + 1) * width] = in_ref[peer, which]


def per_device_line(query_rows, key_rows, value_rows, out_grad, block_mask):
    plane = ("rank", "head")
    devices = ("frame", "rank", "head")
    head_parts = lax.axis_size("head")
    peers = lax.axis_size("rank") * head_parts
    rows, columns = query_rows.shape
    width = columns // peers
    heads = width // HD
    tokens = peers * rows
    one = jax.ShapeDtypeStruct((peers, rows, width), BF16)
    row_type = jax.ShapeDtypeStruct((rows, columns), BF16)
    near_e = jax.ShapeDtypeStruct((heads, 3 * tokens, tokens), BF16)
    far_e = jax.ShapeDtypeStruct((heads, tokens, tokens), BF16)
    stat = jax.ShapeDtypeStruct((heads, 8, tokens), F32)
    accum = jax.ShapeDtypeStruct((heads, HD, tokens), F32)
    frame = lax.axis_index("frame").astype(jnp.int32).reshape(1)
    smem = pl.BlockSpec(memory_space=pltpu.SMEM)
    vmem = pl.BlockSpec(memory_space=pltpu.VMEM)
    anywhere = pl.BlockSpec(memory_space=pl.ANY)
    found = {}

    def estimate(work):
        return pl.CostEstimate(
            flops=int(work * FLOPS_PER_US), bytes_accessed=1 << 16, transcendentals=0
        )

    def call(kernel, outs, work, *operands, names=()):
        several = isinstance(outs, tuple)
        arrays = []
        places = {}
        for name in names:
            array, which = found[name]
            spot = [i for i, x in enumerate(arrays) if x is array]
            if not spot:
                spot = [len(arrays)]
                arrays.append(array)
            places[name] = (spot[0], which)

        def body(*refs):
            lookup = refs[: len(arrays)]
            if not places:
                return kernel(*refs)

            def rows_of(name, head):
                index, which = places[name]
                return flat(lookup[index], head, which)

            return kernel(rows_of, *refs[len(arrays) :])

        operands = tuple(arrays) + operands
        return pl.pallas_call(
            body,
            in_specs=[smem if x.dtype == jnp.int32 else vmem for x in operands],
            out_specs=(vmem,) * len(outs) if several else vmem,
            out_shape=outs,
            compiler_params=pltpu.CompilerParams(vmem_limit_bytes=VMEM_BYTES),
            cost_estimate=estimate(work),
        )(*operands)

    def packed(count):
        return jax.ShapeDtypeStruct((peers, count, rows, width), BF16)

    def pack(*arrays, limit=VMEM_BYTES):
        count = len(arrays)
        return pl.pallas_call(
            pack_kernel,
            in_specs=[anywhere] * count,
            out_specs=anywhere,
            out_shape=packed(count),
            scratch_shapes=[
                pltpu.VMEM((count, rows, columns), BF16),
                pltpu.VMEM((count, peers, rows, width), BF16),
                pltpu.SemaphoreType.DMA((count,)),
                pltpu.SemaphoreType.DMA((count,)),
            ],
            compiler_params=pltpu.CompilerParams(vmem_limit_bytes=limit),
            cost_estimate=estimate(0.5),
        )(*arrays)

    def pick(landed, *places):
        kernel = functools.partial(pick_kernel, places)
        return call(kernel, (one,) * len(places), PICK_WORK, landed)

    def later(work, *arrays):
        return pl.pallas_call(
            pass_kernel,
            in_specs=[anywhere] * len(arrays),
            out_specs=(anywhere,) * len(arrays),
            out_shape=tuple(jax.ShapeDtypeStruct(x.shape, x.dtype) for x in arrays),
            input_output_aliases={i: i for i in range(len(arrays))},
            cost_estimate=estimate(work),
        )(*arrays)

    def swap(array):
        return lax.all_to_all(array, plane, 0, 0, tiled=True)

    def leave(pair):
        return call(unpack_kernel, (row_type, row_type), 0.5, swap(pair))

    def barrier(*values):
        return lax.optimization_barrier(values)

    def pairs_of(partner):
        pairs = []
        for frame_ in range(4):
            for rank in range(GROUP):
                for part in range(head_parts):
                    there = partner.get(frame_)
                    place = (frame_, rank ^ 1) if there is None else (there, rank)
                    pairs.append(
                        (
                            (frame_ * GROUP + rank) * head_parts + part,
                            (place[0] * GROUP + place[1]) * head_parts + part,
                        )
                    )
        return pairs

    edge = pairs_of({0: 1, 1: 0, 2: 3, 3: 2})
    middle = pairs_of({1: 2, 2: 1})

    def send(array, pairs):
        return lax.ppermute(array, devices, pairs)

    def sums(first, third, from_edge, from_middle):
        return call(
            add_both_kernel, (one, one), 0.2, frame, first, from_middle, third, from_edge
        )

    v1_rows, v3_rows = send(value_rows, edge), send(value_rows, middle)
    kqg = swap(pack(key_rows, query_rows, out_grad, limit=FIRST_PACK_BYTES))
    values = pack(value_rows, v1_rows, v3_rows)
    kqg, values = barrier(kqg, values)
    (k0,) = pick(kqg, 0)
    k1, k3 = send(k0, edge), send(k0, middle)
    k1_on, k3_on = later(SECOND_HOP_WORK, k1, k3)
    ka, kb = send(k3_on, edge), send(k1_on, middle)
    for name, array in (("k0", k0), ("k1", k1), ("k3", k3), ("ka", ka), ("kb", kb)):
        found[name] = (array, None)
    found.update(q=(kqg, 1), g=(kqg, 2))
    e_near, ml = call(
        near_scores_kernel, (near_e, stat), 3.5, frame, block_mask,
        names=("q", "k0", "k1", "k3"),
    )
    values, ml = barrier(swap(values), ml)
    v1, v3 = pick(values, 1, 2)
    found.update(v0=(values, 0), v1=(values, 1), v3=(values, 2))
    found.update(va=(send(v3, edge), None), vb=(send(v1, middle), None))

    p_far, w, dv2, k2 = call(
        far_scores_kernel, (far_e, stat, one, one), 2, frame, block_mask, ml,
        names=("q", "g", "ka", "kb"),
    )
    found["k2"] = (k2, None)
    dv_edge, dv_middle = send(dv2, edge), send(dv2, middle)
    dv0, dv1, dv3, acc = call(
        near_values_kernel, (one, one, one, accum), 2, e_near, w,
        names=("g", "v0", "v1", "v3"),
    )
    dk2, att, delta, dq2 = call(
        far_values_kernel, (one, one, stat, accum), 2, frame, p_far, acc,
        names=("q", "g", "k2", "va", "vb"),
    )
    dk_edge, dk_middle = send(dk2, edge), send(dk2, middle)
    dk0, dk1, dk3, att_dq = call(
        near_keys_kernel, (one, one, one, packed(2)), 4, e_near, w, delta, dq2, att,
        names=("q", "g", "k0", "k1", "k3", "v0", "v1", "v3"),
    )
    att_dq, dv1, dv3 = barrier(att_dq, dv1, dv3)
    dv_first, dv_third = sums(dv1, dv3, dv_edge, dv_middle)
    dv_over = send(dv_first, edge), send(dv_third, middle)
    dk_first, dk_third = sums(dk1, dk3, dk_edge, dk_middle)
    dk_over = send(dk_first, edge), send(dk_third, middle)
    attended, grad_query = leave(att_dq)
    dv = call(sum_kernel, one, SUM_WORK, frame, dv0, *dv_over)
    grad_keys, grad_values = leave(
        call(last_kernel, packed(2), 0.5, frame, dk0, *dk_over, dv)
    )
    return attended, grad_query, grad_keys, grad_values


def solution(mesh):
    seq, head = mesh.shape["seq"], mesh.shape["head"]
    frames = seq // GROUP
    line = Mesh(mesh.devices.reshape(frames, GROUP, head), ("frame", "rank", "head"))

    def run(query_rows, key_rows, value_rows, out_grad, block_mask):
        heads = query_rows.shape[1] // HD
        tokens = query_rows.shape[0] // frames
        fits = (
            frames == 4
            and block_mask.shape[0] == 2
            and heads % (GROUP * head) == 0
            and tokens == block_mask.shape[1] * BLOCK
            and tokens // (GROUP * head) % 16 == 0
        )
        if fits:
            body, where, axes = per_device_line, line, ("frame", "rank", "head")
        else:
            body, where, axes = per_device_general, mesh, ("seq", "head")
        row_spec = P(axes, None)
        return jax.shard_map(
            body,
            mesh=where,
            in_specs=(row_spec,) * 4 + (P(),),
            out_specs=(row_spec,) * 4,
            check_vma=False,
        )(query_rows, key_rows, value_rows, out_grad, block_mask)

    return run
```

```python
import functools
import math

import jax
import jax.numpy as jnp
from jax import lax
from jax.experimental import pallas as pl
from jax.experimental.pallas import tpu as pltpu
from jax.sharding import Mesh
from jax.sharding import PartitionSpec as P

HD = 128
BLOCK = 128
GROUP = 4
SCALE = 1.0 / math.sqrt(HD)
SCALE_LOG2 = SCALE * math.log2(math.e)
MASKED = -1e30
VMEM_BYTES = 12 * 1024 * 1024
FIRST_PACK_BYTES = 60 * 1024 * 1024

FLOPS_PER_US = 1_150_000_000
SECOND_HOP_WORK = 20
PICK_WORK = 20
SUM_WORK = 20


def partner_2(shard, axis, distance):
    return lax.ppermute(shard, axis, [(i, i ^ 1 << distance) for i in range(lax.axis_size(axis))])


def passed_along(shard, axis, by):
    peers = lax.axis_size(axis)
    pairs = [(i, i + by) for i in range(peers) if 0 <= i + by < peers]
    return lax.ppermute(shard, axis, pairs)


def widen_mask(bits):
    blocks = bits.shape[0]
    grid = jnp.broadcast_to((bits > 0)[:, None, :, None], (blocks, BLOCK, blocks, BLOCK))
    return grid.reshape(blocks * BLOCK, blocks * BLOCK)


def place_pair(mine, other, is_low, dim):
    return lax.cond(
        is_low,
        lambda pair: jnp.concatenate([pair[0], pair[1]], dim),
        lambda pair: jnp.concatenate([pair[1], pair[0]], dim),
        (mine, other),
    )


def per_device_general(query_rows, key_rows, value_rows, out_grad, block_mask):
    queries, keys_local, values_local, grads_output = (
        lax.all_to_all(query_rows, "head", split_axis=1, concat_axis=0, tiled=True),
        lax.all_to_all(key_rows, "head", split_axis=1, concat_axis=0, tiled=True),
        lax.all_to_all(value_rows, "head", split_axis=1, concat_axis=0, tiled=True),
        lax.all_to_all(out_grad, "head", split_axis=1, concat_axis=0, tiled=True),
    )
    seq_index = lax.axis_index("seq")
    group_bits = GROUP.bit_length() - 1
    rank = seq_index % GROUP
    frame_index = seq_index // GROUP
    frame_count = lax.axis_size("seq") // GROUP
    level_count = block_mask.shape[0]
    block_rows = queries.shape[0]
    frame_tokens = block_rows * GROUP
    head_count = queries.shape[1] // HD
    score_scale = 1.0 / math.sqrt(HD)
    own_pair = jnp.stack([keys_local, values_local])

    def low_bit(bit):
        return seq_index >> bit & 1 == 0

    whole_pair = own_pair
    for bit in range(group_bits):
        other = partner_2(whole_pair, "seq", bit)
        whole_pair = place_pair(whole_pair, other, low_bit(bit), 1)
    partner_list = []
    for level_index in range(level_count):
        for orient in (1, -1):
            partner_list.append(
                passed_along(whole_pair, "seq", orient * GROUP * (1 << level_index))
            )
    every_pair = jnp.concatenate([whole_pair] + partner_list, axis=1)
    keys_all, values_all = (every_pair[0], every_pair[1])
    allowed_list = [jnp.ones((block_rows, frame_tokens), bool)]
    for level_index in range(level_count):
        for orient in (1, -1):
            partner = frame_index - orient * (1 << level_index)
            inside = (partner >= 0) & (partner < frame_count)
            allowed_list.append(
                lax.dynamic_slice_in_dim(
                    widen_mask(block_mask[level_index]), rank * block_rows, block_rows, 0
                )
                & inside
            )
    allowed = jnp.concatenate(allowed_list, axis=1)

    def head_scores(query_head, keys_head):
        scores = (
            jnp.einsum("qd,kd->qk", query_head, keys_head, preferred_element_type=jnp.float32)
            * score_scale
        )
        return jnp.where(allowed, scores, -jnp.inf)

    outputs = []
    logsums = []
    for head_index in range(head_count):
        columns = slice(head_index * HD, (head_index + 1) * HD)
        scores = head_scores(queries[:, columns], keys_all[:, columns])
        peak = jnp.max(scores, axis=1, keepdims=True)
        logsum = peak + jnp.log(jnp.sum(jnp.exp(scores - peak), axis=1, keepdims=True))
        weights = jnp.exp(scores - logsum).astype(jnp.bfloat16)
        outputs.append(
            jnp.dot(weights, values_all[:, columns], preferred_element_type=jnp.float32).astype(
                jnp.bfloat16
            )
        )
        logsums.append(logsum)
    attended = jnp.concatenate(outputs, axis=1)
    query_grads = []
    key_grads = []
    value_grads = []
    for head_index in range(head_count):
        columns = slice(head_index * HD, (head_index + 1) * HD)
        query_head = queries[:, columns]
        grad_head = grads_output[:, columns]
        scores = head_scores(query_head, keys_all[:, columns])
        probability = jnp.exp(scores - logsums[head_index])
        weights = probability.astype(jnp.bfloat16)
        grad_weights = jnp.einsum(
            "qd,kd->qk", grad_head, values_all[:, columns], preferred_element_type=jnp.float32
        )
        delta_row = jnp.sum(
            grad_head.astype(jnp.float32) * attended[:, columns].astype(jnp.float32),
            axis=1,
            keepdims=True,
        )
        grad_scores = (probability * (grad_weights - delta_row) * score_scale).astype(jnp.bfloat16)
        query_grads.append(
            jnp.dot(grad_scores, keys_all[:, columns], preferred_element_type=jnp.float32).astype(
                jnp.bfloat16
            )
        )
        key_grads.append(
            jnp.einsum(
                "qk,qd->kd", grad_scores, query_head, preferred_element_type=jnp.float32
            ).astype(jnp.bfloat16)
        )
        value_grads.append(
            jnp.einsum("qk,qd->kd", weights, grad_head, preferred_element_type=jnp.float32).astype(
                jnp.bfloat16
            )
        )
    grad_query = jnp.concatenate(query_grads, axis=1)
    grad_pair = jnp.stack(
        [jnp.concatenate(key_grads, axis=1), jnp.concatenate(value_grads, axis=1)]
    )
    total = grad_pair[:, :frame_tokens].astype(jnp.float32)
    piece_index = 1
    for level_index in range(level_count):
        for orient in (1, -1):
            piece = grad_pair[:, piece_index * frame_tokens : (piece_index + 1) * frame_tokens]
            returned = passed_along(piece, "seq", -orient * GROUP * (1 << level_index))
            total = total + returned.astype(jnp.float32)
            piece_index += 1
    for bit in reversed(range(group_bits)):
        half = total.shape[1] // 2
        first_half = total[:, :half]
        second_half = total[:, half:]
        is_low = low_bit(bit)
        outgoing = jnp.where(is_low, second_half, first_half)
        staying = jnp.where(is_low, first_half, second_half)
        total = staying + partner_2(outgoing, "seq", bit)
    grad_keys = total[0].astype(jnp.bfloat16)
    grad_values = total[1].astype(jnp.bfloat16)
    return (
        lax.all_to_all(attended, "head", split_axis=0, concat_axis=1, tiled=True),
        lax.all_to_all(grad_query, "head", split_axis=0, concat_axis=1, tiled=True),
        lax.all_to_all(grad_keys, "head", split_axis=0, concat_axis=1, tiled=True),
        lax.all_to_all(grad_values, "head", split_axis=0, concat_axis=1, tiled=True),
    )


NT = (((1,), (1,)), ((), ()))
F32 = jnp.float32
BF16 = jnp.bfloat16


def dot(a, b):
    return jnp.dot(a, b, preferred_element_type=F32)


def dot_nt(a, b):
    return lax.dot_general(a, b, NT, preferred_element_type=F32)


def head_columns(head):
    return slice(head * HD, (head + 1) * HD)


def flat(ref, head, which=None):
    columns = head_columns(head)
    part = ref[:, :, columns] if which is None else ref[:, which, :, columns]
    return part.reshape(part.shape[0] * part.shape[1], HD)


def put(ref, head, rows, which=None):
    if which is None:
        ref[:, :, head_columns(head)] = rows.reshape(ref.shape[0], ref.shape[1], HD)
    else:
        ref[:, which, :, head_columns(head)] = rows.reshape(ref.shape[0], ref.shape[2], HD)


def bias_rows(mask_ref, level, valid, blocks):
    lane_block = lax.broadcasted_iota(jnp.int32, (1, blocks * BLOCK), 1) // BLOCK
    rows = []
    for key_block in range(blocks):
        row = jnp.zeros((1, blocks * BLOCK), F32)
        for query_block in range(blocks):
            open_ = (mask_ref[level, query_block, key_block] > 0) & valid
            value = jnp.where(open_, 0.0, MASKED).astype(F32)
            row = jnp.where(lane_block == query_block, value, row)
        rows.append(row)
    return rows


def masked_scores(keys, queries, bias):
    scores = dot_nt(keys, queries) * SCALE_LOG2
    if bias is None:
        return scores
    blocks = len(bias)
    return jnp.concatenate(
        [scores[j * BLOCK : (j + 1) * BLOCK] + bias[j] for j in range(blocks)], axis=0
    )


def near_scores_kernel(rows, frame_ref, mask_ref, e_ref, ml_ref):
    heads, _, tokens = e_ref.shape
    blocks = tokens // BLOCK
    frame = frame_ref[0]
    inner = (frame == 1) | (frame == 2)
    bias1 = bias_rows(mask_ref, 0, frame >= 0, blocks)
    bias3 = bias_rows(mask_ref, 0, inner, blocks)
    for head in range(heads):
        queries = rows("q", head)
        slots = (("k0", None), ("k1", bias1), ("k3", bias3))
        scores = [masked_scores(rows(name, head), queries, bias) for name, bias in slots]
        peak = scores[0].max(axis=0, keepdims=True)
        for score in scores[1:]:
            peak = jnp.maximum(peak, score.max(axis=0, keepdims=True))
        total = jnp.zeros((1, tokens), F32)
        for index, score in enumerate(scores):
            e = jnp.exp2(score - peak)
            total = total + e.sum(axis=0, keepdims=True)
            e_ref[head, index * tokens : (index + 1) * tokens] = e.astype(BF16)
        ml_ref[head, 0:1] = peak
        ml_ref[head, 1:2] = total


def far_scores_kernel(rows, frame_ref, mask_ref, ml_ref, p_ref, w_ref, dv_ref, k2_ref):
    heads, _, tokens = p_ref.shape
    blocks = tokens // BLOCK
    frame = frame_ref[0]
    inner = (frame == 1) | (frame == 2)
    bias = bias_rows(mask_ref, 1, frame >= 0, blocks)
    for head in range(heads):
        keys = jnp.where(inner, rows("kb", head), rows("ka", head))
        put(k2_ref, head, keys)
        scores = masked_scores(keys, rows("q", head), bias)
        peak2 = scores.max(axis=0, keepdims=True)
        e = jnp.exp2(scores - peak2)
        total2 = e.sum(axis=0, keepdims=True)
        peak1 = ml_ref[head, 0:1]
        peak = jnp.maximum(peak1, peak2)
        near = jnp.exp2(peak1 - peak)
        far = jnp.exp2(peak2 - peak)
        inv = 1.0 / (near * ml_ref[head, 1:2] + far * total2)
        weights = (e * (far * inv)).astype(BF16)
        put(dv_ref, head, dot(weights, rows("g", head)).astype(BF16))
        p_ref[head] = weights
        w_ref[head, 0:1] = near * inv


def near_weights(e_ref, w_ref, head, index):
    tokens = e_ref.shape[2]
    e = e_ref[head, index * tokens : (index + 1) * tokens]
    return e * w_ref[head, 0:1].astype(BF16)


def near_values_kernel(rows, e_ref, w_ref, dv0_ref, dv1_ref, dv3_ref, acc_ref):
    heads, _, tokens = e_ref.shape
    for head in range(heads):
        grads = rows("g", head)
        acc = jnp.zeros((HD, tokens), F32)
        slots = (("v0", dv0_ref), ("v1", dv1_ref), ("v3", dv3_ref))
        for index, (name, dv_ref) in enumerate(slots):
            weights = near_weights(e_ref, w_ref, head, index)
            put(dv_ref, head, dot(weights, grads).astype(BF16))
            acc = acc + dot(rows(name, head).T, weights)
        acc_ref[head] = acc


def far_values_kernel(rows, frame_ref, p_ref, acc_ref, dk_ref, att_ref, delta_ref, dq_ref):
    heads = p_ref.shape[0]
    frame = frame_ref[0]
    inner = (frame == 1) | (frame == 2)
    for head in range(heads):
        keys = rows("k2", head)
        values = jnp.where(inner, rows("vb", head), rows("va", head))
        weights = p_ref[head]
        out = (acc_ref[head] + dot(values.T, weights)).astype(BF16)
        put(att_ref, head, out.T)
        grads = rows("g", head).T
        delta = (grads.astype(F32) * out.astype(F32)).sum(axis=0, keepdims=True)
        delta_ref[head, 0:1] = delta
        ds = (weights.astype(F32) * (dot(values, grads) - delta)).astype(BF16)
        put(dk_ref, head, (dot(ds, rows("q", head)) * SCALE).astype(BF16))
        dq_ref[head] = dot(keys.T, ds)


def near_keys_kernel(
    rows, e_ref, w_ref, delta_ref, dq2_ref, att_ref, dk0_ref, dk1_ref, dk3_ref, pair_ref
):
    pair_ref[:, 0] = att_ref[...]
    for head in range(e_ref.shape[0]):
        queries = rows("q", head)
        grads = rows("g", head).T
        delta = delta_ref[head, 0:1]
        dq = dq2_ref[head]
        slots = (("k0", "v0", dk0_ref), ("k1", "v1", dk1_ref), ("k3", "v3", dk3_ref))
        for index, (k_name, v_name, dk_ref) in enumerate(slots):
            weights = near_weights(e_ref, w_ref, head, index).astype(F32)
            ds = (weights * (dot(rows(v_name, head), grads) - delta)).astype(BF16)
            put(dk_ref, head, (dot(ds, queries) * SCALE).astype(BF16))
            dq = dq + dot(rows(k_name, head).T, ds)
        put(pair_ref, head, (dq * SCALE).astype(BF16).T, 1)


def add_both_kernel(frame_ref, first_ref, middle_ref, third_ref, edge_ref, first_out, third_out):
    inner = (frame_ref[0] == 1) | (frame_ref[0] == 2)
    third_out[...] = (third_ref[...].astype(F32) + edge_ref[...].astype(F32)).astype(BF16)

    @pl.when(inner)
    def _():
        first_out[...] = (first_ref[...].astype(F32) + middle_ref[...].astype(F32)).astype(BF16)

    @pl.when(jnp.logical_not(inner))
    def _():
        first_out[...] = first_ref[...]


def sum_kernel(frame_ref, own_ref, edge_ref, middle_ref, out_ref):
    inner = (frame_ref[0] == 1) | (frame_ref[0] == 2)
    total = own_ref[...].astype(F32) + edge_ref[...].astype(F32)
    out_ref[...] = (total + jnp.where(inner, middle_ref[...].astype(F32), 0.0)).astype(BF16)


def last_kernel(frame_ref, own_ref, edge_ref, middle_ref, second_ref, out_ref):
    inner = (frame_ref[0] == 1) | (frame_ref[0] == 2)
    total = own_ref[...].astype(F32) + edge_ref[...].astype(F32)
    out_ref[:, 0] = (total + jnp.where(inner, middle_ref[...].astype(F32), 0.0)).astype(BF16)
    out_ref[:, 1] = second_ref[...]


def pack_kernel(*refs):
    out_ref, held, packed, sems, out_sems = refs[-5:]
    copies = [
        pltpu.make_async_copy(ref, held.at[which], sems.at[which])
        for which, ref in enumerate(refs[:-5])
    ]
    for copy in copies:
        copy.start()
    peers, _, _, width = out_ref.shape
    leaving = []
    for which, copy in enumerate(copies):
        copy.wait()
        for peer in range(peers):
            packed[which, peer] = held[which, :, peer * width : (peer + 1) * width]
        leaving.append(
            pltpu.make_async_copy(packed.at[which], out_ref.at[:, which], out_sems.at[which])
        )
        leaving[-1].start()
    for copy in leaving:
        copy.wait()


def pass_kernel(*refs):
    pass


def pick_kernel(places, in_ref, *out_refs):
    for place, ref in zip(places, out_refs):
        ref[...] = in_ref[:, place]


def unpack_kernel(in_ref, *out_refs):
    peers, _, _, width = in_ref.shape
    for peer in range(peers):
        for which, ref in enumerate(out_refs):
            ref[:, peer * width : (peer + 1) * width] = in_ref[peer, which]


def per_device_line(query_rows, key_rows, value_rows, out_grad, block_mask):
    plane = ("rank", "head")
    devices = ("frame", "rank", "head")
    head_parts = lax.axis_size("head")
    peers = lax.axis_size("rank") * head_parts
    rows, columns = query_rows.shape
    width = columns // peers
    heads = width // HD
    tokens = peers * rows
    one = jax.ShapeDtypeStruct((peers, rows, width), BF16)
    row_type = jax.ShapeDtypeStruct((rows, columns), BF16)
    near_e = jax.ShapeDtypeStruct((heads, 3 * tokens, tokens), BF16)
    far_e = jax.ShapeDtypeStruct((heads, tokens, tokens), BF16)
    stat = jax.ShapeDtypeStruct((heads, 8, tokens), F32)
    accum = jax.ShapeDtypeStruct((heads, HD, tokens), F32)
    frame = lax.axis_index("frame").astype(jnp.int32).reshape(1)
    smem = pl.BlockSpec(memory_space=pltpu.SMEM)
    vmem = pl.BlockSpec(memory_space=pltpu.VMEM)
    anywhere = pl.BlockSpec(memory_space=pl.ANY)
    found = {}

    def estimate(work):
        return pl.CostEstimate(
            flops=int(work * FLOPS_PER_US), bytes_accessed=1 << 16, transcendentals=0
        )

    def call(kernel, outs, work, *operands, names=()):
        several = isinstance(outs, tuple)
        arrays = []
        places = {}
        for name in names:
            array, which = found[name]
            spot = [i for i, x in enumerate(arrays) if x is array]
            if not spot:
                spot = [len(arrays)]
                arrays.append(array)
            places[name] = (spot[0], which)

        def body(*refs):
            lookup = refs[: len(arrays)]
            if not places:
                return kernel(*refs)

            def rows_of(name, head):
                index, which = places[name]
                return flat(lookup[index], head, which)

            return kernel(rows_of, *refs[len(arrays) :])

        operands = tuple(arrays) + operands
        return pl.pallas_call(
            body,
            in_specs=[smem if x.dtype == jnp.int32 else vmem for x in operands],
            out_specs=(vmem,) * len(outs) if several else vmem,
            out_shape=outs,
            compiler_params=pltpu.CompilerParams(vmem_limit_bytes=VMEM_BYTES),
            cost_estimate=estimate(work),
        )(*operands)

    def packed(count):
        return jax.ShapeDtypeStruct((peers, count, rows, width), BF16)

    def pack(*arrays, limit=VMEM_BYTES):
        count = len(arrays)
        return pl.pallas_call(
            pack_kernel,
            in_specs=[anywhere] * count,
            out_specs=anywhere,
            out_shape=packed(count),
            scratch_shapes=[
                pltpu.VMEM((count, rows, columns), BF16),
                pltpu.VMEM((count, peers, rows, width), BF16),
                pltpu.SemaphoreType.DMA((count,)),
                pltpu.SemaphoreType.DMA((count,)),
            ],
            compiler_params=pltpu.CompilerParams(vmem_limit_bytes=limit),
            cost_estimate=estimate(0.5),
        )(*arrays)

    def pick(landed, *places):
        kernel = functools.partial(pick_kernel, places)
        return call(kernel, (one,) * len(places), PICK_WORK, landed)

    def later(work, *arrays):
        return pl.pallas_call(
            pass_kernel,
            in_specs=[anywhere] * len(arrays),
            out_specs=(anywhere,) * len(arrays),
            out_shape=tuple(jax.ShapeDtypeStruct(x.shape, x.dtype) for x in arrays),
            input_output_aliases={i: i for i in range(len(arrays))},
            cost_estimate=estimate(work),
        )(*arrays)

    def swap(array):
        return lax.all_to_all(array, plane, 0, 0, tiled=True)

    def leave(pair):
        return call(unpack_kernel, (row_type, row_type), 0.5, swap(pair))

    def barrier(*values):
        return lax.optimization_barrier(values)

    def pairs_of(partner):
        pairs = []
        for frame_ in range(4):
            for rank in range(GROUP):
                for part in range(head_parts):
                    there = partner.get(frame_)
                    place = (frame_, rank ^ 1) if there is None else (there, rank)
                    pairs.append(
                        (
                            (frame_ * GROUP + rank) * head_parts + part,
                            (place[0] * GROUP + place[1]) * head_parts + part,
                        )
                    )
        return pairs

    edge = pairs_of({0: 1, 1: 0, 2: 3, 3: 2})
    middle = pairs_of({1: 2, 2: 1})

    def send(array, pairs):
        return lax.ppermute(array, devices, pairs)

    def sums(first, third, from_edge, from_middle):
        return call(
            add_both_kernel, (one, one), 0.2, frame, first, from_middle, third, from_edge
        )

    v1_rows, v3_rows = send(value_rows, edge), send(value_rows, middle)
    kqg = swap(pack(key_rows, query_rows, out_grad, limit=FIRST_PACK_BYTES))
    values = pack(value_rows, v1_rows, v3_rows)
    kqg, values = barrier(kqg, values)
    (k0,) = pick(kqg, 0)
    k1, k3 = send(k0, edge), send(k0, middle)
    k1_on, k3_on = later(SECOND_HOP_WORK, k1, k3)
    ka, kb = send(k3_on, edge), send(k1_on, middle)
    for name, array in (("k0", k0), ("k1", k1), ("k3", k3), ("ka", ka), ("kb", kb)):
        found[name] = (array, None)
    found.update(q=(kqg, 1), g=(kqg, 2))
    e_near, ml = call(
        near_scores_kernel, (near_e, stat), 3.5, frame, block_mask,
        names=("q", "k0", "k1", "k3"),
    )
    values = swap(values)
    v1, v3 = pick(values, 1, 2)
    found.update(v0=(values, 0), v1=(values, 1), v3=(values, 2))
    found.update(va=(send(v3, edge), None), vb=(send(v1, middle), None))

    p_far, w, dv2, k2 = call(
        far_scores_kernel, (far_e, stat, one, one), 2, frame, block_mask, ml,
        names=("q", "g", "ka", "kb"),
    )
    found["k2"] = (k2, None)
    dv_edge, dv_middle = send(dv2, edge), send(dv2, middle)
    dv0, dv1, dv3, acc = call(
        near_values_kernel, (one, one, one, accum), 2, e_near, w,
        names=("g", "v0", "v1", "v3"),
    )
    dk2, att, delta, dq2 = call(
        far_values_kernel, (one, one, stat, accum), 2, frame, p_far, acc,
        names=("q", "g", "k2", "va", "vb"),
    )
    dk_edge, dk_middle = send(dk2, edge), send(dk2, middle)
    dk0, dk1, dk3, att_dq = call(
        near_keys_kernel, (one, one, one, packed(2)), 4, e_near, w, delta, dq2, att,
        names=("q", "g", "k0", "k1", "k3", "v0", "v1", "v3"),
    )
    att_dq, dv1, dv3 = barrier(att_dq, dv1, dv3)
    dv_first, dv_third = sums(dv1, dv3, dv_edge, dv_middle)
    dv_over = send(dv_first, edge), send(dv_third, middle)
    dk_first, dk_third = sums(dk1, dk3, dk_edge, dk_middle)
    dk_over = send(dk_first, edge), send(dk_third, middle)
    attended, grad_query = leave(att_dq)
    dv = call(sum_kernel, one, SUM_WORK, frame, dv0, *dv_over)
    grad_keys, grad_values = leave(
        call(last_kernel, packed(2), 0.5, frame, dk0, *dk_over, dv)
    )
    return attended, grad_query, grad_keys, grad_values


def solution(mesh):
    seq, head = mesh.shape["seq"], mesh.shape["head"]
    frames = seq // GROUP
    line = Mesh(mesh.devices.reshape(frames, GROUP, head), ("frame", "rank", "head"))

    def run(query_rows, key_rows, value_rows, out_grad, block_mask):
        heads = query_rows.shape[1] // HD
        tokens = query_rows.shape[0] // frames
        fits = (
            frames == 4
            and block_mask.shape[0] == 2
            and heads % (GROUP * head) == 0
            and tokens == block_mask.shape[1] * BLOCK
            and tokens // (GROUP * head) % 16 == 0
        )
        if fits:
            body, where, axes = per_device_line, line, ("frame", "rank", "head")
        else:
            body, where, axes = per_device_general, mesh, ("seq", "head")
        row_spec = P(axes, None)
        return jax.shard_map(
            body,
            mesh=where,
            in_specs=(row_spec,) * 4 + (P(),),
            out_specs=(row_spec,) * 4,
            check_vma=False,
        )(query_rows, key_rows, value_rows, out_grad, block_mask)

    return run
```
